32 devices in a mesh: dp: 8 (over z, x), row: 2 (over y), col: 2 (over core).
Axes of the slice: x: 2, y: 2, z: 4, core: 2. Of those that a mesh axis runs over, the one named last changes fastest.
Arguments:
- tokens: bfloat16 [8192, 768], P(('dp', 'row')), may hold values from -6 to 6
- grad_out: bfloat16 [8192, 768], P(('dp', 'row')), may hold values from -6 to 6
- routes: int32 [8192, 1], P(('dp', 'row')), may hold values from 0 to 1; in each aligned block of 512 rows (0 to 511, 512 to 1023, ...) at most 512 rows name the same one
- norm1_gain: bfloat16 [768], replicated, may hold values from 0.099609375 to 1.8984375
- w_query: bfloat16 [768, 768], P('row', 'col'), may hold values from -0.21875 to 0.21875
- w_key: bfloat16 [768, 768], P('row', 'col'), may hold values from -0.21875 to 0.21875
- w_value: bfloat16 [768, 768], P('row', 'col'), may hold values from -0.21875 to 0.21875
- w_output: bfloat16 [768, 768], P('row', 'col'), may hold values from -0.875 to 0.875
- rel_table: bfloat16 [32, 12], replicated, may hold values from -4 to 4
- rel_bucket: int32 [2047], replicated, may hold values from 0 to 31
- norm2_gain: bfloat16 [768], replicated, may hold values from 0.099609375 to 1.8984375
- router: bfloat16 [768, 2], replicated, may hold values from -0.15625 to 0.15625
- w_in: bfloat16 [2, 768, 3072], P('row', None, 'col'), may hold values from -0.21875 to 0.21875
- w_out: bfloat16 [2, 768, 3072], P('row', None, 'col'), may hold values from -0.625 to 0.625
Outputs:
- output: bfloat16 [8192, 768], P(('dp', 'row'))
- grad_tokens: float32 [8192, 768], P(('dp', 'row'))
- grad_norm1: float32 [768], P(('dp', 'row'))
- grad_w_query: float32 [768, 768], P(('dp', 'row'), 'col')
- grad_w_key: float32 [768, 768], P(('dp', 'row'), 'col')
- grad_w_value: float32 [768, 768], P(('dp', 'row'), 'col')
- grad_w_output: float32 [768, 768], P(('dp', 'row'), 'col')
- grad_table: float32 [32, 12], P(None, 'col')
- grad_norm2: float32 [768], P(('dp', 'row'))
- grad_router: float32 [768, 2], P(('dp', 'row'))
- grad_w_in: float32 [2, 768, 3072], P('row', 'dp', 'col')
- grad_w_out: float32 [2, 768, 3072], P('row', 'dp', 'col')
The draws below stay inside these ranges and needn't reach their ends.
Inputs may be any that keep to these rules, and one draw needn't show every extreme that they name: `routes`: within the rows of one device (512 consecutive tokens) no expert is named by more than 512 tokens, and in some such blocks one expert is named by exactly 512.
All inputs are finite; a program needn't handle non-finite values.
Results may differ from the reference program's by a relative error of at most 0.015.
Values may be sent and summed in bfloat16 or wider, within the bound.
No kernel may reach another device: no remote copies, remote signals or barrier semaphores. Data moves between devices by JAX's collectives and lax.ppermute only.
A program may use at most 192 MiB of HBM per device.

```python
import math
from functools import partial
import jax
import jax.numpy as jnp
import numpy as np
from jax import lax

D = 768
H = 12
HDIM = 64
FF = 3072
NBUCKET = 32
SEQ = 1024
TOK_DEV = 512
TOKENS = 8192
EXPERTS = 2
CAP = 512
N_DP = 8
N_ROW = 2


def with_ends(values, stream_key, low, largest):
    place = [jax.random.randint(jax.random.fold_in(stream_key, axis), (), 0, length) for axis, length in enumerate(values.shape)]
    longest = values.shape.index(max(values.shape))
    beside = place[:longest] + [(place[longest] + 1) % values.shape[longest]] + place[longest + 1:]
    return values.at[tuple(place)].set(low).at[tuple(beside)].set(largest)


def strengthened(entries, own_key, source, target, shards_of, factor):
    owner, partner = [(jnp.arange(entries.shape[position]) // (entries.shape[position] // shards_of)).reshape([-1 if axis == position else 1 for axis in range(entries.ndim)]) for position in (source, target)]
    chosen = jax.random.permutation(own_key, shards_of)[partner]
    strong = (owner == chosen) | (owner == (partner + shards_of // 2) % shards_of)
    return jnp.where(strong, factor * entries, entries)


def shard_levels(own_key, shape, pieces, smallest, high):
    level = 1.0
    for dim, shards_of in pieces:
        draws = jax.random.uniform(jax.random.fold_in(jax.random.fold_in(own_key, 6), dim), (shards_of,), jnp.float32, smallest / len(pieces), high / len(pieces))
        level = level * jnp.repeat(jnp.exp(draws), shape[dim] // shards_of).reshape((-1,) + (1,) * (len(shape) - 1 - dim))
    return level


def shared_out(key, own, number, rows, amount, top, reach, slope):
    ranking = jax.random.permutation(key, amount)
    crowded, ordinary = portions_of(amount, rows * top, reach, slope, True), portions_of(amount, rows * top, reach, slope, False)
    places = jnp.arange(amount)

    def named(sizes, rotation):
        used = int((sizes > 0).sum())
        fixed = max(1, used // 4)
        passed = fixed + (places - fixed + rotation * (used - fixed)) % max(1, amount - fixed)
        return jnp.zeros((amount,), jnp.int32).at[ranking[jnp.where(places < fixed, places, passed)]].set(jnp.asarray(sizes, jnp.int32))

    sizes = jnp.where(number % 4 == 0, named(crowded, number // 4), named(ordinary, number - number // 4 - 1))
    mixed = jax.random.permutation(jax.random.fold_in(own, 3), amount)
    donor, sink = mixed[0:amount // 2 * 2:2], mixed[1:amount // 2 * 2:2]
    margin = jnp.minimum(sizes[donor] - 1, reach - sizes[sink]) // 2
    margin = jnp.where((donor == ranking[0]) | (sink == ranking[0]) | (sizes[sink] == 0), 0, jnp.maximum(margin, 0))
    passed = jax.random.randint(jax.random.fold_in(own, 4), (amount // 2,), 0, 1 << 20) % (margin + 1)
    sizes = sizes.at[donor].add(-passed).at[sink].add(passed)
    items = jnp.searchsorted(jnp.cumsum(sizes), jnp.arange(rows * top), side="right").astype(jnp.int32)
    table = items.reshape(top, rows).T
    table = table[jax.random.permutation(jax.random.fold_in(own, 1), rows)]
    rotation = jax.random.randint(jax.random.fold_in(own, 2), (rows, 1), 0, top)
    return jnp.take_along_axis(table, (jnp.arange(top)[None, :] + rotation) % top, axis=1)


def portions_of(count, total, most, slope, full):
    loads = [(1 << 20) // math.isqrt(grade ** slope) + 1 for grade in range(1, count + 1)]
    largest = most if full else min(most, max(-(-total // count), total * loads[0] // sum(loads)))
    least = 1 if total - largest >= count - 1 else 0
    counts, spare = [largest] + [least] * (count - 1), total - largest - least * (count - 1)
    while spare > 0:
        candidates = [i for i in range(1, count) if counts[i] < largest] or [i for i in range(1, count) if counts[i] < most]
        whole, budget = sum([loads[i] for i in candidates]), spare
        for i in candidates:
            addition = min(most - counts[i], max(1, budget * loads[i] // whole), spare)
            counts[i] = counts[i] + addition
            spare = spare - addition
    return np.array(counts)


def centred(stream_key, extent, spread, most, cuts=(), kind=jnp.bfloat16):
    entries = jax.random.normal(stream_key, extent, jnp.float32) * spread
    if len(cuts) > 0:
        entries = shard_levels(stream_key, extent, cuts, -0.22, 0.18) * entries
    return jnp.clip(entries, min=-most, max=most).astype(kind)


def noise_with(own_key, dims, spread, bound, pieces, heavy, held_as=jnp.bfloat16):
    values = spread * jax.random.normal(own_key, dims, jnp.float32)
    if pieces:
        values = values * shard_levels(own_key, dims, pieces, -0.22, 0.18)
    return jnp.clip(strengthened(values, jax.random.fold_in(own_key, 3), *heavy), -bound, bound).astype(held_as)


def setup_inputs(seed: int = 0) -> dict:
    streams_of = jax.random.split(jax.random.key(seed), 15)
    tokens = centred(streams_of[0], (TOKENS, D), 1.0, 6.0, ((0, 16),))
    grad_out = noise_with(streams_of[1], (TOKENS, D), 1.0, 6.0, ((0, 16),), (0, 1, 16, 2.0))
    routes_keys = jax.random.split(jax.random.fold_in(streams_of[2], 1), TOKENS // TOK_DEV)
    routes_turns = jax.random.permutation(jax.random.fold_in(streams_of[2], 3), TOKENS // TOK_DEV)
    routes = jax.vmap(lambda own, number: shared_out(jax.random.fold_in(streams_of[2], 2), own, number, TOK_DEV, EXPERTS, 1, CAP, 2))(routes_keys, routes_turns).reshape((TOKENS, 1))
    norm1_gain = jnp.clip(1.0 + 0.18 * jax.random.normal(streams_of[3], (D,), jnp.float32), 0.099609375, 1.8984375).astype(jnp.bfloat16)
    w_query = centred(streams_of[4], (D, H * HDIM), D ** -0.5, 0.21875, ((0, 2), (1, 2)))
    w_key = centred(streams_of[5], (D, H * HDIM), D ** -0.5, 0.21875, ((0, 2), (1, 2)))
    w_value = centred(streams_of[6], (D, H * HDIM), D ** -0.5, 0.21875, ((0, 2), (1, 2)))
    w_output = centred(streams_of[7], (D, H * HDIM), (H * HDIM // 16) ** -0.5, 0.875, ((0, 2), (1, 2)))
    rel_table = centred(streams_of[8], (NBUCKET, H), 1.0, 4.0)
    rel_bucket = with_ends(jax.random.randint(streams_of[9], (2 * SEQ - 1,), 0, NBUCKET), jax.random.fold_in(streams_of[9], 1), 0, NBUCKET - 1).astype(jnp.int32)
    norm2_gain = jnp.clip(1.0 + 0.18 * jax.random.normal(streams_of[10], (D,), jnp.float32), 0.099609375, 1.8984375).astype(jnp.bfloat16)
    router = centred(streams_of[11], (D, EXPERTS), (2 * D) ** -0.5, 0.15625)
    w_in = centred(streams_of[12], (EXPERTS, D, FF), D ** -0.5, 0.21875, ((0, 2), (2, 2)))
    w_out = centred(streams_of[13], (EXPERTS, D, FF), (FF // 32) ** -0.5, 0.625, ((0, 2), (2, 2)))
    return dict(tokens=tokens, grad_out=grad_out, routes=routes, norm1_gain=norm1_gain, w_query=w_query, w_key=w_key, w_value=w_value, w_output=w_output, rel_table=rel_table, rel_bucket=rel_bucket, norm2_gain=norm2_gain, router=router, w_in=w_in, w_out=w_out)


HIGHEST = lax.Precision.HIGHEST
EPS = 1e-06
SCALE = 0.125

@jax.custom_vjp
def low(v):
    return lax.optimization_barrier(v.astype(jnp.bfloat16)).astype(jnp.float32)

@jax.custom_vjp
def low_back(v):
    return v

def low_keep(v):
    return (low(v), None)

def low_pass(kept, grad):
    return (grad,)

def back_keep(v):
    return (v, None)

def back_low(kept, grad):
    return (low(grad),)
low.defvjp(low_keep, low_pass)
low_back.defvjp(back_keep, back_low)

def rms_norm(rows, gain):
    return rows * lax.rsqrt(lax.optimization_barrier(jnp.mean(rows * rows, axis=-1, keepdims=True)) + EPS) * gain

def attend_sequence(offsets, parts):
    query_seq, key_seq, value_seq = parts
    length = query_seq.shape[0]
    query_h = query_seq.reshape(length, H, HDIM)
    key_h = key_seq.reshape(length, H, HDIM)
    value_h = value_seq.reshape(length, H, HDIM)
    index = length - 1 + jnp.arange(length, dtype=jnp.int32)[None, :] - jnp.arange(length, dtype=jnp.int32)[:, None]
    scores = SCALE * jnp.einsum('qhd,khd->hqk', query_h, key_h, precision=HIGHEST) + jnp.take(offsets, index, axis=1)
    shares = jax.nn.softmax(low_back(scores), axis=-1)
    attended = jnp.einsum('hqk,khd->qhd', low(shares), value_h, precision=HIGHEST)
    return attended.reshape(length, H * HDIM)

def expert_block(parts):
    rows, weight_in, weight_out = parts
    pre = jnp.dot(rows, weight_in, precision=HIGHEST)
    act = low(jax.nn.gelu(low_back(pre), approximate=True))
    return jnp.dot(act, weight_out.T, precision=HIGHEST)

def forward(tokens, gain_one, w_query, w_key, w_value, w_output, table, gain_two, router, w_in, w_out, bucket_hot, expert_ids):
    count_rows = tokens.shape[0]
    normed = low(rms_norm(tokens, gain_one))
    query = low(low_back(jnp.dot(normed, w_query, precision=HIGHEST)))
    key = low(low_back(jnp.dot(normed, w_key, precision=HIGHEST)))
    value = low(low_back(jnp.dot(normed, w_value, precision=HIGHEST)))
    offsets = jnp.dot(table.T, bucket_hot, precision=HIGHEST)
    sequences = count_rows // SEQ
    attended = lax.map(jax.checkpoint(partial(attend_sequence, offsets)), (query.reshape(sequences, SEQ, -1), key.reshape(sequences, SEQ, -1), value.reshape(sequences, SEQ, -1)))
    attended = low(low_back(attended.reshape(count_rows, -1)))
    hidden = tokens + low_back(jnp.dot(attended, w_output.T, precision=HIGHEST))
    hn = rms_norm(hidden, gain_two)
    gate_probs = jax.nn.softmax(jnp.dot(hn, router, precision=HIGHEST), axis=-1)
    one_hot = expert_ids[:, None] == jnp.arange(EXPERTS, dtype=jnp.int32)[None, :]
    gate = lax.optimization_barrier(jnp.sum(jnp.where(one_hot, gate_probs, 0.0), axis=1))
    one_hot_int = one_hot.astype(jnp.int32)
    ranks = (jnp.cumsum(one_hot_int.reshape(-1, TOK_DEV, EXPERTS), axis=1).astype(jnp.int32) - 1).reshape(-1, EXPERTS)
    rank_own = lax.optimization_barrier(jnp.sum(ranks * one_hot_int, axis=1)).astype(jnp.int32)
    block_id = (jnp.arange(count_rows, dtype=jnp.int32) // TOK_DEV).astype(jnp.int32)
    whole_cap = N_DP * N_ROW * CAP
    slot_ids = expert_ids * whole_cap + block_id * CAP + rank_own
    expert_rows = low(low_back(hn))
    boxes = jnp.zeros((EXPERTS * whole_cap, D), hn.dtype).at[slot_ids].set(expert_rows).reshape(EXPERTS, whole_cap, D)
    results = lax.map(jax.checkpoint(expert_block), (boxes, w_in, w_out))
    expert_out = low(low_back(results.reshape(-1, D)[slot_ids]))
    return hidden + gate[:, None] * expert_out

def reference(tokens, grad_out, routes, norm1_gain, w_query, w_key, w_value, w_output, rel_table, rel_bucket, norm2_gain, router, w_in, w_out):
    bucket_hot = (rel_bucket[None, :] == jnp.arange(NBUCKET, dtype=jnp.int32)[:, None]).astype(jnp.float32)
    expert_ids = routes[:, 0].astype(jnp.int32)

    def layer(tokens_f, gain_one, query_f, key_f, value_f, output_f, table_f, gain_two, router_f, in_f, out_f):
        return forward(tokens_f, gain_one, query_f, key_f, value_f, output_f, table_f, gain_two, router_f, in_f, out_f, bucket_hot, expert_ids)
    wide = tuple((array.astype(jnp.float32) for array in (tokens, norm1_gain, w_query, w_key, w_value, w_output, rel_table, norm2_gain, router, w_in, w_out)))
    result, pullback = jax.vjp(layer, *wide)
    grads = pullback(grad_out.astype(jnp.float32))
    return (result.astype(jnp.bfloat16), grads[0], grads[1], grads[2], grads[3], grads[4], grads[5], grads[6], grads[7], grads[8], grads[9], grads[10])
```

```python
import functools

import jax
import jax.numpy as jnp
from jax import lax
from jax.experimental import pallas as pl
from jax.experimental.pallas import tpu as pltpu
from jax.sharding import PartitionSpec as P

H = 12
NBUCKET = 32


EPS = 1e-06
SCALE = 0.125
HIGHEST = lax.Precision.HIGHEST
NARROW = jnp.bfloat16
WIDE = jnp.float32


def gelu_tanh(values):
    return jax.nn.gelu(values, approximate=True)


def norm_forward(rows, gain):
    inverse = lax.rsqrt(jnp.mean(rows * rows, axis=-1, keepdims=True) + EPS)
    return (rows * inverse * gain, inverse)


def norm_backward(rows, inverse, gain, grad_normed):
    scaled = grad_normed * gain
    grad_rows = inverse * scaled - rows * inverse**3 * jnp.mean(
        scaled * rows, axis=-1, keepdims=True
    )
    return (grad_rows, jnp.sum(grad_normed * rows * inverse, axis=0))


def contract_rows(left, right):
    return lax.dot_general(left, right, (((0,), (0,)), ((), ())), preferred_element_type=WIDE)


def contract_cols(left, right):
    return lax.dot_general(left, right, (((1,), (1,)), ((), ())), preferred_element_type=WIDE)


def split_heads(matrix, heads):
    return matrix.reshape(matrix.shape[0], heads, -1).transpose(1, 0, 2)


def join_heads(stacked):
    return stacked.transpose(1, 0, 2).reshape(stacked.shape[1], -1)


def diagonal_sums(block):
    heads, height, breadth = block.shape
    shifted = jnp.pad(block, ((0, 0), (0, 0), (height, 0))).reshape(
        heads, height * (height + breadth)
    )
    shifted = jnp.pad(shifted, ((0, 0), (0, height))).reshape(heads, height, height + breadth + 1)
    totals = jnp.sum(shifted, axis=1, dtype=WIDE)
    return totals[:, 1 : height + breadth]


def bias_block(offsets, query_start, key_start, queries, keys, seq_len):
    heads = offsets.shape[0]
    begin = key_start - query_start + seq_len - queries
    window = lax.dynamic_slice_in_dim(offsets, begin, queries + keys - 1, 1)
    period = queries + keys
    padded = jnp.pad(window, ((0, 0), (0, 1)))
    spread = jnp.broadcast_to(padded[:, None, :], (heads, queries, period)).reshape(
        heads, queries * period
    )
    skewed = spread[:, : queries * (period - 1)].reshape(heads, queries, period - 1)
    return skewed[:, :, queries - 1 : queries - 1 + keys]


def batch_scores(query_heads, key_heads, bias):
    return (
        SCALE * jnp.einsum("hqd,hkd->hqk", query_heads, key_heads, preferred_element_type=WIDE)
        + bias
    )


def local(
    tokens,
    grad_out,
    routes,
    norm1_gain,
    w_query,
    w_key,
    w_value,
    w_output,
    rel_table,
    rel_bucket,
    norm2_gain,
    router,
    w_in,
    w_out,
):
    tok_rows, width = tokens.shape
    seq_len = tok_rows * lax.axis_size("row")
    heads = H // lax.axis_size("col")
    row_start = lax.axis_index("row") * tok_rows
    tokens_wide = tokens.astype(WIDE)
    gain_one = norm1_gain.astype(WIDE)
    normed, inverse_one = norm_forward(tokens_wide, gain_one)
    normed_low = normed.astype(NARROW)
    query_weight, key_weight, value_weight, output_weight = (
        lax.all_gather(w_query, "row", axis=0, tiled=True),
        lax.all_gather(w_key, "row", axis=0, tiled=True),
        lax.all_gather(w_value, "row", axis=0, tiled=True),
        lax.all_gather(w_output, "row", axis=0, tiled=True),
    )
    query = jnp.dot(normed_low, query_weight, preferred_element_type=WIDE).astype(NARROW)
    key = jnp.dot(normed_low, key_weight, preferred_element_type=WIDE).astype(NARROW)
    value = jnp.dot(normed_low, value_weight, preferred_element_type=WIDE).astype(NARROW)
    keys_all, values_all = (
        lax.all_gather(key, "row", axis=0, tiled=True),
        lax.all_gather(value, "row", axis=0, tiled=True),
    )
    bucket_hot = (rel_bucket[None, :] == jnp.arange(NBUCKET, dtype=jnp.int32)[:, None]).astype(WIDE)
    table_local = lax.dynamic_slice_in_dim(
        rel_table.astype(WIDE), lax.axis_index("col") * heads, heads, 1
    )
    offsets = jnp.dot(table_local.T, bucket_hot, precision=HIGHEST)
    bias = bias_block(offsets, row_start, 0, tok_rows, seq_len, seq_len)
    query_heads = split_heads(query, heads)
    key_heads = split_heads(keys_all, heads)
    value_heads = split_heads(values_all, heads)
    scores = batch_scores(query_heads, key_heads, bias)
    ceiling = jnp.max(scores, axis=2, keepdims=True)
    raised = jnp.exp(scores - ceiling)
    summed = jnp.sum(raised, axis=2, keepdims=True)
    attended_heads = jnp.einsum(
        "hqk,hkd->hqd", (raised / summed).astype(NARROW), value_heads, preferred_element_type=WIDE
    )
    log_total = ceiling[:, :, 0] + jnp.log(summed[:, :, 0])
    attended = join_heads(attended_heads).astype(NARROW)
    branch = lax.psum(contract_cols(attended, output_weight), "col")
    hidden = tokens_wide + branch
    gain_two = norm2_gain.astype(WIDE)
    hn, inverse_two = norm_forward(hidden, gain_two)
    router_wide = router.astype(WIDE)
    gate_probs = jax.nn.softmax(jnp.dot(hn, router_wide, precision=HIGHEST), axis=-1)
    n_exp = router.shape[1]
    capacity = 2 * tok_rows // n_exp
    expert_ids = routes[:, 0]
    one_hot_int = (expert_ids[:, None] == jnp.arange(n_exp, dtype=jnp.int32)[None, :]).astype(
        jnp.int32
    )
    one_hot = one_hot_int.astype(WIDE)
    gate = jnp.sum(gate_probs * one_hot, axis=1)
    rank_own = jnp.sum((jnp.cumsum(one_hot_int, axis=0) - 1) * one_hot_int, axis=1)
    slot_ids = expert_ids * capacity + rank_own
    grad_wide = grad_out.astype(WIDE)
    send_rows = hn.astype(NARROW)
    send_grads = (gate[:, None] * grad_wide).astype(NARROW)
    box_rows = (
        jnp.zeros((n_exp * capacity, width), NARROW)
        .at[slot_ids]
        .set(send_rows)
        .reshape(n_exp, capacity, width)
    )
    box_grads = (
        jnp.zeros((n_exp * capacity, width), NARROW)
        .at[slot_ids]
        .set(send_grads)
        .reshape(n_exp, capacity, width)
    )
    got_rows, got_grads = (
        lax.all_to_all(box_rows, "row", split_axis=0, concat_axis=0, tiled=True),
        lax.all_to_all(box_grads, "row", split_axis=0, concat_axis=0, tiled=True),
    )
    expert_in = got_rows.reshape(-1, width)
    expert_grad = got_grads.reshape(-1, width)
    weight_in = w_in[0]
    weight_out = w_out[0]
    pre = jnp.dot(expert_in, weight_in, preferred_element_type=WIDE)
    act, act_back = jax.vjp(gelu_tanh, pre)
    act_low = act.astype(NARROW)
    out_part = contract_cols(act_low, weight_out)
    grad_act = jnp.dot(expert_grad, weight_out, preferred_element_type=WIDE)
    grad_pre = act_back(grad_act)[0].astype(NARROW)
    rows_part = contract_cols(grad_pre, weight_in)
    grad_weight_in = contract_rows(expert_in, grad_pre)
    grad_weight_out = contract_rows(expert_grad, act_low)
    out_sum, rows_sum = lax.psum((out_part, rows_part), "col")
    back_out, back_rows = (
        lax.all_to_all(
            out_sum.astype(NARROW).reshape(n_exp, capacity, width),
            "row",
            split_axis=0,
            concat_axis=0,
            tiled=True,
        ),
        lax.all_to_all(
            rows_sum.astype(NARROW).reshape(n_exp, capacity, width),
            "row",
            split_axis=0,
            concat_axis=0,
            tiled=True,
        ),
    )
    expert_out = back_out.reshape(-1, width)[slot_ids].astype(WIDE)
    grad_rows = back_rows.reshape(-1, width)[slot_ids].astype(WIDE)
    output = (hidden + gate[:, None] * expert_out).astype(NARROW)
    grad_in_shard, grad_out_shard = (
        lax.psum_scatter(
            grad_weight_in.astype(jnp.bfloat16), "dp", scatter_dimension=0, tiled=True
        ).astype(jnp.float32),
        lax.psum_scatter(
            grad_weight_out.astype(jnp.bfloat16), "dp", scatter_dimension=0, tiled=True
        ).astype(jnp.float32),
    )
    grad_gate = jnp.sum(grad_wide * expert_out, axis=1)
    grad_logits = (grad_gate * gate)[:, None] * (one_hot - gate_probs)
    grad_router = jnp.dot(hn.T, grad_logits, precision=HIGHEST)
    grad_hn = grad_rows + jnp.dot(grad_logits, router_wide.T, precision=HIGHEST)
    grad_hidden_norm, grad_gain_two = norm_backward(hidden, inverse_two, gain_two, grad_hn)
    grad_hidden = grad_wide + grad_hidden_norm
    grad_branch = grad_hidden.astype(NARROW)
    grad_w_output = contract_rows(grad_branch, attended)
    grad_attended = jnp.dot(grad_branch, output_weight, preferred_element_type=WIDE).astype(NARROW)
    grad_heads = split_heads(grad_attended, heads)
    diagonal_start = seq_len - row_start - tok_rows
    shares = jnp.exp(batch_scores(query_heads, key_heads, bias) - log_total[:, :, None])
    grad_shares = jnp.einsum("hqd,hkd->hqk", grad_heads, value_heads, preferred_element_type=WIDE)
    deltas = jnp.sum(shares * grad_shares, axis=2)
    grad_scores = (shares * (grad_shares - deltas[:, :, None])).astype(NARROW)
    grad_query_heads = SCALE * jnp.einsum(
        "hqk,hkd->hqd", grad_scores, key_heads, preferred_element_type=WIDE
    )
    diagonals = diagonal_sums(grad_scores)
    bucket_window = lax.dynamic_slice_in_dim(bucket_hot, diagonal_start, tok_rows + seq_len - 1, 1)
    table_part = jnp.dot(bucket_window, diagonals.T, precision=HIGHEST)
    grad_key_heads = SCALE * jnp.einsum(
        "hqk,hqd->hkd", grad_scores, query_heads, preferred_element_type=WIDE
    )
    grad_value_heads = jnp.einsum(
        "hqk,hqd->hkd", shares.astype(NARROW), grad_heads, preferred_element_type=WIDE
    )
    grad_key, grad_value = (
        lax.psum_scatter(
            join_heads(grad_key_heads).astype(jnp.bfloat16), "row", scatter_dimension=0, tiled=True
        ).astype(jnp.float32),
        lax.psum_scatter(
            join_heads(grad_value_heads).astype(jnp.bfloat16),
            "row",
            scatter_dimension=0,
            tiled=True,
        ).astype(jnp.float32),
    )
    grad_query = join_heads(grad_query_heads).astype(NARROW)
    grad_key_low = grad_key.astype(NARROW)
    grad_value_low = grad_value.astype(NARROW)
    grad_w_query = contract_rows(normed_low, grad_query)
    grad_w_key = contract_rows(normed_low, grad_key_low)
    grad_w_value = contract_rows(normed_low, grad_value_low)
    normed_part = (
        contract_cols(grad_query, query_weight)
        + contract_cols(grad_key_low, key_weight)
        + contract_cols(grad_value_low, value_weight)
    )
    grad_normed = lax.psum(normed_part.astype(jnp.bfloat16), "col").astype(jnp.float32)
    grad_tokens_norm, grad_gain_one = norm_backward(tokens_wide, inverse_one, gain_one, grad_normed)
    grad_tokens = grad_hidden + grad_tokens_norm
    grad_table = lax.psum(table_part, ("dp", "row"))
    (
        grads_query,
        grads_key,
        grads_value,
        grads_output,
        grads_gain_one,
        grads_gain_two,
        grads_router,
    ) = (
        lax.psum_scatter(grad_w_query, ("dp", "row"), scatter_dimension=0, tiled=True),
        lax.psum_scatter(grad_w_key, ("dp", "row"), scatter_dimension=0, tiled=True),
        lax.psum_scatter(grad_w_value, ("dp", "row"), scatter_dimension=0, tiled=True),
        lax.psum_scatter(grad_w_output, ("dp", "row"), scatter_dimension=0, tiled=True),
        lax.psum_scatter(grad_gain_one, ("dp", "row"), scatter_dimension=0, tiled=True),
        lax.psum_scatter(grad_gain_two, ("dp", "row"), scatter_dimension=0, tiled=True),
        lax.psum_scatter(grad_router, ("dp", "row"), scatter_dimension=0, tiled=True),
    )
    return (
        output,
        grad_tokens,
        grads_gain_one,
        grads_query,
        grads_key,
        grads_value,
        grads_output,
        grad_table,
        grads_gain_two,
        grads_router,
        grad_in_shard[None],
        grad_out_shard[None],
    )


VMEM = pltpu.VMEM
SMEM = pltpu.SMEM


def dot_nn(a, b):
    return lax.dot_general(a, b, (((1,), (0,)), ((), ())), preferred_element_type=WIDE)


def dot_nt(a, b):
    return lax.dot_general(a, b, (((1,), (1,)), ((), ())), preferred_element_type=WIDE)


def dot_tn(a, b):
    return lax.dot_general(a, b, (((0,), (0,)), ((), ())), preferred_element_type=WIDE)


def full_spec(shape):
    return pl.BlockSpec(shape, lambda *_: (0,) * len(shape))


def smem_spec():
    return pl.BlockSpec(memory_space=SMEM)


def params(megabytes=48):
    return pltpu.CompilerParams(vmem_limit_bytes=megabytes * 1024 * 1024)


def cost(flops, moved):
    return pl.CostEstimate(flops=int(flops), bytes_accessed=int(moved), transcendentals=0)


def shape_of(shape, dtype):
    return jax.ShapeDtypeStruct(shape, dtype)


def project_kernel(place, tok, gain, w_own, w_oth, normed, q, k, v, w_all):
    half = w_own.shape[0]
    row = place[0]

    @pl.when(jnp.logical_and(pl.program_id(0) == 0, row == 0))
    def _():
        w_all[:half] = w_own[...]
        w_all[half:] = w_oth[...]

    @pl.when(jnp.logical_and(pl.program_id(0) == 0, row == 1))
    def _():
        w_all[:half] = w_oth[...]
        w_all[half:] = w_own[...]

    rows = tok[...].astype(WIDE)
    inverse = lax.rsqrt(jnp.mean(rows * rows, axis=-1, keepdims=True) + EPS)
    low = (rows * inverse * gain[...].astype(WIDE)).astype(NARROW)
    normed[...] = low
    out = dot_nn(low, w_all[...])
    heads, _, size = q.shape
    wide = heads * size
    for h in range(heads):
        q[h] = (out[:, h * size : (h + 1) * size] * SCALE).astype(NARROW)
        k[h] = out[:, wide + h * size : wide + (h + 1) * size].astype(NARROW)
        v[h] = out[:, 2 * wide + h * size : 2 * wide + (h + 1) * size].astype(NARROW)


def project(place, tok_all, gain, w_own, w_oth, heads, size, block):
    seq, width = tok_all.shape
    cols = w_own.shape[1]
    head_spec = pl.BlockSpec((heads, block, size), lambda i: (0, i, 0))
    row_spec = pl.BlockSpec((block, width), lambda i: (i, 0))
    head_shape = shape_of((heads, seq, size), NARROW)
    return pl.pallas_call(
        project_kernel,
        grid=(seq // block,),
        in_specs=[smem_spec(), row_spec, full_spec(gain.shape), full_spec(w_own.shape), full_spec(w_oth.shape)],
        out_specs=[row_spec, head_spec, head_spec, head_spec, full_spec((width, cols))],
        out_shape=[shape_of((seq, width), NARROW)] + [head_shape] * 3 + [shape_of((width, cols), NARROW)],
        compiler_params=params(),
        cost_estimate=cost(2 * seq * width * cols, 4 * seq * width * 2),
        name="project",
    )(place, tok_all, gain, w_own, w_oth)


TILE = 128


def bias_lanes(row, block_index, blocks):
    half = blocks // 2
    query = lax.rem(block_index + half * row, blocks)
    own = half * row - query + blocks
    other = half * (1 - row) - query + blocks
    return pl.multiple_of(own * TILE, TILE), pl.multiple_of(other * TILE, TILE)


def attend_kernel(first, place, bucket, table, q, k, v, att, p, skew):
    heads, block, size = q.shape
    seq = k.shape[1]
    half = seq // 2
    row = place[0]
    step = pl.program_id(0)

    @pl.when(step == 0)
    def _():
        n = bucket.shape[1]
        hot = (bucket[...] == lax.broadcasted_iota(jnp.int32, (NBUCKET, n), 0)).astype(WIDE)
        for h in range(heads):
            line = jnp.sum(hot * table[:, h : h + 1], axis=0, keepdims=True)
            skew[h] = pltpu.roll(jnp.broadcast_to(line, (TILE, n)), 0, 1, stride=1, stride_axis=0)

    for h in range(heads):
        raw = dot_nt(q[h], k[h])
        parts = []
        for sub in range(block // TILE):
            own, other = bias_lanes(row, first + step * (block // TILE) + sub, seq // TILE)
            bias = jnp.concatenate([skew[h, :, pl.ds(own, half)], skew[h, :, pl.ds(other, half)]], axis=1)
            scores = raw[sub * TILE : (sub + 1) * TILE] + bias
            raised = jnp.exp(scores - jnp.max(scores, axis=1, keepdims=True))
            share = raised * (1.0 / jnp.sum(raised, axis=1, keepdims=True))
            parts.append(share.astype(NARROW))
        shares = jnp.concatenate(parts, axis=0)
        p[h] = shares
        att[:, h * size : (h + 1) * size] = dot_nn(shares, v[h]).astype(NARROW)


def attend(place, bucket, table, q, k, v, block, begin, rows):
    heads, seq, size = q.shape
    start = begin // block
    return pl.pallas_call(
        functools.partial(attend_kernel, begin // TILE),
        grid=(rows // block,),
        in_specs=[
            smem_spec(),
            full_spec(bucket.shape),
            full_spec(table.shape),
            pl.BlockSpec((heads, block, size), lambda i: (0, i + start, 0)),
            full_spec(k.shape),
            full_spec(v.shape),
        ],
        out_specs=[
            pl.BlockSpec((block, heads * size), lambda i: (i, 0)),
            pl.BlockSpec((heads, block, seq), lambda i: (0, i, 0)),
        ],
        out_shape=[shape_of((rows, heads * size), NARROW), shape_of((heads, rows, seq), NARROW)],
        scratch_shapes=[VMEM((heads, TILE, bucket.shape[1]), WIDE)],
        compiler_params=params(),
        cost_estimate=cost(8 * heads * rows * seq * 128, heads * rows * seq * 4),
        name="attend",
    )(place, bucket, table, q, k, v)


def attend_back_kernel(first, last, place, bucket, q, k, v, p, g, *refs):
    if first == 0:
        keep_in = None
    else:
        keep_in, refs = refs[:3], refs[3:]
    if last:
        out, table, key_sum, value_sum, diag = refs
        query_out = None
    else:
        query_out, key_sum, value_sum, diag = refs
        out = None
    heads, block, size = q.shape
    seq = k.shape[1]
    half = seq // 2
    row = place[0]
    step = pl.program_id(0)

    @pl.when(step == 0)
    def _():
        if keep_in is None:
            key_sum[...] = jnp.zeros_like(key_sum)
            value_sum[...] = jnp.zeros_like(value_sum)
            diag[...] = jnp.zeros_like(diag)
        else:
            key_sum[...] = keep_in[0][...]
            value_sum[...] = keep_in[1][...]
            diag[...] = keep_in[2][...]

    wide = heads * size
    for h in range(heads):
        grad = g[:, h * size : (h + 1) * size]
        share_low = p[h]
        share = share_low.astype(WIDE)
        grad_share = dot_nt(grad, v[h])
        delta = jnp.sum(share * grad_share, axis=1, keepdims=True)
        grad_score = share * (grad_share - delta)
        for sub in range(block // TILE):
            own, other = bias_lanes(row, first + step * (block // TILE) + sub, seq // TILE)
            piece = grad_score[sub * TILE : (sub + 1) * TILE]
            diag[h, :, pl.ds(own, half)] += piece[:, :half]
            diag[h, :, pl.ds(other, half)] += piece[:, half:]
        low = grad_score.astype(NARROW)
        grad_query = (SCALE * dot_nn(low, k[h])).astype(NARROW)
        if last:
            out[pl.ds(pl.multiple_of(first * TILE + step * block, block), block), h * size : (h + 1) * size] = grad_query
        else:
            query_out[:, h * size : (h + 1) * size] = grad_query
        key_sum[h] += dot_tn(q[h], low)
        value_sum[h] += dot_tn(grad, share_low)

    if last:
        lanes = diag.shape[2]

        @pl.when(step == pl.num_programs(0) - 1)
        def _():
            hot = (bucket[...] == lax.broadcasted_iota(jnp.int32, (NBUCKET, lanes), 0)).astype(WIDE)
            lane = lax.broadcasted_iota(jnp.int32, table.shape, 1)
            total = jnp.zeros(table.shape, WIDE)
            for h in range(heads):
                lo = h * size
                out[:, wide + lo : wide + lo + size] = key_sum[h].T.astype(NARROW)
                out[:, 2 * wide + lo : 2 * wide + lo + size] = value_sum[h].T.astype(NARROW)
                sums = diag[h]
                height = TILE // 2
                while height >= 8:
                    sums = sums[:height] + pltpu.roll(sums[height:], lanes - height, 1)
                    height //= 2
                where = lax.broadcasted_iota(jnp.int32, sums.shape, 0)
                for bit in (4, 2, 1):
                    sums = jnp.where((where & bit) != 0, pltpu.roll(sums, lanes - bit, 1), sums)
                line = jnp.sum(sums, axis=0, keepdims=True)
                total = total + jnp.where(lane == h, jnp.sum(hot * line, axis=1, keepdims=True), 0.0)
            table[...] = total


def attend_back(place, bucket, q, k, v, p, g, block, begin, keep):
    heads, seq, size = q.shape
    rows = g.shape[0]
    start = begin // block
    last = keep is not None
    lanes = bucket.shape[1]
    sum_shape = (heads, size, seq)
    diag_shape = (heads, TILE, lanes)
    wide = heads * size
    in_specs = [
        smem_spec(),
        full_spec(bucket.shape),
        pl.BlockSpec((heads, block, size), lambda i: (0, i + start, 0)),
        full_spec(k.shape),
        full_spec(v.shape),
        pl.BlockSpec((heads, block, seq), lambda i: (0, i, 0)),
        pl.BlockSpec((block, wide), lambda i: (i, 0)),
    ]
    args = [place, bucket, q, k, v, p, g]
    sums = [shape_of(sum_shape, WIDE), shape_of(sum_shape, WIDE), shape_of(diag_shape, WIDE)]
    if last:
        in_specs += [full_spec(s.shape) for s in sums]
        args += list(keep[1:])
        in_specs += [full_spec(keep[0].shape)]
        args += [keep[0]]
        out_specs = [full_spec((seq, 3 * wide)), full_spec((NBUCKET, 128))]
        out_shape = [shape_of((seq, 3 * wide), NARROW), shape_of((NBUCKET, 128), WIDE)]
        scratch = [VMEM(s.shape, WIDE) for s in sums]

        def kernel(*refs):
            earlier = refs[10]
            out = refs[11]

            @pl.when(pl.program_id(0) == 0)
            def _():
                out[: earlier.shape[0], :wide] = earlier[...]

            attend_back_kernel(begin // TILE, True, *refs[:10], *refs[11:])

    else:
        out_specs = [pl.BlockSpec((block, wide), lambda i: (i, 0))] + [full_spec(s.shape) for s in sums]
        out_shape = [shape_of((rows, wide), NARROW)] + sums
        scratch = []
        kernel = functools.partial(attend_back_kernel, begin // TILE, False)
    return pl.pallas_call(
        kernel,
        grid=(rows // block,),
        in_specs=in_specs,
        out_specs=out_specs,
        out_shape=out_shape,
        scratch_shapes=scratch,
        compiler_params=params(),
        cost_estimate=cost(14 * heads * rows * seq * 128, heads * rows * seq * 4),
        name="attend_back",
    )(*args)


def gate_values(hn, route, router):
    count = router.shape[0]
    logits = [jnp.sum(hn * router[e : e + 1], axis=1, keepdims=True) for e in range(count)]
    top = functools.reduce(jnp.maximum, logits)
    raised = [jnp.exp(x - top) for x in logits]
    total = functools.reduce(jnp.add, raised)
    probs = [x / total for x in raised]
    hots = [(route == e).astype(WIDE) for e in range(count)]
    gate = functools.reduce(jnp.add, [p * o for p, o in zip(probs, hots)])
    return probs, hots, gate


def hidden_kernel(place, a_mine, a_row, a_col, a_diag, w_mine, w_other, tok, gain, router, route, grad, hidden, att, rows, grads, pack):
    row = place[0]
    step = pl.program_id(0)
    size = a_mine.shape[1]

    @pl.when(row == 0)
    def _():
        pack[0, :, :size] = a_mine[...]
        pack[0, :, size:] = a_row[...]
        pack[1, :, :size] = a_col[...]
        pack[1, :, size:] = a_diag[...]

    @pl.when(row == 1)
    def _():
        pack[0, :, size:] = a_mine[...]
        pack[0, :, :size] = a_row[...]
        pack[1, :, size:] = a_col[...]
        pack[1, :, :size] = a_diag[...]

    branch = dot_nt(pack[0], w_mine[...]) + dot_nt(pack[1], w_other[...])
    wide = tok[...].astype(WIDE) + branch

    @pl.when(step < 2)
    def _():
        hidden[...] = wide
        att[...] = pack[0]

    inverse = lax.rsqrt(jnp.mean(wide * wide, axis=-1, keepdims=True) + EPS)
    hn = wide * inverse * gain[...].astype(WIDE)
    kind = route[...]
    _, hots, gate = gate_values(hn, kind, router)
    chosen = jnp.where(kind == row, 1.0, 0.0)
    rows[...] = (hn * chosen).astype(NARROW)
    grads[...] = (grad[...].astype(WIDE) * (gate * chosen)).astype(NARROW)


def hidden_rows(place, pieces, w_mine, w_other, tok_all, gain, router, route_all, grad_all):
    seq, width = tok_all.shape
    block = seq // 4
    size = pieces[0].shape[1]
    half = w_mine.shape[1]
    turned = pl.BlockSpec((block, size), lambda i: (lax.rem(i + 2, 4), 0))
    plain = pl.BlockSpec((block, size), lambda i: (i, 0))
    wide_spec = pl.BlockSpec((block, width), lambda i: (i, 0))
    own_spec = pl.BlockSpec((block, width), lambda i: (jnp.minimum(i, 1), 0))
    mixed = pl.BlockSpec((block, width), lambda i: (lax.rem(i, 2) * 2 + lax.div(i, 2), 0))
    return pl.pallas_call(
        hidden_kernel,
        grid=(4,),
        in_specs=[
            smem_spec(),
            plain,
            turned,
            plain,
            turned,
            full_spec(w_mine.shape),
            full_spec(w_other.shape),
            wide_spec,
            full_spec(gain.shape),
            full_spec(router.shape),
            pl.BlockSpec((block, 1), lambda i: (i, 0)),
            wide_spec,
        ],
        out_specs=[own_spec, pl.BlockSpec((block, half), lambda i: (jnp.minimum(i, 1), 0)), mixed, mixed],
        out_shape=[
            shape_of((seq // 2, width), WIDE),
            shape_of((seq // 2, half), NARROW),
            shape_of((seq, width), NARROW),
            shape_of((seq, width), NARROW),
        ],
        scratch_shapes=[VMEM((2, block, half), NARROW)],
        compiler_params=params(),
        cost_estimate=cost(2 * seq * width * width, 5 * seq * width * 2),
        name="hidden_rows",
    )(place, *pieces, w_mine, w_other, tok_all, gain, router, route_all, grad_all)


def expert_out_kernel(x, w_in, w_out, act, slope, out, total):
    step = pl.program_id(0)
    pre = dot_nn(x[...], w_in[...])
    square = pre * pre
    bent = jnp.tanh(0.7978845608028654 * pre * (1.0 + 0.044715 * square))
    act_low = (0.5 * pre * (1.0 + bent)).astype(NARROW)
    act[...] = act_low
    inner = 0.7978845608028654 * (1.0 + 0.134145 * square)
    slope[...] = (0.5 * (1.0 + bent) + 0.5 * pre * (1.0 - bent * bent) * inner).astype(NARROW)
    piece = dot_nt(act_low, w_out[...])

    @pl.when(step == 0)
    def _():
        total[...] = piece

    @pl.when(step > 0)
    def _():
        total[...] += piece

    @pl.when(step == pl.num_programs(0) - 1)
    def _():
        out[...] = total[...].astype(NARROW)


def expert_back_kernel(g, slope, w_in, w_out, grad_pre, out, total):
    step = pl.program_id(0)
    low = (dot_nn(g[...], w_out[...]) * slope[...].astype(WIDE)).astype(NARROW)
    grad_pre[...] = low
    piece = dot_nt(low, w_in[...])

    @pl.when(step == 0)
    def _():
        total[...] = piece

    @pl.when(step > 0)
    def _():
        total[...] += piece

    @pl.when(step == pl.num_programs(0) - 1)
    def _():
        out[...] = total[...].astype(NARROW)


def expert_forward(x, w_in, w_out, block):
    seq, width = x.shape
    units = w_in.shape[1]
    w_spec = pl.BlockSpec((width, block), lambda i: (0, i))
    unit_spec = pl.BlockSpec((seq, block), lambda i: (0, i))
    return pl.pallas_call(
        expert_out_kernel,
        grid=(units // block,),
        in_specs=[full_spec(x.shape), w_spec, w_spec],
        out_specs=[unit_spec, unit_spec, full_spec(x.shape)],
        out_shape=[shape_of((seq, units), NARROW)] * 2 + [shape_of(x.shape, NARROW)],
        scratch_shapes=[VMEM(x.shape, WIDE)],
        compiler_params=params(),
        cost_estimate=cost(4 * seq * width * units, 4 * seq * units),
        name="expert_forward",
    )(x, w_in, w_out)


def expert_backward(g, slope, w_in, w_out, block):
    seq, width = g.shape
    units = w_in.shape[1]
    w_spec = pl.BlockSpec((width, block), lambda i: (0, i))
    unit_spec = pl.BlockSpec((seq, block), lambda i: (0, i))
    return pl.pallas_call(
        expert_back_kernel,
        grid=(units // block,),
        in_specs=[full_spec(g.shape), unit_spec, w_spec, w_spec],
        out_specs=[unit_spec, full_spec(g.shape)],
        out_shape=[shape_of((seq, units), NARROW), shape_of(g.shape, NARROW)],
        scratch_shapes=[VMEM(g.shape, WIDE)],
        compiler_params=params(),
        cost_estimate=cost(4 * seq * width * units, 4 * seq * units),
        name="expert_backward",
    )(g, slope, w_in, w_out)


def weight_grad_kernel(left, right, out):
    out[...] = dot_tn(left[...], right[...]).astype(NARROW)


def weight_grad(left, right, block):
    seq, width = left.shape
    units = right.shape[1]
    return pl.pallas_call(
        weight_grad_kernel,
        grid=(units // block,),
        in_specs=[full_spec(left.shape), pl.BlockSpec((seq, block), lambda i: (0, i))],
        out_specs=pl.BlockSpec((width, block), lambda i: (0, i)),
        out_shape=shape_of((width, units), NARROW),
        compiler_params=params(),
        cost_estimate=cost(2 * seq * width * units, 4 * seq * units),
        name="weight_grad",
    )(left, right)


def combine_kernel(place, hidden, out_mine, out_got, rows_mine, rows_got, grad, route, gain, router, w_mine, att, output, grad_hidden, sums, back_own, back_send, w_grad, grad_y):
    row, col = place[0], place[1]
    block = out_mine.shape[0]
    count = router.shape[0]
    size = back_own.shape[1]
    gain_wide = gain[...].astype(WIDE)
    total = [jnp.zeros((1, gain_wide.shape[1]), WIDE) for _ in range(1 + count)]
    for half in range(2):
        part = pl.ds(half * block, block)
        mine = col == half
        expert_out = jnp.where(mine, out_mine[...].astype(WIDE), out_got[...].astype(WIDE))
        grad_rows = jnp.where(mine, rows_mine[...].astype(WIDE), rows_got[...].astype(WIDE))
        wide = hidden[part, :]
        grad_wide = grad[part, :].astype(WIDE)
        inverse = lax.rsqrt(jnp.mean(wide * wide, axis=-1, keepdims=True) + EPS)
        scaled = wide * inverse
        hn = scaled * gain_wide
        probs, hots, gate = gate_values(hn, route[part, :], router)
        output[part, :] = (wide + gate * expert_out).astype(NARROW)
        grad_gate = jnp.sum(grad_wide * expert_out, axis=1, keepdims=True) * gate
        grad_hn = grad_rows
        for e in range(count):
            grad_logit = grad_gate * (hots[e] - probs[e])
            grad_hn = grad_hn + grad_logit * router[e : e + 1]
            total[1 + e] += jnp.sum(hn * grad_logit, axis=0, keepdims=True)
        total[0] += jnp.sum(grad_hn * scaled, axis=0, keepdims=True)
        u = grad_hn * gain_wide
        back = grad_wide + inverse * u - wide * (inverse * inverse * inverse) * jnp.mean(u * wide, axis=-1, keepdims=True)
        grad_hidden[part, :] = back
        low = back.astype(NARROW)
        grad_y[part, :] = low
        grad_att = dot_nn(low, w_mine[...]).astype(NARROW)

        @pl.when(row == 0)
        def _():
            back_own[part, :] = grad_att[:, :size]
            back_send[part, :] = grad_att[:, size:]

        @pl.when(row == 1)
        def _():
            back_own[part, :] = grad_att[:, size:]
            back_send[part, :] = grad_att[:, :size]

    line = lax.broadcasted_iota(jnp.int32, sums.shape, 0)
    packed = jnp.zeros(sums.shape, WIDE)
    for e in range(1 + count):
        packed = packed + jnp.where(line == e, total[e], 0.0)
    sums[...] = packed
    w_grad[...] = dot_tn(grad_y[...], att[...]).astype(NARROW)


def combine(place, hidden, outs, backs, grad, route, gain, router, w_mine, att, size):
    tokens, width = hidden.shape
    half = w_mine.shape[1]
    args = (place, hidden, *outs, *backs, grad, route, gain, router, w_mine, att)
    shapes = [
        shape_of((tokens, width), NARROW),
        shape_of((tokens, width), WIDE),
        shape_of((8, width), WIDE),
        shape_of((tokens, size), NARROW),
        shape_of((tokens, size), NARROW),
        shape_of((width, half), NARROW),
    ]
    return pl.pallas_call(
        combine_kernel,
        in_specs=[smem_spec()] + [pl.BlockSpec(memory_space=VMEM)] * (len(args) - 1),
        out_specs=[pl.BlockSpec(memory_space=VMEM)] * len(shapes),
        out_shape=shapes,
        scratch_shapes=[VMEM((tokens, width), NARROW)],
        compiler_params=params(),
        cost_estimate=cost(4 * tokens * width * half, 8 * tokens * width * 2),
        name="combine",
    )(*args)


def project_back_kernel(g, normed, w_all, tok, sums, w_grad, grad_normed):
    seq = g.shape[0]
    cols = g.shape[1]
    width = tok.shape[1]
    total = jnp.zeros((1, width), WIDE)
    block = seq // 4
    for i in range(4):
        part = pl.ds(i * block, block)
        back = dot_nt(g[part, :], w_all[...])
        rows = tok[part, :].astype(WIDE)
        inverse = lax.rsqrt(jnp.mean(rows * rows, axis=-1, keepdims=True) + EPS)
        total = total + jnp.sum(back * rows * inverse, axis=0, keepdims=True)
        grad_normed[pl.ds((i % 2) * 2 * block + (i // 2) * block, block), :] = back.astype(NARROW)
    w_grad[:, :cols] = dot_tn(normed[...], g[...]).astype(NARROW)
    line = lax.broadcasted_iota(jnp.int32, (128, width), 0)
    lines = jnp.where(line == 0, total, 0.0)
    for e in range(3):
        lines = lines + jnp.where(line == 1 + e, sums[e : e + 1], 0.0)
    w_grad[:, cols:] = lines.T[:, : w_grad.shape[1] - cols].astype(NARROW)


def project_back(g, normed, w_all, tok_all, sums):
    seq, width = tok_all.shape
    cols = g.shape[1]
    args = (g, normed, w_all, tok_all, sums)
    return pl.pallas_call(
        project_back_kernel,
        in_specs=[pl.BlockSpec(memory_space=VMEM)] * len(args),
        out_specs=[pl.BlockSpec(memory_space=VMEM)] * 2,
        out_shape=[shape_of((width, cols + 64), NARROW), shape_of((seq, width), NARROW)],
        compiler_params=params(),
        cost_estimate=cost(4 * seq * width * cols, 4 * seq * width * 2),
        name="project_back",
    )(*args)


def finish_kernel(place, tok, gain, grad_hidden, mine, got, out):
    col = place[1]
    block = mine.shape[0]
    gain_wide = gain[...].astype(WIDE)
    for half in range(2):
        part = pl.ds(half * block, block)
        grad_normed = jnp.where(col == half, mine[...].astype(WIDE), got[...].astype(WIDE))
        rows = tok[part, :].astype(WIDE)
        inverse = lax.rsqrt(jnp.mean(rows * rows, axis=-1, keepdims=True) + EPS)
        u = grad_normed * gain_wide
        out[part, :] = grad_hidden[part, :] + inverse * u - rows * (inverse * inverse * inverse) * jnp.mean(u * rows, axis=-1, keepdims=True)


def finish(place, tok, gain, grad_hidden, mine, got):
    args = (place, tok, gain, grad_hidden, mine, got)
    return pl.pallas_call(
        finish_kernel,
        in_specs=[smem_spec()] + [pl.BlockSpec(memory_space=VMEM)] * (len(args) - 1),
        out_specs=pl.BlockSpec(memory_space=VMEM),
        out_shape=shape_of(tok.shape, WIDE),
        compiler_params=params(),
        cost_estimate=cost(tok.size * 16, tok.size * 12),
        name="finish",
    )(*args)


def swap(value, axis, flip=1):
    size = lax.axis_size(axis)
    return lax.ppermute(value, axis, [(i, i ^ flip) for i in range(size)])


def pick(value, index, axis=0):
    return lax.dynamic_index_in_dim(value, index, axis, keepdims=False)


def in_order(first, mine, got, axis=0):
    return jnp.where(first, jnp.concatenate([mine, got], axis), jnp.concatenate([got, mine], axis))


def from_other_row(value, col):
    half = value.shape[0] // 2
    got = swap(lax.dynamic_slice_in_dim(value, col * half, half, 0), "row")
    return in_order(col == 0, got, swap(got, "col"))


def sum_to_rows(part, col):
    rows = part.shape[0]
    halves = part.reshape(2, rows // 2, -1)
    got = swap(pick(halves, 1 - col), "col")
    both = (pick(halves, col).astype(WIDE) + got.astype(WIDE)).astype(NARROW).reshape(2, rows // 4, -1)
    mine = (both[0].astype(WIDE) + swap(both[1], "row").astype(WIDE)).astype(NARROW)
    return mine, swap(mine, "col")


def add_low(a, b):
    return (a.astype(WIDE) + b.astype(WIDE)).astype(NARROW)


def scatter_dp(value, order):
    count = lax.axis_size("dp")
    place = lax.axis_index("dp")
    bits = count.bit_length() - 1
    rows = value.shape[0] // count
    value = value.reshape((2,) * bits + (rows, value.shape[1]))
    left = list(range(bits - 1, -1, -1))
    for bit in order:
        axis = left.index(bit)
        at = (place >> bit) & 1
        got = swap(pick(value, 1 - at, axis), "dp", 1 << bit)
        value = add_low(pick(value, at, axis), got)
        left.remove(bit)
    return value


def sum_dp(value):
    count = lax.axis_size("dp")
    flip = 1
    while flip < count:
        value = value + swap(value, "dp", flip)
        flip *= 2
    return value


def local_pair(tokens, grad_out, routes, norm1_gain, w_query, w_key, w_value, w_output, rel_table, rel_bucket, norm2_gain, router, w_in, w_out):
    tok_rows, width = tokens.shape
    seq = 2 * tok_rows
    row, col = lax.axis_index("row"), lax.axis_index("col")
    place = jnp.stack([row, col]).astype(jnp.int32)
    col_heads = H // lax.axis_size("col")
    heads = col_heads // 2
    size = w_query.shape[1] // col_heads
    wide = heads * size

    stacked = jnp.stack([w_query, w_key, w_value], 1).reshape(w_query.shape[0], 3, 2, wide)
    w_own = pick(stacked, row, 2).reshape(w_query.shape[0], 3 * wide)
    w_oth = swap(pick(stacked, 1 - row, 2).reshape(w_query.shape[0], 3 * wide), "row")
    tok_all = jnp.concatenate([tokens, from_other_row(tokens, col)], 0)
    gain_one, gain_two = norm1_gain[None, :], norm2_gain[None, :]

    table = lax.dynamic_slice_in_dim(rel_table.astype(WIDE), col * col_heads + row * heads, heads, 1)
    bucket = jnp.pad(rel_bucket[None, :], ((0, 0), (1, 0)), constant_values=-1)
    router_lines = router.astype(WIDE).T

    normed, q, k, v, w_all = project(place, tok_all, gain_one, w_own, w_oth, heads, size, 256)

    grad_all = jnp.concatenate([grad_out, from_other_row(grad_out, col)], 0)
    kinds = routes.astype(WIDE).reshape(-1, 128)
    kinds_all = jnp.concatenate([kinds, swap(kinds, "row")], 0).reshape(seq, 1).astype(jnp.int32)
    w_mine = in_order(row == 0, w_output, swap(w_output, "row"))
    w_other = swap(w_mine, "col")

    att, shares = attend(place, bucket, table, q, k, v, 256, 0, seq)
    att_row = swap(att, "row")
    pieces = (att, att_row, swap(att, "col"), swap(att_row, "col"))
    hidden, att_own, rows, grads = hidden_rows(place, pieces, w_mine, w_other, tok_all, gain_two, router_lines, kinds_all, grad_all)

    weight_in, weight_out = w_in[0], w_out[0]
    act, slope, out_part = expert_forward(rows, weight_in, weight_out, 512)
    grad_pre, rows_part = expert_backward(grads, slope, weight_in, weight_out, 512)
    outs = sum_to_rows(out_part, col)
    backs = sum_to_rows(rows_part, col)
    grad_in = weight_grad(rows, grad_pre, 512)
    grad_out_w = weight_grad(grads, act, 512)
    grad_in_shard = scatter_dp(grad_in, (0, 1, 2)).astype(WIDE)
    grad_out_shard = scatter_dp(grad_out_w, (1, 0, 2)).astype(WIDE)

    output, grad_hidden, sums, back_own, back_send, grad_wo = combine(
        place, hidden, outs, backs, grad_out, routes, gain_two, router_lines, w_mine, att_own, wide
    )
    back_oth = swap(back_send, "row")
    keep = attend_back(place, bucket, q, k, v, shares[:, :tok_rows], back_own, 256, 0, None)
    g, table_part = attend_back(place, bucket, q, k, v, shares[:, tok_rows:], back_oth, 256, tok_rows, keep)

    w_part, normed_part = project_back(g, normed, w_all, tok_all, sums)
    normed_sums = sum_to_rows(normed_part, col)
    grad_tokens = finish(place, tokens, gain_one, grad_hidden, *normed_sums)

    part = scatter_dp(jnp.concatenate([w_part, grad_wo], 1), (0, 1, 2))
    per_row = part.shape[0] // 2
    halves = part.reshape(2, per_row, -1)
    mine, got = pick(halves, row).astype(WIDE), swap(pick(halves, 1 - row), "row").astype(WIDE)
    wqkv = 3 * wide

    def columns(i):
        return in_order(row == 0, mine[:, i * wide : (i + 1) * wide], got[:, i * wide : (i + 1) * wide], 1)

    small = mine[:, wqkv : wqkv + 4] + got[:, wqkv : wqkv + 4]
    grads_gain_one = small[:, 0] + swap(small[:, 0], "col")
    grads_output = mine[:, wqkv + 64 :] + got[:, wqkv + 64 :]

    table_sum = sum_dp(table_part[:, :8])
    grad_table = in_order(row == 0, table_sum[:, :heads], swap(table_sum, "row")[:, :heads], 1)
    return (
        output,
        grad_tokens,
        grads_gain_one,
        columns(0),
        columns(1),
        columns(2),
        grads_output,
        grad_table,
        small[:, 1],
        small[:, 2:4],
        grad_in_shard[None],
        grad_out_shard[None],
    )


def solution(mesh):
    in_specs = (
        P(("dp", "row"), None),
        P(("dp", "row"), None),
        P(("dp", "row"), None),
        P(),
        P("row", "col"),
        P("row", "col"),
        P("row", "col"),
        P("row", "col"),
        P(),
        P(),
        P(),
        P(),
        P("row", None, "col"),
        P("row", None, "col"),
    )
    out_specs = (
        P(("dp", "row"), None),
        P(("dp", "row"), None),
        P(("dp", "row")),
        P(("dp", "row"), "col"),
        P(("dp", "row"), "col"),
        P(("dp", "row"), "col"),
        P(("dp", "row"), "col"),
        P(None, "col"),
        P(("dp", "row")),
        P(("dp", "row"), None),
        P("row", "dp", "col"),
        P("row", "dp", "col"),
    )
    paired = mesh.shape["row"] == 2 and mesh.shape["col"] == 2
    return jax.shard_map(local_pair if paired else local, mesh=mesh, in_specs=in_specs, out_specs=out_specs, check_vma=False)
```

```python
import functools

import jax
import jax.numpy as jnp
from jax import lax
from jax.experimental import pallas as pl
from jax.experimental.pallas import tpu as pltpu
from jax.sharding import PartitionSpec as P

H = 12
NBUCKET = 32


EPS = 1e-06
SCALE = 0.125
HIGHEST = lax.Precision.HIGHEST
NARROW = jnp.bfloat16
WIDE = jnp.float32


def gelu_tanh(values):
    return jax.nn.gelu(values, approximate=True)


def norm_forward(rows, gain):
    inverse = lax.rsqrt(jnp.mean(rows * rows, axis=-1, keepdims=True) + EPS)
    return (rows * inverse * gain, inverse)


def norm_backward(rows, inverse, gain, grad_normed):
    scaled = grad_normed * gain
    grad_rows = inverse * scaled - rows * inverse**3 * jnp.mean(
        scaled * rows, axis=-1, keepdims=True
    )
    return (grad_rows, jnp.sum(grad_normed * rows * inverse, axis=0))


def contract_rows(left, right):
    return lax.dot_general(left, right, (((0,), (0,)), ((), ())), preferred_element_type=WIDE)


def contract_cols(left, right):
    return lax.dot_general(left, right, (((1,), (1,)), ((), ())), preferred_element_type=WIDE)


def split_heads(matrix, heads):
    return matrix.reshape(matrix.shape[0], heads, -1).transpose(1, 0, 2)


def join_heads(stacked):
    return stacked.transpose(1, 0, 2).reshape(stacked.shape[1], -1)


def diagonal_sums(block):
    heads, height, breadth = block.shape
    shifted = jnp.pad(block, ((0, 0), (0, 0), (height, 0))).reshape(
        heads, height * (height + breadth)
    )
    shifted = jnp.pad(shifted, ((0, 0), (0, height))).reshape(heads, height, height + breadth + 1)
    totals = jnp.sum(shifted, axis=1, dtype=WIDE)
    return totals[:, 1 : height + breadth]


def bias_block(offsets, query_start, key_start, queries, keys, seq_len):
    heads = offsets.shape[0]
    begin = key_start - query_start + seq_len - queries
    window = lax.dynamic_slice_in_dim(offsets, begin, queries + keys - 1, 1)
    period = queries + keys
    padded = jnp.pad(window, ((0, 0), (0, 1)))
    spread = jnp.broadcast_to(padded[:, None, :], (heads, queries, period)).reshape(
        heads, queries * period
    )
    skewed = spread[:, : queries * (period - 1)].reshape(heads, queries, period - 1)
    return skewed[:, :, queries - 1 : queries - 1 + keys]


def batch_scores(query_heads, key_heads, bias):
    return (
        SCALE * jnp.einsum("hqd,hkd->hqk", query_heads, key_heads, preferred_element_type=WIDE)
        + bias
    )


def local(
    tokens,
    grad_out,
    routes,
    norm1_gain,
    w_query,
    w_key,
    w_value,
    w_output,
    rel_table,
    rel_bucket,
    norm2_gain,
    router,
    w_in,
    w_out,
):
    tok_rows, width = tokens.shape
    seq_len = tok_rows * lax.axis_size("row")
    heads = H // lax.axis_size("col")
    row_start = lax.axis_index("row") * tok_rows
    tokens_wide = tokens.astype(WIDE)
    gain_one = norm1_gain.astype(WIDE)
    normed, inverse_one = norm_forward(tokens_wide, gain_one)
    normed_low = normed.astype(NARROW)
    query_weight, key_weight, value_weight, output_weight = (
        lax.all_gather(w_query, "row", axis=0, tiled=True),
        lax.all_gather(w_key, "row", axis=0, tiled=True),
        lax.all_gather(w_value, "row", axis=0, tiled=True),
        lax.all_gather(w_output, "row", axis=0, tiled=True),
    )
    query = jnp.dot(normed_low, query_weight, preferred_element_type=WIDE).astype(NARROW)
    key = jnp.dot(normed_low, key_weight, preferred_element_type=WIDE).astype(NARROW)
    value = jnp.dot(normed_low, value_weight, preferred_element_type=WIDE).astype(NARROW)
    keys_all, values_all = (
        lax.all_gather(key, "row", axis=0, tiled=True),
        lax.all_gather(value, "row", axis=0, tiled=True),
    )
    bucket_hot = (rel_bucket[None, :] == jnp.arange(NBUCKET, dtype=jnp.int32)[:, None]).astype(WIDE)
    table_local = lax.dynamic_slice_in_dim(
        rel_table.astype(WIDE), lax.axis_index("col") * heads, heads, 1
    )
    offsets = jnp.dot(table_local.T, bucket_hot, precision=HIGHEST)
    bias = bias_block(offsets, row_start, 0, tok_rows, seq_len, seq_len)
    query_heads = split_heads(query, heads)
    key_heads = split_heads(keys_all, heads)
    value_heads = split_heads(values_all, heads)
    scores = batch_scores(query_heads, key_heads, bias)
    ceiling = jnp.max(scores, axis=2, keepdims=True)
    raised = jnp.exp(scores - ceiling)
    summed = jnp.sum(raised, axis=2, keepdims=True)
    attended_heads = jnp.einsum(
        "hqk,hkd->hqd", (raised / summed).astype(NARROW), value_heads, preferred_element_type=WIDE
    )
    log_total = ceiling[:, :, 0] + jnp.log(summed[:, :, 0])
    attended = join_heads(attended_heads).astype(NARROW)
    branch = lax.psum(contract_cols(attended, output_weight), "col")
    hidden = tokens_wide + branch
    gain_two = norm2_gain.astype(WIDE)
    hn, inverse_two = norm_forward(hidden, gain_two)
    router_wide = router.astype(WIDE)
    gate_probs = jax.nn.softmax(jnp.dot(hn, router_wide, precision=HIGHEST), axis=-1)
    n_exp = router.shape[1]
    capacity = 2 * tok_rows // n_exp
    expert_ids = routes[:, 0]
    one_hot_int = (expert_ids[:, None] == jnp.arange(n_exp, dtype=jnp.int32)[None, :]).astype(
        jnp.int32
    )
    one_hot = one_hot_int.astype(WIDE)
    gate = jnp.sum(gate_probs * one_hot, axis=1)
    rank_own = jnp.sum((jnp.cumsum(one_hot_int, axis=0) - 1) * one_hot_int, axis=1)
    slot_ids = expert_ids * capacity + rank_own
    grad_wide = grad_out.astype(WIDE)
    send_rows = hn.astype(NARROW)
    send_grads = (gate[:, None] * grad_wide).astype(NARROW)
    box_rows = (
        jnp.zeros((n_exp * capacity, width), NARROW)
        .at[slot_ids]
        .set(send_rows)
        .reshape(n_exp, capacity, width)
    )
    box_grads = (
        jnp.zeros((n_exp * capacity, width), NARROW)
        .at[slot_ids]
        .set(send_grads)
        .reshape(n_exp, capacity, width)
    )
    got_rows, got_grads = (
        lax.all_to_all(box_rows, "row", split_axis=0, concat_axis=0, tiled=True),
        lax.all_to_all(box_grads, "row", split_axis=0, concat_axis=0, tiled=True),
    )
    expert_in = got_rows.reshape(-1, width)
    expert_grad = got_grads.reshape(-1, width)
    weight_in = w_in[0]
    weight_out = w_out[0]
    pre = jnp.dot(expert_in, weight_in, preferred_element_type=WIDE)
    act, act_back = jax.vjp(gelu_tanh, pre)
    act_low = act.astype(NARROW)
    out_part = contract_cols(act_low, weight_out)
    grad_act = jnp.dot(expert_grad, weight_out, preferred_element_type=WIDE)
    grad_pre = act_back(grad_act)[0].astype(NARROW)
    rows_part = contract_cols(grad_pre, weight_in)
    grad_weight_in = contract_rows(expert_in, grad_pre)
    grad_weight_out = contract_rows(expert_grad, act_low)
    out_sum, rows_sum = lax.psum((out_part, rows_part), "col")
    back_out, back_rows = (
        lax.all_to_all(
            out_sum.astype(NARROW).reshape(n_exp, capacity, width),
            "row",
            split_axis=0,
            concat_axis=0,
            tiled=True,
        ),
        lax.all_to_all(
            rows_sum.astype(NARROW).reshape(n_exp, capacity, width),
            "row",
            split_axis=0,
            concat_axis=0,
            tiled=True,
        ),
    )
    expert_out = back_out.reshape(-1, width)[slot_ids].astype(WIDE)
    grad_rows = back_rows.reshape(-1, width)[slot_ids].astype(WIDE)
    output = (hidden + gate[:, None] * expert_out).astype(NARROW)
    grad_in_shard, grad_out_shard = (
        lax.psum_scatter(
            grad_weight_in.astype(jnp.bfloat16), "dp", scatter_dimension=0, tiled=True
        ).astype(jnp.float32),
        lax.psum_scatter(
            grad_weight_out.astype(jnp.bfloat16), "dp", scatter_dimension=0, tiled=True
        ).astype(jnp.float32),
    )
    grad_gate = jnp.sum(grad_wide * expert_out, axis=1)
    grad_logits = (grad_gate * gate)[:, None] * (one_hot - gate_probs)
    grad_router = jnp.dot(hn.T, grad_logits, precision=HIGHEST)
    grad_hn = grad_rows + jnp.dot(grad_logits, router_wide.T, precision=HIGHEST)
    grad_hidden_norm, grad_gain_two = norm_backward(hidden, inverse_two, gain_two, grad_hn)
    grad_hidden = grad_wide + grad_hidden_norm
    grad_branch = grad_hidden.astype(NARROW)
    grad_w_output = contract_rows(grad_branch, attended)
    grad_attended = jnp.dot(grad_branch, output_weight, preferred_element_type=WIDE).astype(NARROW)
    grad_heads = split_heads(grad_attended, heads)
    diagonal_start = seq_len - row_start - tok_rows
    shares = jnp.exp(batch_scores(query_heads, key_heads, bias) - log_total[:, :, None])
    grad_shares = jnp.einsum("hqd,hkd->hqk", grad_heads, value_heads, preferred_element_type=WIDE)
    deltas = jnp.sum(shares * grad_shares, axis=2)
    grad_scores = (shares * (grad_shares - deltas[:, :, None])).astype(NARROW)
    grad_query_heads = SCALE * jnp.einsum(
        "hqk,hkd->hqd", grad_scores, key_heads, preferred_element_type=WIDE
    )
    diagonals = diagonal_sums(grad_scores)
    bucket_window = lax.dynamic_slice_in_dim(bucket_hot, diagonal_start, tok_rows + seq_len - 1, 1)
    table_part = jnp.dot(bucket_window, diagonals.T, precision=HIGHEST)
    grad_key_heads = SCALE * jnp.einsum(
        "hqk,hqd->hkd", grad_scores, query_heads, preferred_element_type=WIDE
    )
    grad_value_heads = jnp.einsum(
        "hqk,hqd->hkd", shares.astype(NARROW), grad_heads, preferred_element_type=WIDE
    )
    grad_key, grad_value = (
        lax.psum_scatter(
            join_heads(grad_key_heads).astype(jnp.bfloat16), "row", scatter_dimension=0, tiled=True
        ).astype(jnp.float32),
        lax.psum_scatter(
            join_heads(grad_value_heads).astype(jnp.bfloat16),
            "row",
            scatter_dimension=0,
            tiled=True,
        ).astype(jnp.float32),
    )
    grad_query = join_heads(grad_query_heads).astype(NARROW)
    grad_key_low = grad_key.astype(NARROW)
    grad_value_low = grad_value.astype(NARROW)
    grad_w_query = contract_rows(normed_low, grad_query)
    grad_w_key = contract_rows(normed_low, grad_key_low)
    grad_w_value = contract_rows(normed_low, grad_value_low)
    normed_part = (
        contract_cols(grad_query, query_weight)
        + contract_cols(grad_key_low, key_weight)
        + contract_cols(grad_value_low, value_weight)
    )
    grad_normed = lax.psum(normed_part.astype(jnp.bfloat16), "col").astype(jnp.float32)
    grad_tokens_norm, grad_gain_one = norm_backward(tokens_wide, inverse_one, gain_one, grad_normed)
    grad_tokens = grad_hidden + grad_tokens_norm
    grad_table = lax.psum(table_part, ("dp", "row"))
    (
        grads_query,
        grads_key,
        grads_value,
        grads_output,
        grads_gain_one,
        grads_gain_two,
        grads_router,
    ) = (
        lax.psum_scatter(grad_w_query, ("dp", "row"), scatter_dimension=0, tiled=True),
        lax.psum_scatter(grad_w_key, ("dp", "row"), scatter_dimension=0, tiled=True),
        lax.psum_scatter(grad_w_value, ("dp", "row"), scatter_dimension=0, tiled=True),
        lax.psum_scatter(grad_w_output, ("dp", "row"), scatter_dimension=0, tiled=True),
        lax.psum_scatter(grad_gain_one, ("dp", "row"), scatter_dimension=0, tiled=True),
        lax.psum_scatter(grad_gain_two, ("dp", "row"), scatter_dimension=0, tiled=True),
        lax.psum_scatter(grad_router, ("dp", "row"), scatter_dimension=0, tiled=True),
    )
    return (
        output,
        grad_tokens,
        grads_gain_one,
        grads_query,
        grads_key,
        grads_value,
        grads_output,
        grad_table,
        grads_gain_two,
        grads_router,
        grad_in_shard[None],
        grad_out_shard[None],
    )


VMEM = pltpu.VMEM
SMEM = pltpu.SMEM


def dot_nn(a, b):
    return lax.dot_general(a, b, (((1,), (0,)), ((), ())), preferred_element_type=WIDE)


def dot_nt(a, b):
    return lax.dot_general(a, b, (((1,), (1,)), ((), ())), preferred_element_type=WIDE)


def dot_tn(a, b):
    return lax.dot_general(a, b, (((0,), (0,)), ((), ())), preferred_element_type=WIDE)


def full_spec(shape):
    return pl.BlockSpec(shape, lambda *_: (0,) * len(shape))


def smem_spec():
    return pl.BlockSpec(memory_space=SMEM)


def params(megabytes=28):
    return pltpu.CompilerParams(vmem_limit_bytes=megabytes * 1024 * 1024)


def cost(micros):
    return pl.CostEstimate(flops=int(micros * 575e6), bytes_accessed=0, transcendentals=0)


def shape_of(shape, dtype):
    return jax.ShapeDtypeStruct(shape, dtype)


def pack_kernel(place, w_query, w_key, w_value, own, send):
    row, bit = place[0], place[2] & 1
    wide = own.shape[1] // 3
    part = pl.ds(pl.multiple_of(bit * send.shape[0], 16), send.shape[0])
    for i, w in enumerate((w_query, w_key, w_value)):
        lanes = slice(i * wide, (i + 1) * wide)

        @pl.when(row == 0)
        def _():
            own[:, lanes] = w[:, :wide]
            send[:, lanes] = w[part, wide:]

        @pl.when(row == 1)
        def _():
            own[:, lanes] = w[:, wide:]
            send[:, lanes] = w[part, :wide]


def pack(place, w_query, w_key, w_value):
    rows, cols = w_query.shape
    vmem = pl.BlockSpec(memory_space=VMEM)
    return pl.pallas_call(
        pack_kernel,
        in_specs=[smem_spec()] + [vmem] * 3,
        out_specs=[vmem] * 2,
        out_shape=[shape_of((rows, 3 * cols // 2), NARROW), shape_of((rows // 2, 3 * cols // 2), NARROW)],
        compiler_params=params(60),
        cost_estimate=cost(2),
        name="pack",
    )(place, w_query, w_key, w_value)


def half_kernel(place, value, after, out):
    out[...] = value[...]


def half_of(place, value, after):
    rows, width = value.shape[0] // 2, value.shape[1]
    return pl.pallas_call(
        half_kernel,
        grid_spec=pltpu.PrefetchScalarGridSpec(
            num_scalar_prefetch=1,
            grid=(1,),
            in_specs=[pl.BlockSpec((rows, width), lambda i, place: (place[1], 0)), pl.BlockSpec(memory_space=pl.ANY)],
            out_specs=pl.BlockSpec((rows, width), lambda i, place: (0, 0)),
        ),
        out_shape=shape_of((rows, width), value.dtype),
        compiler_params=params(),
        cost_estimate=cost(1),
        name="half_of",
    )(place, value, after)


def project_kernel(place, tok_own, tok_got, tok_col, gain, w_own, w_got, w_far, tok, normed, q, k, v, w_all):
    half = w_own.shape[0]
    quarter = w_got.shape[0]
    row, col, bit = place[0], place[1], place[2] & 1
    step = pl.program_id(0)

    @pl.when(step == 0)
    def _():
        base = (1 - row) * half
        w_all[pl.ds(pl.multiple_of(row * half, 16), half)] = w_own[...]
        w_all[pl.ds(pl.multiple_of(base + bit * quarter, 16), quarter)] = w_got[...]
        w_all[pl.ds(pl.multiple_of(base + (1 - bit) * quarter, 16), quarter)] = w_far[...]

    @pl.when(step < 2)
    def _():
        tok[...] = tok_own[...]

    @pl.when(step - 2 == col)
    def _():
        tok[...] = tok_got[...]

    @pl.when(step - 2 == 1 - col)
    def _():
        tok[...] = tok_col[...]

    rows = tok[...].astype(WIDE)
    inverse = lax.rsqrt(jnp.mean(rows * rows, axis=-1, keepdims=True) + EPS)
    low = (rows * inverse * gain[...].astype(WIDE)).astype(NARROW)
    normed[...] = low
    out = dot_nn(low, w_all[...])
    heads, _, size = q.shape
    wide = heads * size
    for h in range(heads):
        q[h] = (out[:, h * size : (h + 1) * size] * SCALE).astype(NARROW)
        k[h] = out[:, wide + h * size : wide + (h + 1) * size].astype(NARROW)
        v[h] = out[:, 2 * wide + h * size : 2 * wide + (h + 1) * size].astype(NARROW)


def project(place, toks, gain, w_parts, heads, size):
    block, width = toks[1].shape
    seq = 4 * block
    cols = w_parts[0].shape[1]
    head_spec = pl.BlockSpec((heads, block, size), lambda i: (0, i, 0))
    row_spec = pl.BlockSpec((block, width), lambda i: (i, 0))
    head_shape = shape_of((heads, seq, size), NARROW)
    return pl.pallas_call(
        project_kernel,
        grid=(4,),
        in_specs=[smem_spec(), pl.BlockSpec((block, width), lambda i: (jnp.minimum(i, 1), 0))]
        + [full_spec(x.shape) for x in (*toks[1:], gain, *w_parts)],
        out_specs=[row_spec, row_spec, head_spec, head_spec, head_spec, full_spec((width, cols))],
        out_shape=[shape_of((seq, width), NARROW)] * 2 + [head_shape] * 3 + [shape_of((width, cols), NARROW)],
        compiler_params=params(),
        cost_estimate=cost(3.3),
        name="project",
    )(place, *toks, gain, *w_parts)


TILE = 128
TABLE_LANE = 4


def bias_lanes(row, block_index, blocks):
    half = blocks // 2
    query = lax.rem(block_index + half * row, blocks)
    own = half * row - query + blocks
    other = half * (1 - row) - query + blocks
    return pl.multiple_of(own * TILE, TILE), pl.multiple_of(other * TILE, TILE)


def skew_kernel(bucket, table, after, skew):
    n = bucket.shape[1]
    hot = (bucket[...] == lax.broadcasted_iota(jnp.int32, (NBUCKET, n), 0)).astype(WIDE)
    for h in range(skew.shape[0]):
        line = jnp.sum(hot * table[:, h : h + 1], axis=0, keepdims=True)
        skew[h] = pltpu.roll(jnp.broadcast_to(line, (TILE, n)), 0, 1, stride=1, stride_axis=0)


def skewed_bias(bucket, table, after):
    vmem = pl.BlockSpec(memory_space=VMEM)
    return pl.pallas_call(
        skew_kernel,
        in_specs=[vmem] * 2 + [pl.BlockSpec(memory_space=pl.ANY)],
        out_specs=vmem,
        out_shape=shape_of((table.shape[1], TILE, bucket.shape[1]), WIDE),
        compiler_params=params(),
        cost_estimate=cost(1),
        name="skewed_bias",
    )(bucket, table, after)


def attend_kernel(first, place, skew, q, k, v, att, p):
    heads, block, size = q.shape
    seq = k.shape[1]
    half = seq // 2
    row = place[0]
    step = pl.program_id(0)

    for h in range(heads):
        raw = dot_nt(q[h], k[h])
        parts = []
        for sub in range(block // TILE):
            own, other = bias_lanes(row, first + step * (block // TILE) + sub, seq // TILE)
            bias = jnp.concatenate([skew[h, :, pl.ds(own, half)], skew[h, :, pl.ds(other, half)]], axis=1)
            scores = raw[sub * TILE : (sub + 1) * TILE] + bias
            raised = jnp.exp(scores - jnp.max(scores, axis=1, keepdims=True))
            share = raised * (1.0 / jnp.sum(raised, axis=1, keepdims=True))
            parts.append(share.astype(NARROW))
        shares = jnp.concatenate(parts, axis=0)
        p[h] = shares
        att[:, h * size : (h + 1) * size] = dot_nn(shares, v[h]).astype(NARROW)


def attend(place, skew, q, k, v, block, begin, rows):
    heads, seq, size = q.shape
    start = begin // block
    return pl.pallas_call(
        functools.partial(attend_kernel, begin // TILE),
        grid=(rows // block,),
        in_specs=[
            smem_spec(),
            full_spec(skew.shape),
            pl.BlockSpec((heads, block, size), lambda i: (0, i + start, 0)),
            full_spec(k.shape),
            full_spec(v.shape),
        ],
        out_specs=[
            pl.BlockSpec((block, heads * size), lambda i: (i, 0)),
            pl.BlockSpec((heads, block, seq), lambda i: (0, i, 0)),
        ],
        out_shape=[shape_of((rows, heads * size), NARROW), shape_of((heads, rows, seq), NARROW)],
        compiler_params=params(),
        cost_estimate=cost(9.3),
        name="attend",
    )(place, skew, q, k, v)


def attend_back_kernel(first, last, place, bucket, q, k, v, p, g, *refs):
    if first == 0:
        keep_in = None
    else:
        keep_in, refs = refs[:3], refs[3:]
    if last:
        out, table, key_sum, value_sum, diag = refs
        query_out = None
    else:
        query_out, key_sum, value_sum, diag = refs
        out = None
    heads, block, size = q.shape
    seq = k.shape[1]
    half = seq // 2
    row = place[0]
    step = pl.program_id(0)

    @pl.when(step == 0)
    def _():
        if keep_in is None:
            key_sum[...] = jnp.zeros_like(key_sum)
            value_sum[...] = jnp.zeros_like(value_sum)
            diag[...] = jnp.zeros_like(diag)
        else:
            key_sum[...] = keep_in[0][...]
            value_sum[...] = keep_in[1][...]
            diag[...] = keep_in[2][...]

    wide = heads * size
    for h in range(heads):
        grad = g[:, h * size : (h + 1) * size]
        share_low = p[h]
        share = share_low.astype(WIDE)
        grad_share = dot_nt(grad, v[h])
        delta = jnp.sum(share * grad_share, axis=1, keepdims=True)
        grad_score = share * (grad_share - delta)
        for sub in range(block // TILE):
            own, other = bias_lanes(row, first + step * (block // TILE) + sub, seq // TILE)
            piece = grad_score[sub * TILE : (sub + 1) * TILE]
            diag[h, :, pl.ds(own, half)] += piece[:, :half]
            diag[h, :, pl.ds(other, half)] += piece[:, half:]
        low = grad_score.astype(NARROW)
        grad_query = (SCALE * dot_nn(low, k[h])).astype(NARROW)
        if last:
            out[pl.ds(pl.multiple_of(first * TILE + step * block, block), block), h * size : (h + 1) * size] = grad_query
        else:
            query_out[:, h * size : (h + 1) * size] = grad_query
        key_sum[h] += dot_tn(q[h], low)
        value_sum[h] += dot_tn(grad, share_low)

    if last:
        lanes = diag.shape[2]

        @pl.when(step == pl.num_programs(0) - 1)
        def _():
            hot = (bucket[...] == lax.broadcasted_iota(jnp.int32, (NBUCKET, lanes), 0)).astype(WIDE)
            lane = lax.broadcasted_iota(jnp.int32, table.shape, 1)
            total = jnp.zeros(table.shape, WIDE)
            for h in range(heads):
                lo = h * size
                out[:, wide + lo : wide + lo + size] = key_sum[h].T.astype(NARROW)
                out[:, 2 * wide + lo : 2 * wide + lo + size] = value_sum[h].T.astype(NARROW)
                sums = diag[h]
                height = TILE // 2
                while height >= 8:
                    sums = sums[:height] + pltpu.roll(sums[height:], lanes - height, 1)
                    height //= 2
                where = lax.broadcasted_iota(jnp.int32, sums.shape, 0)
                for bit in (4, 2, 1):
                    sums = jnp.where((where & bit) != 0, pltpu.roll(sums, lanes - bit, 1), sums)
                line = jnp.sum(sums, axis=0, keepdims=True)
                total = total + jnp.where(lane == TABLE_LANE + h, jnp.sum(hot * line, axis=1, keepdims=True), 0.0)
            table[...] = total


def attend_back(place, bucket, q, k, v, p, g, block, begin, keep, after=None):
    heads, seq, size = q.shape
    rows = g.shape[0]
    start = begin // block
    last = keep is not None
    lanes = bucket.shape[1]
    sum_shape = (heads, size, seq)
    diag_shape = (heads, TILE, lanes)
    wide = heads * size
    in_specs = [
        smem_spec(),
        full_spec(bucket.shape),
        pl.BlockSpec((heads, block, size), lambda i: (0, i + start, 0)),
        full_spec(k.shape),
        full_spec(v.shape),
        pl.BlockSpec((heads, block, seq), lambda i: (0, i + start, 0)),
        pl.BlockSpec((block, wide), lambda i: (i, 0)),
    ]
    args = [place, bucket, q, k, v, p, g]
    sums = [shape_of(sum_shape, WIDE), shape_of(sum_shape, WIDE), shape_of(diag_shape, WIDE)]
    if last:
        in_specs += [full_spec(s.shape) for s in sums]
        args += list(keep[1:])
        in_specs += [full_spec(keep[0].shape)]
        args += [keep[0], after]
        in_specs += [pl.BlockSpec(memory_space=pl.ANY)]
        out_specs = [full_spec((seq, 3 * wide)), full_spec((NBUCKET, 128))]
        out_shape = [shape_of((seq, 3 * wide), NARROW), shape_of((NBUCKET, 128), WIDE)]
        scratch = [VMEM(s.shape, WIDE) for s in sums]

        def kernel(*refs):
            earlier = refs[10]
            out = refs[12]

            @pl.when(pl.program_id(0) == 0)
            def _():
                out[: earlier.shape[0], :wide] = earlier[...]

            attend_back_kernel(begin // TILE, True, *refs[:10], *refs[12:])

    else:
        out_specs = [pl.BlockSpec((block, wide), lambda i: (i, 0))] + [full_spec(s.shape) for s in sums]
        out_shape = [shape_of((rows, wide), NARROW)] + sums
        scratch = []
        kernel = functools.partial(attend_back_kernel, begin // TILE, False)
    return pl.pallas_call(
        kernel,
        grid=(rows // block,),
        in_specs=in_specs,
        out_specs=out_specs,
        out_shape=out_shape,
        scratch_shapes=scratch,
        compiler_params=params(),
        cost_estimate=cost(6.5),
        name="attend_back",
    )(*args)


def column(lines):
    count = lines.shape[0]
    wide = jnp.concatenate([lines, jnp.zeros((128 - count, 128), lines.dtype)], axis=0).T
    return jnp.concatenate([wide[:, i : i + 1] for i in range(count)], axis=0)


def gate_values(hn, route, router):
    count = router.shape[0]
    logits = [jnp.sum(hn * router[e : e + 1], axis=1, keepdims=True) for e in range(count)]
    top = functools.reduce(jnp.maximum, logits)
    raised = [jnp.exp(x - top) for x in logits]
    total = functools.reduce(jnp.add, raised)
    probs = [x / total for x in raised]
    hots = [(route == float(e)).astype(WIDE) for e in range(count)]
    gate = functools.reduce(jnp.add, [p * o for p, o in zip(probs, hots)])
    return probs, hots, gate


def hidden_kernel(place, a_mine, a_row, a_col, a_diag, w_mine, w_other, tok, gain, router, kinds, hidden, att, rows, scale, pack, route):
    row = place[0]
    step = pl.program_id(0)
    size = a_mine.shape[1]

    @pl.when(step == 0)
    def _():
        route[...] = column(kinds[...])

    @pl.when(row == 0)
    def _():
        pack[0, :, :size] = a_mine[...]
        pack[0, :, size:] = a_row[...]
        pack[1, :, :size] = a_col[...]
        pack[1, :, size:] = a_diag[...]

    @pl.when(row == 1)
    def _():
        pack[0, :, size:] = a_mine[...]
        pack[0, :, :size] = a_row[...]
        pack[1, :, size:] = a_col[...]
        pack[1, :, :size] = a_diag[...]

    branch = dot_nt(pack[0], w_mine[...]) + dot_nt(pack[1], w_other[...])
    wide = tok[...].astype(WIDE) + branch

    @pl.when(step < 2)
    def _():
        hidden[...] = wide
        att[...] = pack[0]

    inverse = lax.rsqrt(jnp.mean(wide * wide, axis=-1, keepdims=True) + EPS)
    hn = wide * inverse * gain[...].astype(WIDE)
    block = wide.shape[0]
    kind = route[pl.ds(pl.multiple_of(step * block, 16), block), :]
    _, hots, gate = gate_values(hn, kind, router)
    chosen = jnp.where(kind == row.astype(WIDE), 1.0, 0.0)
    rows[...] = (hn * chosen).astype(NARROW)
    scale[...] = gate * chosen


def hidden_rows(place, pieces, w_mine, w_other, tok_all, gain, router, route_all):
    seq, width = tok_all.shape
    block = seq // 4
    size = pieces[0].shape[1]
    half = w_mine.shape[1]
    turned = pl.BlockSpec((block, size), lambda i: (lax.rem(i + 2, 4), 0))
    plain = pl.BlockSpec((block, size), lambda i: (i, 0))
    wide_spec = pl.BlockSpec((block, width), lambda i: (i, 0))
    own_spec = pl.BlockSpec((block, width), lambda i: (jnp.minimum(i, 1), 0))
    mixed = pl.BlockSpec((block, width), lambda i: (lax.rem(i, 2) * 2 + lax.div(i, 2), 0))
    mixed_line = pl.BlockSpec((block, 1), lambda i: (lax.rem(i, 2) * 2 + lax.div(i, 2), 0))
    return pl.pallas_call(
        hidden_kernel,
        grid=(4,),
        in_specs=[
            smem_spec(),
            plain,
            turned,
            plain,
            turned,
            full_spec(w_mine.shape),
            full_spec(w_other.shape),
            wide_spec,
            full_spec(gain.shape),
            full_spec(router.shape),
            full_spec(route_all.shape),
        ],
        out_specs=[own_spec, pl.BlockSpec((block, half), lambda i: (jnp.minimum(i, 1), 0)), mixed, mixed_line],
        out_shape=[
            shape_of((seq // 2, width), WIDE),
            shape_of((seq // 2, half), NARROW),
            shape_of((seq, width), NARROW),
            shape_of((seq, 1), WIDE),
        ],
        scratch_shapes=[VMEM((2, block, half), NARROW), VMEM((seq, 1), WIDE)],
        compiler_params=params(),
        cost_estimate=cost(6),
        name="hidden_rows",
    )(place, *pieces, w_mine, w_other, tok_all, gain, router, route_all)


def scale_kernel(place, own, got, got_col, scale, out):
    col = place[1]
    block = got.shape[0]
    for half in range(2):
        first = pl.ds(2 * half * block, block)
        second = pl.ds((2 * half + 1) * block, block)
        out[first, :] = (own[half * block : (half + 1) * block, :].astype(WIDE) * scale[first, :]).astype(NARROW)
        other = jnp.where(col == half, got[...].astype(WIDE), got_col[...].astype(WIDE))
        out[second, :] = (other * scale[second, :]).astype(NARROW)


def scale_grads(place, own, got, got_col, scale):
    args = (place, own, got, got_col, scale)
    vmem = pl.BlockSpec(memory_space=VMEM)
    return pl.pallas_call(
        scale_kernel,
        in_specs=[smem_spec()] + [vmem] * 4,
        out_specs=vmem,
        out_shape=shape_of((2 * own.shape[0], own.shape[1]), NARROW),
        compiler_params=params(),
        cost_estimate=cost(1.4),
        name="scale_grads",
    )(*args)


def store_quarters(mine, value, keeps, sends):
    rows = keeps[0].shape[0]
    for part in range(2):
        low = slice(part * rows, (part + 1) * rows)
        high = slice((2 + part) * rows, (3 + part) * rows)

        @pl.when(mine == 0)
        def _():
            keeps[part][...] = value[low].astype(NARROW)
            sends[part][...] = value[high].astype(NARROW)

        @pl.when(mine == 1)
        def _():
            keeps[part][...] = value[high].astype(NARROW)
            sends[part][...] = value[low].astype(NARROW)


def expert_out_kernel(place, x, w_in, w_out, act, slope, keep_own, keep_other, send_own, send_other, total):
    step = pl.program_id(0)
    pre = dot_nn(x[...], w_in[...])
    square = pre * pre
    bent = jnp.tanh(pre * (0.7978845608028654 + (0.7978845608028654 * 0.044715) * square))
    half = 0.5 + 0.5 * bent
    act_low = (pre * half).astype(NARROW)
    act[...] = act_low
    inner = 0.7978845608028654 + (0.7978845608028654 * 0.134145) * square
    slope[...] = (half + (0.5 * pre) * ((1.0 - bent * bent) * inner)).astype(NARROW)
    piece = dot_nt(act_low, w_out[...])

    @pl.when(step == 0)
    def _():
        total[...] = piece

    @pl.when(step > 0)
    def _():
        total[...] += piece

    @pl.when(step == pl.num_programs(0) - 1)
    def _():
        store_quarters(place[1], total, (keep_own, keep_other), (send_own, send_other))


def expert_back_kernel(place, g, slope, w_in, w_out, after, later, grad_pre, keep_own, keep_other, send_own, send_other, total):
    step = pl.program_id(0)
    low = (dot_nn(g[...], w_out[...]) * slope[...].astype(WIDE)).astype(NARROW)
    grad_pre[...] = low
    piece = dot_nt(low, w_in[...])

    @pl.when(step == 0)
    def _():
        total[...] = piece

    @pl.when(step > 0)
    def _():
        total[...] += piece

    @pl.when(step == pl.num_programs(0) - 1)
    def _():
        store_quarters(place[1], total, (keep_own, keep_other), (send_own, send_other))


def expert_forward(place, x, w_in, w_out, block):
    seq, width = x.shape
    units = w_in.shape[1]
    w_spec = pl.BlockSpec((width, block), lambda i: (0, i))
    unit_spec = pl.BlockSpec((seq, block), lambda i: (0, i))
    quarter = (seq // 4, width)
    return pl.pallas_call(
        expert_out_kernel,
        grid=(units // block,),
        in_specs=[smem_spec(), full_spec(x.shape), w_spec, w_spec],
        out_specs=[unit_spec, unit_spec] + [full_spec(quarter)] * 4,
        out_shape=[shape_of((seq, units), NARROW)] * 2 + [shape_of(quarter, NARROW)] * 4,
        scratch_shapes=[VMEM(x.shape, WIDE)],
        compiler_params=params(),
        cost_estimate=cost(9.4),
        name="expert_forward",
    )(place, x, w_in, w_out)


def expert_backward(place, g, slope, w_in, w_out, block, after, later):
    seq, width = g.shape
    units = w_in.shape[1]
    w_spec = pl.BlockSpec((width, block), lambda i: (0, i))
    unit_spec = pl.BlockSpec((seq, block), lambda i: (0, i))
    quarter = (seq // 4, width)
    return pl.pallas_call(
        expert_back_kernel,
        grid=(units // block,),
        in_specs=[smem_spec(), full_spec(g.shape), unit_spec, w_spec, w_spec] + [pl.BlockSpec(memory_space=pl.ANY)] * 2,
        out_specs=[unit_spec] + [full_spec(quarter)] * 4,
        out_shape=[shape_of((seq, units), NARROW)] + [shape_of(quarter, NARROW)] * 4,
        scratch_shapes=[VMEM(g.shape, WIDE)],
        compiler_params=params(),
        cost_estimate=cost(8),
        name="expert_backward",
    )(place, g, slope, w_in, w_out, after, later)


def store_chunks(place, bit, value, keep, send, lanes=slice(None)):
    rows = keep.shape[1]
    mine = (place[2] >> bit) & 1
    low = (1 << bit) - 1
    for j in range(2 * keep.shape[0]):
        at = ((j >> (bit + 1)) << bit) | (j & low)
        chunk = value[j * rows : (j + 1) * rows].astype(NARROW)

        @pl.when(mine == (j >> bit) & 1)
        def _():
            keep[at, :, lanes] = chunk

        @pl.when(mine != (j >> bit) & 1)
        def _():
            send[at, :, lanes] = chunk


def weight_grad_kernel(pieces, block, place, left, right, after, *refs):
    turned = refs[-1]
    turned[...] = left[...].T
    lanes = right.shape[1] // pieces
    for piece in range(pieces):
        for at in range(0, lanes, block):
            value = dot_nn(turned[...], right[:, piece * lanes + at : piece * lanes + at + block])
            store_chunks(place, 0, value, refs[2 * piece], refs[2 * piece + 1], slice(at, at + block))


def weight_grad(place, left, right, pieces, block, count, after):
    seq, width = left.shape
    units = right.shape[1]
    shape = shape_of((count // 2, width // count, units // pieces), NARROW)
    outs = [shape] * (2 * pieces)
    return pl.pallas_call(
        functools.partial(weight_grad_kernel, pieces, block),
        grid=(1,),
        in_specs=[smem_spec(), full_spec(left.shape), full_spec(right.shape), pl.BlockSpec(memory_space=pl.ANY)],
        out_specs=[full_spec(x.shape) for x in outs],
        out_shape=outs,
        scratch_shapes=[VMEM((width, seq), NARROW)],
        compiler_params=params(),
        cost_estimate=cost(5),
        name="weight_grad",
    )(place, left, right, after)


def combine_kernel(
    place, hidden, outs, out_far, out_row, out_row_far, backs, back_far, back_row, back_row_far, grad, kinds, gain, router, w_mine, att, after,
    output, grad_hidden, sums, back_own, back_send, w_keep, w_send, w_sum, route,
):
    row, col = place[0], place[1]
    step = pl.program_id(0)
    block = hidden.shape[0]
    count = router.shape[0]
    size = back_own.shape[1]

    @pl.when(step == 0)
    def _():
        route[...] = column(kinds[...])
        sums[...] = jnp.zeros_like(sums)

    gain_wide = gain[...].astype(WIDE)
    mine = col == step

    def chosen(own, own_row, far, far_row):
        return jnp.where(mine, own[...].astype(WIDE) + own_row[...].astype(WIDE), far[...].astype(WIDE) + far_row[...].astype(WIDE))

    expert_out = chosen(outs, out_row, out_far, out_row_far)
    grad_rows = chosen(backs, back_row, back_far, back_row_far)
    wide = hidden[...]
    grad_wide = grad[...].astype(WIDE)
    inverse = lax.rsqrt(jnp.mean(wide * wide, axis=-1, keepdims=True) + EPS)
    scaled = wide * inverse
    hn = scaled * gain_wide
    probs, hots, gate = gate_values(hn, route[pl.ds(pl.multiple_of(step * block, 16), block), :], router)
    output[...] = (wide + gate * expert_out).astype(NARROW)
    grad_gate = jnp.sum(grad_wide * expert_out, axis=1, keepdims=True) * gate
    grad_hn = grad_rows
    line = lax.broadcasted_iota(jnp.int32, sums.shape, 0)
    packed = jnp.zeros(sums.shape, WIDE)
    for e in range(count):
        grad_logit = grad_gate * (hots[e] - probs[e])
        grad_hn = grad_hn + grad_logit * router[e : e + 1]
        packed = packed + jnp.where(line == 1 + e, jnp.sum(hn * grad_logit, axis=0, keepdims=True), 0.0)
    sums[...] += packed + jnp.where(line == 0, jnp.sum(grad_hn * scaled, axis=0, keepdims=True), 0.0)
    u = grad_hn * gain_wide
    back = grad_wide + inverse * u - wide * (inverse * inverse * inverse) * jnp.mean(u * wide, axis=-1, keepdims=True)
    grad_hidden[...] = back
    low = back.astype(NARROW)
    grad_att = dot_nn(low, w_mine[...]).astype(NARROW)

    @pl.when(row == 0)
    def _():
        back_own[...] = grad_att[:, :size]
        back_send[...] = grad_att[:, size:]

    @pl.when(row == 1)
    def _():
        back_own[...] = grad_att[:, size:]
        back_send[...] = grad_att[:, :size]

    piece = dot_tn(low, att[...])

    @pl.when(step == 0)
    def _():
        w_sum[...] = piece

    @pl.when(step == 1)
    def _():
        store_chunks(place, 0, w_sum[...] + piece, w_keep, w_send)


def combine(place, hidden, outs, backs, grad, kinds, gain, router, w_mine, att, size, count, after):
    tokens, width = hidden.shape
    half = w_mine.shape[1]
    block = tokens // 2
    rows = pl.BlockSpec((block, width), lambda i: (i, 0))
    narrow = pl.BlockSpec((block, size), lambda i: (i, 0))
    chunks = (count // 2, width // count, half)
    return pl.pallas_call(
        combine_kernel,
        grid=(2,),
        in_specs=[smem_spec(), rows]
        + [full_spec((block, width))] * 8
        + [rows]
        + [full_spec(x.shape) for x in (kinds, gain, router, w_mine)]
        + [pl.BlockSpec((block, half), lambda i: (i, 0)), pl.BlockSpec(memory_space=pl.ANY)],
        out_specs=[rows, rows, full_spec((8, width)), narrow, narrow, full_spec(chunks), full_spec(chunks)],
        out_shape=[
            shape_of((tokens, width), NARROW),
            shape_of((tokens, width), WIDE),
            shape_of((8, width), WIDE),
            shape_of((tokens, size), NARROW),
            shape_of((tokens, size), NARROW),
            shape_of(chunks, NARROW),
            shape_of(chunks, NARROW),
        ],
        scratch_shapes=[VMEM((width, half), WIDE), VMEM((tokens, 1), WIDE)],
        compiler_params=params(),
        cost_estimate=cost(6.5),
        name="combine",
    )(place, hidden, *outs, *backs, grad, kinds, gain, router, w_mine, att, after)


def project_back_kernel(place, g, w_all, after, keep_own, keep_other, send_own, send_other, back_all):
    block = g.shape[0] // 4
    back = dot_nt(g[...], w_all[...]).astype(NARROW)
    for i in range(4):
        at = (i % 2) * 2 * block + (i // 2) * block
        back_all[at : at + block] = back[i * block : (i + 1) * block]
    store_quarters(place[1], back_all, (keep_own, keep_other), (send_own, send_other))


def project_back(place, g, w_all, after):
    seq, cols = g.shape
    width = w_all.shape[0]
    vmem = pl.BlockSpec(memory_space=VMEM)
    quarter = shape_of((seq // 4, width), NARROW)
    return pl.pallas_call(
        project_back_kernel,
        in_specs=[smem_spec()] + [vmem] * 2 + [pl.BlockSpec(memory_space=pl.ANY)],
        out_specs=[vmem] * 4,
        out_shape=[quarter] * 4,
        scratch_shapes=[VMEM((seq, width), NARROW)],
        compiler_params=params(),
        cost_estimate=cost(2),
        name="project_back",
    )(place, g, w_all, after)


def project_grad_kernel(place, g, normed, w_all, gain, sums, table, after, keep, send):
    width = normed.shape[1]
    wide = g.shape[1] // 3
    per_row = width // (4 * keep.shape[0])
    grads = dot_tn(normed[...], g[...])
    store_chunks(place, 0, grads[:, : 2 * wide], keep, send, slice(0, 2 * wide))
    gain_grad = jnp.sum(grads * w_all[...].astype(WIDE), axis=1, keepdims=True)
    line = lax.broadcasted_iota(jnp.int32, (128, width), 0)
    lines = jnp.where(line == 0, 1.0 / gain[...].astype(WIDE), 0.0)
    for e in range(TABLE_LANE - 1):
        lines = lines + jnp.where(line == 1 + e, sums[e : e + 1], 0.0)
    lane = lax.broadcasted_iota(jnp.int32, (width, 128), 1)
    turned = lines.T
    turned = turned * jnp.where(lane == 0, gain_grad, 1.0)
    gap = jnp.zeros((per_row - NBUCKET, 128), WIDE)
    tables = jnp.concatenate([table[...], gap] * (width // per_row), axis=0)
    store_chunks(place, 0, turned + tables, keep, send, slice(2 * wide, 2 * wide + 128))
    store_chunks(place, 0, grads[:, 2 * wide :], keep, send, slice(2 * wide + 128, 3 * wide + 128))


def project_grad(place, g, normed, w_all, gain, sums, table, count, after):
    seq, width = normed.shape
    wide = g.shape[1] // 3
    args = (place, g, normed, w_all, gain, sums, table, after)
    chunks = (count // 2, width // count)
    vmem = pl.BlockSpec(memory_space=VMEM)
    shape = shape_of((*chunks, 3 * wide + 128), NARROW)
    return pl.pallas_call(
        project_grad_kernel,
        in_specs=[smem_spec()] + [vmem] * 6 + [pl.BlockSpec(memory_space=pl.ANY)],
        out_specs=[vmem] * 2,
        out_shape=[shape] * 2,
        compiler_params=params(),
        cost_estimate=cost(2.7),
        name="project_grad",
    )(*args)


def finish_kernel(place, tok, gain, grad_hidden, mine, far, row, row_far, out):
    col = place[1]
    block = mine.shape[0]
    gain_wide = gain[...].astype(WIDE)
    for half in range(2):
        part = pl.ds(half * block, block)
        grad_normed = jnp.where(col == half, mine[...].astype(WIDE) + row[...].astype(WIDE), far[...].astype(WIDE) + row_far[...].astype(WIDE))
        rows = tok[part, :].astype(WIDE)
        inverse = lax.rsqrt(jnp.mean(rows * rows, axis=-1, keepdims=True) + EPS)
        u = grad_normed * gain_wide
        out[part, :] = grad_hidden[part, :] + inverse * u - rows * (inverse * inverse * inverse) * jnp.mean(u * rows, axis=-1, keepdims=True)


def finish(place, tok, gain, grad_hidden, *sums):
    args = (place, tok, gain, grad_hidden, *sums)
    return pl.pallas_call(
        finish_kernel,
        in_specs=[smem_spec()] + [pl.BlockSpec(memory_space=VMEM)] * (len(args) - 1),
        out_specs=pl.BlockSpec(memory_space=VMEM),
        out_shape=shape_of(tok.shape, WIDE),
        compiler_params=params(),
        cost_estimate=cost(2.5),
        name="finish",
    )(*args)


def assemble_kernel(place, part, got, grad_q, grad_k, grad_v, grad_o, grad_router, grad_table, lines):
    row = place[0]
    wide = grad_q.shape[1] // 2
    rows = got.shape[0]
    mine = part[...].astype(WIDE)
    theirs = got[...].astype(WIDE)
    extra = 2 * wide
    late = extra + 128
    last = late + wide
    heads = grad_table.shape[1] // 2
    grad_o[...] = mine[:, last:] + theirs[:, last:]
    small = mine[:, extra:late] + theirs[:, extra:late]
    grad_router[...] = small[:, 2:4]
    lines[...] = jnp.concatenate([small, jnp.zeros((128 - rows, 128), WIDE)], axis=0).T[: lines.shape[0], :]
    at = extra + TABLE_LANE

    @pl.when(row == 0)
    def _():
        for out, lo in ((grad_q, 0), (grad_k, wide), (grad_v, late)):
            out[...] = jnp.concatenate([mine[:, lo : lo + wide], theirs[:, lo : lo + wide]], axis=1)
        grad_table[...] = jnp.concatenate([mine[:NBUCKET, at : at + heads], theirs[:NBUCKET, at : at + heads]], axis=1)

    @pl.when(row == 1)
    def _():
        for out, lo in ((grad_q, 0), (grad_k, wide), (grad_v, late)):
            out[...] = jnp.concatenate([theirs[:, lo : lo + wide], mine[:, lo : lo + wide]], axis=1)
        grad_table[...] = jnp.concatenate([theirs[:NBUCKET, at : at + heads], mine[:NBUCKET, at : at + heads]], axis=1)


def assemble(place, part, got, wide, heads, count):
    rows = got.shape[0]
    vmem = pl.BlockSpec(memory_space=VMEM)
    return pl.pallas_call(
        assemble_kernel,
        in_specs=[smem_spec()] + [vmem] * 2,
        out_specs=[vmem] * 7,
        out_shape=[shape_of((rows, 2 * wide), WIDE)] * 4
        + [shape_of((rows, count), WIDE), shape_of((NBUCKET, 2 * heads), WIDE), shape_of((8, 128), WIDE)],
        compiler_params=params(),
        cost_estimate=cost(1.4),
        name="assemble",
    )(place, part, got)


def swap(value, axis, flip=1):
    size = lax.axis_size(axis)
    return lax.ppermute(value, axis, [(i, i ^ flip) for i in range(size)])


def pick(value, index, axis=0):
    return lax.dynamic_index_in_dim(value, index, axis, keepdims=False)


def in_order(first, mine, got, axis=0):
    return jnp.where(first, jnp.concatenate([mine, got], axis), jnp.concatenate([got, mine], axis))


def later(value, *others):
    return lax.optimization_barrier((value, *others))[0]


def halve_kernel(bit, place, kept, got, after, keep, send):
    mine = (place[2] >> bit) & 1
    low = (1 << bit) - 1
    for j in range(kept.shape[0]):
        at = ((j >> (bit + 1)) << bit) | (j & low)
        chunk = (kept[j].astype(WIDE) + got[j].astype(WIDE)).astype(NARROW)

        @pl.when(mine == (j >> bit) & 1)
        def _():
            keep[at] = chunk

        @pl.when(mine != (j >> bit) & 1)
        def _():
            send[at] = chunk


def halve(place, kept, got, bit, at, after):
    n, rows, lanes = kept.shape
    shape = shape_of((n // 2, rows, lanes), NARROW)
    vmem = pl.BlockSpec(memory_space=VMEM)

    def kernel(place, *refs):
        shifted = [None, None, place[2] >> (at - bit) if at > bit else place[2]]
        halve_kernel(bit, shifted, *refs)

    return pl.pallas_call(
        kernel,
        in_specs=[smem_spec()] + [vmem] * 2 + [pl.BlockSpec(memory_space=pl.ANY)],
        out_specs=[vmem] * 2,
        out_shape=[shape] * 2,
        compiler_params=params(),
        cost_estimate=cost(1),
        name="halve",
    )(place, kept, got, after)


def add_kernel(kept, got, after, out):
    out[...] = kept[0].astype(WIDE) + got[0].astype(WIDE)


def add_wide(kept, got, after):
    vmem = pl.BlockSpec(memory_space=VMEM)
    return pl.pallas_call(
        add_kernel,
        in_specs=[vmem] * 2 + [pl.BlockSpec(memory_space=pl.ANY)],
        out_specs=vmem,
        out_shape=shape_of(kept.shape[1:], WIDE),
        compiler_params=params(),
        cost_estimate=cost(1),
        name="add_wide",
    )(kept, got, after)


def add_pieces_kernel(kept, got, kept_next, got_next, after, out, beside):
    lanes = kept.shape[2]
    out[:, :lanes] = kept[0].astype(WIDE) + got[0].astype(WIDE)
    rest = kept_next[0].astype(WIDE) + got_next[0].astype(WIDE)
    out[:, lanes:] = rest[:, :lanes]
    beside[...] = rest[:, lanes:].astype(NARROW)


def add_pieces(kept, got, kept_next, got_next, after):
    vmem = pl.BlockSpec(memory_space=VMEM)
    _, rows, lanes = kept.shape
    return pl.pallas_call(
        add_pieces_kernel,
        in_specs=[vmem] * 4 + [pl.BlockSpec(memory_space=pl.ANY)],
        out_specs=[vmem] * 2,
        out_shape=[shape_of((rows, 2 * lanes), WIDE), shape_of((rows, kept_next.shape[2] - lanes), NARROW)],
        compiler_params=params(),
        cost_estimate=cost(1.5),
        name="add_pieces",
    )(kept, got, kept_next, got_next, after)


def part_kernel(place, kept, got, beside, after, mine, send):
    rows = mine.shape[0]
    values = (
        (kept[0].astype(WIDE) + got[0].astype(WIDE)).astype(NARROW),
        beside[...],
    )
    at = 0
    for value in values:
        lanes = slice(at, at + value.shape[1])
        at += value.shape[1]

        @pl.when(place[0] == 0)
        def _():
            mine[:, lanes] = value[:rows]
            send[:, lanes] = value[rows:]

        @pl.when(place[0] == 1)
        def _():
            mine[:, lanes] = value[rows:]
            send[:, lanes] = value[:rows]


def parts_by_row(place, kept, got, beside, after):
    vmem = pl.BlockSpec(memory_space=VMEM)
    shape = shape_of((kept.shape[1] // 2, kept.shape[2] + beside.shape[1]), NARROW)
    return pl.pallas_call(
        part_kernel,
        in_specs=[smem_spec()] + [vmem] * 3 + [pl.BlockSpec(memory_space=pl.ANY)],
        out_specs=[vmem] * 2,
        out_shape=[shape, shape],
        compiler_params=params(),
        cost_estimate=cost(1),
        name="parts_by_row",
    )(place, kept, got, beside, after)


def add_low_kernel(keep, got, after, out):
    out[...] = (keep[...].astype(WIDE) + got[...].astype(WIDE)).astype(NARROW)


def add_low(keep, got, after):
    vmem = pl.BlockSpec(memory_space=VMEM)
    return pl.pallas_call(
        add_low_kernel,
        in_specs=[vmem] * 2 + [pl.BlockSpec(memory_space=pl.ANY)],
        out_specs=vmem,
        out_shape=shape_of(keep.shape, NARROW),
        compiler_params=params(),
        cost_estimate=cost(0.6),
        name="add_low",
    )(keep, got, after)


def along(send, bit):
    return swap(send, "dp", 1 << bit)


def local_pair(tokens, grad_out, routes, norm1_gain, w_query, w_key, w_value, w_output, rel_table, rel_bucket, norm2_gain, router, w_in, w_out):
    tok_rows, width = tokens.shape
    seq = 2 * tok_rows
    row, col = lax.axis_index("row"), lax.axis_index("col")
    count = lax.axis_size("dp")
    bits = count.bit_length() - 1
    place = jnp.stack([row, col, lax.axis_index("dp")]).astype(jnp.int32)
    col_heads = H // lax.axis_size("col")
    heads = col_heads // 2
    size = w_query.shape[1] // col_heads
    wide = heads * size

    w_own, w_send = pack(place, w_query, w_key, w_value)
    w_got = swap(w_send, "row")
    table = lax.dynamic_slice_in_dim(rel_table.astype(WIDE), col * col_heads + row * heads, heads, 1)
    bucket = jnp.pad(rel_bucket[None, :], ((0, 0), (1, 0)), constant_values=-1)
    skew = skewed_bias(bucket, table, w_send)
    tok_got = swap(half_of(place, tokens, w_send), "row")
    w_far = swap(w_got, "dp", 1)
    tok_got = later(tok_got, w_far, skew)
    tok_col = swap(tok_got, "col")
    gain_one, gain_two = norm1_gain[None, :], norm2_gain[None, :]
    router_lines = router.astype(WIDE).T

    tok_all, normed, q, k, v, w_all = project(place, (tokens, tok_got, tok_col), gain_one, (w_own, w_got, w_far), heads, size)

    kinds = routes.astype(WIDE).reshape(-1, 128)
    w_output_late, kinds, _ = lax.optimization_barrier((w_output, kinds, w_all))
    kinds_got = swap(kinds, "row")
    wo_got = swap(w_output_late, "row")

    att, shares = attend(place, skew, q, k, v, 256, 0, seq)
    grad_half = half_of(place, grad_out, att)
    kinds_got, wo_got, _ = lax.optimization_barrier((kinds_got, wo_got, grad_half))
    kinds_all = jnp.concatenate([kinds, kinds_got], 0)
    w_mine = in_order(row == 0, w_output, wo_got)
    w_other = swap(w_mine, "col")
    att_row = swap(att, "row")
    att_col = swap(att, "col")
    att_row = later(att_row, w_mine, grad_half, kinds_all, gain_two, router_lines)
    pieces = (att, att_row, att_col, swap(att_row, "col"))
    grad_got = swap(grad_half, "row")
    hidden, att_own, rows, scale = hidden_rows(place, pieces, w_mine, w_other, tok_all, gain_two, router_lines, kinds_all)

    weight_in, weight_out = w_in[0], w_out[0]
    grad_got = later(grad_got, rows)
    grad_col = swap(grad_got, "col")
    act, slope, out_own, out_other, out_own_send, out_other_send = expert_forward(place, rows, weight_in, weight_out, 512)
    out_other_col = swap(later(out_other_send, grad_col), "col")
    grads = scale_grads(place, grad_out, grad_got, grad_col, scale)
    keep_o, send_o = weight_grad(place, grads, act, 1, 768, count, grads)
    got_o = along(send_o, 0)
    out_other = add_low(out_other, out_other_col, keep_o)
    out_row = swap(out_other, "row")
    out_own_col = swap(out_own_send, "col")
    grad_pre, rows_own, rows_other, rows_own_send, rows_other_send = expert_backward(
        place, grads, slope, weight_in, weight_out, 512, out_other, keep_o
    )
    out_row = later(out_row, rows_own)
    rows_other = add_low(rows_other, swap(later(rows_other_send, out_row), "col"), rows_own)
    rows_row = swap(rows_other, "row")
    rows_own_col = swap(rows_own_send, "col")
    out_mine = add_low(out_own, out_own_col, rows_other)
    outs = (out_mine, swap(out_mine, "col"), out_row, swap(out_row, "col"))
    keep_i, send_i, keep_j, send_j = weight_grad(place, rows, grad_pre, 2, 768, count, rows_other)
    got_i = along(send_i, 0)
    rows_mine = add_low(rows_own, rows_own_col, keep_i)
    rows_row = later(rows_row, keep_i)
    backs = (rows_mine, swap(rows_mine, "col"), rows_row, swap(rows_row, "col"))
    keep_o, send_o = halve(place, keep_o, got_o, 0, 1, rows_row)
    got_o = along(send_o, 1)

    output, grad_hidden, sums, back_own, back_send, wo_keep, wo_send = combine(
        place, hidden, outs, backs, grad_out, kinds, gain_two, router_lines, w_mine, att_own, wide, count, keep_o
    )
    back_oth = swap(back_send, "row")
    keep_j, send_j = jnp.concatenate([keep_j, wo_keep], 2), jnp.concatenate([send_j, wo_send], 2)
    got_j = along(send_j, 0)
    keep_i, send_i = halve(place, keep_i, got_i, 0, 1, send_j)
    got_i = along(send_i, 1)
    keep = attend_back(place, bucket, q, k, v, shares, later(back_own, keep_i), 256, 0, None)
    keep_o, send_o = halve(place, keep_o, got_o, 0, 2, keep[0])
    got_o = along(send_o, 2)
    keep_i, send_i = halve(place, keep_i, got_i, 0, 2, keep_o)
    got_i = along(send_i, 2)
    g, table_part = attend_back(place, bucket, q, k, v, shares, back_oth, 256, tok_rows, keep, keep_i)
    keep_j, send_j = halve(place, keep_j, got_j, 0, 1, g)
    got_j = along(send_j, 1)

    normed_own, normed_other, normed_own_send, normed_other_send = project_back(place, g, w_all, keep_j)
    normed_other_col = swap(normed_other_send, "col")
    keep_f, send_f = project_grad(place, g, normed, w_all, gain_one, sums, table_part, count, normed_other)
    got_f = along(send_f, 0)
    normed_other = add_low(normed_other, later(normed_other_col, keep_f), keep_f)
    normed_row = swap(normed_other, "row")
    normed_own_col = swap(normed_own_send, "col")
    keep_j, send_j = halve(place, keep_j, got_j, 0, 2, normed_other)
    got_j = along(send_j, 2)
    grad_out_part = add_wide(keep_o, got_o, keep_j)
    keep_f, send_f = halve(place, keep_f, got_f, 0, 1, grad_out_part)
    got_f = along(send_f, 1)
    normed_mine = add_low(normed_own, normed_own_col, keep_f)
    normed_far = swap(normed_mine, "col")
    normed_row = later(normed_row, normed_mine)
    normed_row_far = swap(normed_row, "col")
    keep_f, send_f = halve(place, keep_f, got_f, 0, 2, normed_row)
    got_f = along(send_f, 2)
    grad_tokens = finish(place, tokens, gain_one, grad_hidden, normed_mine, normed_far, normed_row, normed_row_far)
    grad_in_part, part_wo = add_pieces(keep_i, got_i, keep_j, got_j, grad_tokens)
    mine, send = parts_by_row(place, keep_f, got_f, part_wo, grad_in_part)
    per_row = mine.shape[0]
    got = swap(send, "row")
    grad_q, grad_k, grad_v, grad_o, grad_router, grad_table, lines = assemble(place, mine, got, wide, heads, router.shape[1])
    lines = lines[:, :per_row]
    return (
        output,
        grad_tokens,
        (lines + swap(lines, "col"))[0],
        grad_q,
        grad_k,
        grad_v,
        grad_o,
        grad_table,
        lines[1],
        grad_router,
        grad_in_part[None],
        grad_out_part[None],
    )


def solution(mesh):
    in_specs = (
        P(("dp", "row"), None),
        P(("dp", "row"), None),
        P(("dp", "row"), None),
        P(),
        P("row", "col"),
        P("row", "col"),
        P("row", "col"),
        P("row", "col"),
        P(),
        P(),
        P(),
        P(),
        P("row", None, "col"),
        P("row", None, "col"),
    )
    out_specs = (
        P(("dp", "row"), None),
        P(("dp", "row"), None),
        P(("dp", "row")),
        P(("dp", "row"), "col"),
        P(("dp", "row"), "col"),
        P(("dp", "row"), "col"),
        P(("dp", "row"), "col"),
        P(None, "col"),
        P(("dp", "row")),
        P(("dp", "row"), None),
        P("row", "dp", "col"),
        P("row", "dp", "col"),
    )
    paired = mesh.shape["row"] == 2 and mesh.shape["col"] == 2 and mesh.shape["dp"] == 8
    return jax.shard_map(local_pair if paired else local, mesh=mesh, in_specs=in_specs, out_specs=out_specs, check_vma=False)
```

```python
import functools

import jax
import jax.numpy as jnp
from jax import lax
from jax.experimental import pallas as pl
from jax.experimental.pallas import tpu as pltpu
from jax.sharding import PartitionSpec as P

H = 12
NBUCKET = 32


EPS = 1e-06
SCALE = 0.125
HIGHEST = lax.Precision.HIGHEST
NARROW = jnp.bfloat16
WIDE = jnp.float32


def gelu_tanh(values):
    return jax.nn.gelu(values, approximate=True)


def norm_forward(rows, gain):
    inverse = lax.rsqrt(jnp.mean(rows * rows, axis=-1, keepdims=True) + EPS)
    return (rows * inverse * gain, inverse)


def norm_backward(rows, inverse, gain, grad_normed):
    scaled = grad_normed * gain
    grad_rows = inverse * scaled - rows * inverse**3 * jnp.mean(
        scaled * rows, axis=-1, keepdims=True
    )
    return (grad_rows, jnp.sum(grad_normed * rows * inverse, axis=0))


def contract_rows(left, right):
    return lax.dot_general(left, right, (((0,), (0,)), ((), ())), preferred_element_type=WIDE)


def contract_cols(left, right):
    return lax.dot_general(left, right, (((1,), (1,)), ((), ())), preferred_element_type=WIDE)


def split_heads(matrix, heads):
    return matrix.reshape(matrix.shape[0], heads, -1).transpose(1, 0, 2)


def join_heads(stacked):
    return stacked.transpose(1, 0, 2).reshape(stacked.shape[1], -1)


def diagonal_sums(block):
    heads, height, breadth = block.shape
    shifted = jnp.pad(block, ((0, 0), (0, 0), (height, 0))).reshape(
        heads, height * (height + breadth)
    )
    shifted = jnp.pad(shifted, ((0, 0), (0, height))).reshape(heads, height, height + breadth + 1)
    totals = jnp.sum(shifted, axis=1, dtype=WIDE)
    return totals[:, 1 : height + breadth]


def bias_block(offsets, query_start, key_start, queries, keys, seq_len):
    heads = offsets.shape[0]
    begin = key_start - query_start + seq_len - queries
    window = lax.dynamic_slice_in_dim(offsets, begin, queries + keys - 1, 1)
    period = queries + keys
    padded = jnp.pad(window, ((0, 0), (0, 1)))
    spread = jnp.broadcast_to(padded[:, None, :], (heads, queries, period)).reshape(
        heads, queries * period
    )
    skewed = spread[:, : queries * (period - 1)].reshape(heads, queries, period - 1)
    return skewed[:, :, queries - 1 : queries - 1 + keys]


def batch_scores(query_heads, key_heads, bias):
    return (
        SCALE * jnp.einsum("hqd,hkd->hqk", query_heads, key_heads, preferred_element_type=WIDE)
        + bias
    )


def local(
    tokens,
    grad_out,
    routes,
    norm1_gain,
    w_query,
    w_key,
    w_value,
    w_output,
    rel_table,
    rel_bucket,
    norm2_gain,
    router,
    w_in,
    w_out,
):
    tok_rows, width = tokens.shape
    seq_len = tok_rows * lax.axis_size("row")
    heads = H // lax.axis_size("col")
    row_start = lax.axis_index("row") * tok_rows
    tokens_wide = tokens.astype(WIDE)
    gain_one = norm1_gain.astype(WIDE)
    normed, inverse_one = norm_forward(tokens_wide, gain_one)
    normed_low = normed.astype(NARROW)
    query_weight, key_weight, value_weight, output_weight = (
        lax.all_gather(w_query, "row", axis=0, tiled=True),
        lax.all_gather(w_key, "row", axis=0, tiled=True),
        lax.all_gather(w_value, "row", axis=0, tiled=True),
        lax.all_gather(w_output, "row", axis=0, tiled=True),
    )
    query = jnp.dot(normed_low, query_weight, preferred_element_type=WIDE).astype(NARROW)
    key = jnp.dot(normed_low, key_weight, preferred_element_type=WIDE).astype(NARROW)
    value = jnp.dot(normed_low, value_weight, preferred_element_type=WIDE).astype(NARROW)
    keys_all, values_all = (
        lax.all_gather(key, "row", axis=0, tiled=True),
        lax.all_gather(value, "row", axis=0, tiled=True),
    )
    bucket_hot = (rel_bucket[None, :] == jnp.arange(NBUCKET, dtype=jnp.int32)[:, None]).astype(WIDE)
    table_local = lax.dynamic_slice_in_dim(
        rel_table.astype(WIDE), lax.axis_index("col") * heads, heads, 1
    )
    offsets = jnp.dot(table_local.T, bucket_hot, precision=HIGHEST)
    bias = bias_block(offsets, row_start, 0, tok_rows, seq_len, seq_len)
    query_heads = split_heads(query, heads)
    key_heads = split_heads(keys_all, heads)
    value_heads = split_heads(values_all, heads)
    scores = batch_scores(query_heads, key_heads, bias)
    ceiling = jnp.max(scores, axis=2, keepdims=True)
    raised = jnp.exp(scores - ceiling)
    summed = jnp.sum(raised, axis=2, keepdims=True)
    attended_heads = jnp.einsum(
        "hqk,hkd->hqd", (raised / summed).astype(NARROW), value_heads, preferred_element_type=WIDE
    )
    log_total = ceiling[:, :, 0] + jnp.log(summed[:, :, 0])
    attended = join_heads(attended_heads).astype(NARROW)
    branch = lax.psum(contract_cols(attended, output_weight), "col")
    hidden = tokens_wide + branch
    gain_two = norm2_gain.astype(WIDE)
    hn, inverse_two = norm_forward(hidden, gain_two)
    router_wide = router.astype(WIDE)
    gate_probs = jax.nn.softmax(jnp.dot(hn, router_wide, precision=HIGHEST), axis=-1)
    n_exp = router.shape[1]
    capacity = 2 * tok_rows // n_exp
    expert_ids = routes[:, 0]
    one_hot_int = (expert_ids[:, None] == jnp.arange(n_exp, dtype=jnp.int32)[None, :]).astype(
        jnp.int32
    )
    one_hot = one_hot_int.astype(WIDE)
    gate = jnp.sum(gate_probs * one_hot, axis=1)
    rank_own = jnp.sum((jnp.cumsum(one_hot_int, axis=0) - 1) * one_hot_int, axis=1)
    slot_ids = expert_ids * capacity + rank_own
    grad_wide = grad_out.astype(WIDE)
    send_rows = hn.astype(NARROW)
    send_grads = (gate[:, None] * grad_wide).astype(NARROW)
    box_rows = (
        jnp.zeros((n_exp * capacity, width), NARROW)
        .at[slot_ids]
        .set(send_rows)
        .reshape(n_exp, capacity, width)
    )
    box_grads = (
        jnp.zeros((n_exp * capacity, width), NARROW)
        .at[slot_ids]
        .set(send_grads)
        .reshape(n_exp, capacity, width)
    )
    got_rows, got_grads = (
        lax.all_to_all(box_rows, "row", split_axis=0, concat_axis=0, tiled=True),
        lax.all_to_all(box_grads, "row", split_axis=0, concat_axis=0, tiled=True),
    )
    expert_in = got_rows.reshape(-1, width)
    expert_grad = got_grads.reshape(-1, width)
    weight_in = w_in[0]
    weight_out = w_out[0]
    pre = jnp.dot(expert_in, weight_in, preferred_element_type=WIDE)
    act, act_back = jax.vjp(gelu_tanh, pre)
    act_low = act.astype(NARROW)
    out_part = contract_cols(act_low, weight_out)
    grad_act = jnp.dot(expert_grad, weight_out, preferred_element_type=WIDE)
    grad_pre = act_back(grad_act)[0].astype(NARROW)
    rows_part = contract_cols(grad_pre, weight_in)
    grad_weight_in = contract_rows(expert_in, grad_pre)
    grad_weight_out = contract_rows(expert_grad, act_low)
    out_sum, rows_sum = lax.psum((out_part, rows_part), "col")
    back_out, back_rows = (
        lax.all_to_all(
            out_sum.astype(NARROW).reshape(n_exp, capacity, width),
            "row",
            split_axis=0,
            concat_axis=0,
            tiled=True,
        ),
        lax.all_to_all(
            rows_sum.astype(NARROW).reshape(n_exp, capacity, width),
            "row",
            split_axis=0,
            concat_axis=0,
            tiled=True,
        ),
    )
    expert_out = back_out.reshape(-1, width)[slot_ids].astype(WIDE)
    grad_rows = back_rows.reshape(-1, width)[slot_ids].astype(WIDE)
    output = (hidden + gate[:, None] * expert_out).astype(NARROW)
    grad_in_shard, grad_out_shard = (
        lax.psum_scatter(
            grad_weight_in.astype(jnp.bfloat16), "dp", scatter_dimension=0, tiled=True
        ).astype(jnp.float32),
        lax.psum_scatter(
            grad_weight_out.astype(jnp.bfloat16), "dp", scatter_dimension=0, tiled=True
        ).astype(jnp.float32),
    )
    grad_gate = jnp.sum(grad_wide * expert_out, axis=1)
    grad_logits = (grad_gate * gate)[:, None] * (one_hot - gate_probs)
    grad_router = jnp.dot(hn.T, grad_logits, precision=HIGHEST)
    grad_hn = grad_rows + jnp.dot(grad_logits, router_wide.T, precision=HIGHEST)
    grad_hidden_norm, grad_gain_two = norm_backward(hidden, inverse_two, gain_two, grad_hn)
    grad_hidden = grad_wide + grad_hidden_norm
    grad_branch = grad_hidden.astype(NARROW)
    grad_w_output = contract_rows(grad_branch, attended)
    grad_attended = jnp.dot(grad_branch, output_weight, preferred_element_type=WIDE).astype(NARROW)
    grad_heads = split_heads(grad_attended, heads)
    diagonal_start = seq_len - row_start - tok_rows
    shares = jnp.exp(batch_scores(query_heads, key_heads, bias) - log_total[:, :, None])
    grad_shares = jnp.einsum("hqd,hkd->hqk", grad_heads, value_heads, preferred_element_type=WIDE)
    deltas = jnp.sum(shares * grad_shares, axis=2)
    grad_scores = (shares * (grad_shares - deltas[:, :, None])).astype(NARROW)
    grad_query_heads = SCALE * jnp.einsum(
        "hqk,hkd->hqd", grad_scores, key_heads, preferred_element_type=WIDE
    )
    diagonals = diagonal_sums(grad_scores)
    bucket_window = lax.dynamic_slice_in_dim(bucket_hot, diagonal_start, tok_rows + seq_len - 1, 1)
    table_part = jnp.dot(bucket_window, diagonals.T, precision=HIGHEST)
    grad_key_heads = SCALE * jnp.einsum(
        "hqk,hqd->hkd", grad_scores, query_heads, preferred_element_type=WIDE
    )
    grad_value_heads = jnp.einsum(
        "hqk,hqd->hkd", shares.astype(NARROW), grad_heads, preferred_element_type=WIDE
    )
    grad_key, grad_value = (
        lax.psum_scatter(
            join_heads(grad_key_heads).astype(jnp.bfloat16), "row", scatter_dimension=0, tiled=True
        ).astype(jnp.float32),
        lax.psum_scatter(
            join_heads(grad_value_heads).astype(jnp.bfloat16),
            "row",
            scatter_dimension=0,
            tiled=True,
        ).astype(jnp.float32),
    )
    grad_query = join_heads(grad_query_heads).astype(NARROW)
    grad_key_low = grad_key.astype(NARROW)
    grad_value_low = grad_value.astype(NARROW)
    grad_w_query = contract_rows(normed_low, grad_query)
    grad_w_key = contract_rows(normed_low, grad_key_low)
    grad_w_value = contract_rows(normed_low, grad_value_low)
    normed_part = (
        contract_cols(grad_query, query_weight)
        + contract_cols(grad_key_low, key_weight)
        + contract_cols(grad_value_low, value_weight)
    )
    grad_normed = lax.psum(normed_part.astype(jnp.bfloat16), "col").astype(jnp.float32)
    grad_tokens_norm, grad_gain_one = norm_backward(tokens_wide, inverse_one, gain_one, grad_normed)
    grad_tokens = grad_hidden + grad_tokens_norm
    grad_table = lax.psum(table_part, ("dp", "row"))
    (
        grads_query,
        grads_key,
        grads_value,
        grads_output,
        grads_gain_one,
        grads_gain_two,
        grads_router,
    ) = (
        lax.psum_scatter(grad_w_query, ("dp", "row"), scatter_dimension=0, tiled=True),
        lax.psum_scatter(grad_w_key, ("dp", "row"), scatter_dimension=0, tiled=True),
        lax.psum_scatter(grad_w_value, ("dp", "row"), scatter_dimension=0, tiled=True),
        lax.psum_scatter(grad_w_output, ("dp", "row"), scatter_dimension=0, tiled=True),
        lax.psum_scatter(grad_gain_one, ("dp", "row"), scatter_dimension=0, tiled=True),
        lax.psum_scatter(grad_gain_two, ("dp", "row"), scatter_dimension=0, tiled=True),
        lax.psum_scatter(grad_router, ("dp", "row"), scatter_dimension=0, tiled=True),
    )
    return (
        output,
        grad_tokens,
        grads_gain_one,
        grads_query,
        grads_key,
        grads_value,
        grads_output,
        grad_table,
        grads_gain_two,
        grads_router,
        grad_in_shard[None],
        grad_out_shard[None],
    )


VMEM = pltpu.VMEM
SMEM = pltpu.SMEM


def dot_nn(a, b):
    return lax.dot_general(a, b, (((1,), (0,)), ((), ())), preferred_element_type=WIDE)


def dot_nt(a, b):
    return lax.dot_general(a, b, (((1,), (1,)), ((), ())), preferred_element_type=WIDE)


def dot_tn(a, b):
    return lax.dot_general(a, b, (((0,), (0,)), ((), ())), preferred_element_type=WIDE)


def later(value, *others):
    return lax.optimization_barrier((value, *others))[0]


def full_spec(shape):
    return pl.BlockSpec(shape, lambda *_: (0,) * len(shape))


def smem_spec():
    return pl.BlockSpec(memory_space=SMEM)


def params(megabytes=28):
    return pltpu.CompilerParams(vmem_limit_bytes=megabytes * 1024 * 1024)


def cost(micros):
    return pl.CostEstimate(flops=int(micros * 575e6), bytes_accessed=0, transcendentals=0)


def shape_of(shape, dtype):
    return jax.ShapeDtypeStruct(shape, dtype)


def pack_kernel(place, w_query, w_key, w_value, own, send):
    row, bit = place[0], place[2] & 1
    wide = own.shape[1] // 3
    part = pl.ds(pl.multiple_of(bit * send.shape[0], 16), send.shape[0])
    for i, w in enumerate((w_query, w_key, w_value)):
        lanes = slice(i * wide, (i + 1) * wide)

        @pl.when(row == 0)
        def _():
            own[:, lanes] = w[:, :wide]
            send[:, lanes] = w[part, wide:]

        @pl.when(row == 1)
        def _():
            own[:, lanes] = w[:, wide:]
            send[:, lanes] = w[part, :wide]


def pack(place, w_query, w_key, w_value):
    rows, cols = w_query.shape
    vmem = pl.BlockSpec(memory_space=VMEM)
    return pl.pallas_call(
        pack_kernel,
        in_specs=[smem_spec()] + [vmem] * 3,
        out_specs=[vmem] * 2,
        out_shape=[shape_of((rows, 3 * cols // 2), NARROW), shape_of((rows // 2, 3 * cols // 2), NARROW)],
        compiler_params=params(60),
        cost_estimate=cost(2),
        name="pack",
    )(place, w_query, w_key, w_value)


def half_kernel(place, value, out):
    out[...] = value[...]


def half_of(place, value, after):
    rows, width = value.shape[0] // 2, value.shape[1]
    return pl.pallas_call(
        half_kernel,
        grid_spec=pltpu.PrefetchScalarGridSpec(
            num_scalar_prefetch=1,
            grid=(1,),
            in_specs=[pl.BlockSpec((rows, width), lambda i, place: (place[1], 0))],
            out_specs=pl.BlockSpec((rows, width), lambda i, place: (0, 0)),
        ),
        out_shape=shape_of((rows, width), value.dtype),
        compiler_params=params(10),
        cost_estimate=cost(1),
        name="half_of",
    )(place, later(value, after))


def project_kernel(place, tok_own, tok_got, tok_col, gain, w_own, w_got, w_far, tok, normed, q, k, v, w_all):
    half = w_own.shape[0]
    quarter = w_got.shape[0]
    row, col, bit = place[0], place[1], place[2] & 1
    step = pl.program_id(0)

    @pl.when(step == 0)
    def _():
        base = (1 - row) * half
        w_all[pl.ds(pl.multiple_of(row * half, 16), half)] = w_own[...]
        w_all[pl.ds(pl.multiple_of(base + bit * quarter, 16), quarter)] = w_got[...]
        w_all[pl.ds(pl.multiple_of(base + (1 - bit) * quarter, 16), quarter)] = w_far[...]

    @pl.when(step < 2)
    def _():
        tok[...] = tok_own[...]

    @pl.when(step - 2 == col)
    def _():
        tok[...] = tok_got[...]

    @pl.when(step - 2 == 1 - col)
    def _():
        tok[...] = tok_col[...]

    rows = tok[...].astype(WIDE)
    inverse = lax.rsqrt(jnp.mean(rows * rows, axis=-1, keepdims=True) + EPS)
    low = (rows * inverse * gain[...].astype(WIDE)).astype(NARROW)
    normed[...] = low
    out = dot_nn(low, w_all[...])
    heads, _, size = q.shape
    wide = heads * size
    for h in range(heads):
        q[h] = (out[:, h * size : (h + 1) * size] * SCALE).astype(NARROW)
        k[h] = out[:, wide + h * size : wide + (h + 1) * size].astype(NARROW)
        v[h] = out[:, 2 * wide + h * size : 2 * wide + (h + 1) * size].astype(NARROW)


def project(place, toks, gain, w_parts, heads, size):
    block, width = toks[1].shape
    seq = 4 * block
    cols = w_parts[0].shape[1]
    head_spec = pl.BlockSpec((heads, block, size), lambda i: (0, i, 0))
    row_spec = pl.BlockSpec((block, width), lambda i: (i, 0))
    head_shape = shape_of((heads, seq, size), NARROW)
    return pl.pallas_call(
        project_kernel,
        grid=(4,),
        in_specs=[smem_spec(), pl.BlockSpec((block, width), lambda i: (jnp.minimum(i, 1), 0))]
        + [full_spec(x.shape) for x in (*toks[1:], gain, *w_parts)],
        out_specs=[row_spec, row_spec, head_spec, head_spec, head_spec, full_spec((width, cols))],
        out_shape=[shape_of((seq, width), NARROW)] * 2 + [head_shape] * 3 + [shape_of((width, cols), NARROW)],
        compiler_params=params(28),
        cost_estimate=cost(3.3),
        name="project",
    )(
        place,
        pltpu.with_memory_space_constraint(toks[0], pltpu.HBM),
        *toks[1:],
        gain,
        pltpu.with_memory_space_constraint(w_parts[0], pltpu.HBM),
        *w_parts[1:],
    )


TILE = 128
TABLE_LANE = 4


def bias_lanes(row, block_index, blocks):
    half = blocks // 2
    query = lax.rem(block_index + half * row, blocks)
    own = half * row - query + blocks
    other = half * (1 - row) - query + blocks
    return pl.multiple_of(own * TILE, TILE), pl.multiple_of(other * TILE, TILE)


def skew_kernel(bucket, table, skew):
    n = bucket.shape[1]
    hot = (bucket[...] == lax.broadcasted_iota(jnp.int32, (NBUCKET, n), 0)).astype(WIDE)
    for h in range(skew.shape[0]):
        line = jnp.sum(hot * table[:, h : h + 1], axis=0, keepdims=True)
        skew[h] = pltpu.roll(jnp.broadcast_to(line, (TILE, n)), 0, 1, stride=1, stride_axis=0)


def skewed_bias(bucket, table, after):
    vmem = pl.BlockSpec(memory_space=VMEM)
    return pl.pallas_call(
        skew_kernel,
        in_specs=[vmem] * 2,
        out_specs=vmem,
        out_shape=shape_of((table.shape[1], TILE, bucket.shape[1]), WIDE),
        compiler_params=params(12),
        cost_estimate=cost(1),
        name="skewed_bias",
    )(bucket, later(table, after))


def attend_kernel(first, place, skew, q, k, v, att, p):
    heads, block, size = q.shape
    seq = k.shape[1]
    half = seq // 2
    row = place[0]
    step = pl.program_id(0)

    for h in range(heads):
        raw = dot_nt(q[h], k[h])
        parts = []
        for sub in range(block // TILE):
            own, other = bias_lanes(row, first + step * (block // TILE) + sub, seq // TILE)
            bias = jnp.concatenate([skew[h, :, pl.ds(own, half)], skew[h, :, pl.ds(other, half)]], axis=1)
            scores = raw[sub * TILE : (sub + 1) * TILE] + bias
            raised = jnp.exp(scores - jnp.max(scores, axis=1, keepdims=True))
            share = raised * (1.0 / jnp.sum(raised, axis=1, keepdims=True))
            parts.append(share.astype(NARROW))
        shares = jnp.concatenate(parts, axis=0)
        p[h] = shares
        att[:, h * size : (h + 1) * size] = dot_nn(shares, v[h]).astype(NARROW)


def attend(place, skew, q, k, v, block, begin, rows):
    heads, seq, size = q.shape
    start = begin // block
    return pl.pallas_call(
        functools.partial(attend_kernel, begin // TILE),
        grid=(rows // block,),
        in_specs=[
            smem_spec(),
            full_spec(skew.shape),
            pl.BlockSpec((heads, block, size), lambda i: (0, i + start, 0)),
            full_spec(k.shape),
            full_spec(v.shape),
        ],
        out_specs=[
            pl.BlockSpec((block, heads * size), lambda i: (i, 0)),
            pl.BlockSpec((heads, block, seq), lambda i: (0, i, 0)),
        ],
        out_shape=[shape_of((rows, heads * size), NARROW), pltpu.HBM((heads, rows, seq), NARROW)],
        compiler_params=params(),
        cost_estimate=cost(9.3),
        name="attend",
    )(place, skew, q, k, v)


def attend_back_kernel(first, last, place, bucket, q, k, v, p, g, *refs):
    if first == 0:
        keep_in = None
    else:
        keep_in, refs = refs[:3], refs[3:]
    if last:
        out, table, key_sum, value_sum, diag = refs
        query_out = None
    else:
        query_out, key_sum, value_sum, diag = refs
        out = None
    heads, block, size = q.shape
    seq = k.shape[1]
    half = seq // 2
    row = place[0]
    step = pl.program_id(0)

    @pl.when(step == 0)
    def _():
        if keep_in is None:
            key_sum[...] = jnp.zeros_like(key_sum)
            value_sum[...] = jnp.zeros_like(value_sum)
            diag[...] = jnp.zeros_like(diag)
        else:
            key_sum[...] = keep_in[0][...]
            value_sum[...] = keep_in[1][...]
            diag[...] = keep_in[2][...]

    wide = heads * size
    for h in range(heads):
        grad = g[:, h * size : (h + 1) * size]
        share_low = p[h]
        share = share_low.astype(WIDE)
        grad_share = dot_nt(grad, v[h])
        delta = jnp.sum(share * grad_share, axis=1, keepdims=True)
        grad_score = share * (grad_share - delta)
        for sub in range(block // TILE):
            own, other = bias_lanes(row, first + step * (block // TILE) + sub, seq // TILE)
            piece = grad_score[sub * TILE : (sub + 1) * TILE]
            diag[h, :, pl.ds(own, half)] += piece[:, :half]
            diag[h, :, pl.ds(other, half)] += piece[:, half:]
        low = grad_score.astype(NARROW)
        grad_query = (SCALE * dot_nn(low, k[h])).astype(NARROW)
        if last:
            out[pl.ds(pl.multiple_of(first * TILE + step * block, block), block), h * size : (h + 1) * size] = grad_query
        else:
            query_out[:, h * size : (h + 1) * size] = grad_query
        key_sum[h] += dot_tn(q[h], low)
        value_sum[h] += dot_tn(grad, share_low)

    if last:
        lanes = diag.shape[2]

        @pl.when(step == pl.num_programs(0) - 1)
        def _():
            hot = (bucket[...] == lax.broadcasted_iota(jnp.int32, (NBUCKET, lanes), 0)).astype(WIDE)
            lane = lax.broadcasted_iota(jnp.int32, table.shape, 1)
            total = jnp.zeros(table.shape, WIDE)
            for h in range(heads):
                lo = h * size
                out[:, wide + lo : wide + lo + size] = key_sum[h].T.astype(NARROW)
                out[:, 2 * wide + lo : 2 * wide + lo + size] = value_sum[h].T.astype(NARROW)
                sums = diag[h]
                height = TILE // 2
                while height >= 8:
                    sums = sums[:height] + pltpu.roll(sums[height:], lanes - height, 1)
                    height //= 2
                where = lax.broadcasted_iota(jnp.int32, sums.shape, 0)
                for bit in (4, 2, 1):
                    sums = jnp.where((where & bit) != 0, pltpu.roll(sums, lanes - bit, 1), sums)
                line = jnp.sum(sums, axis=0, keepdims=True)
                total = total + jnp.where(lane == TABLE_LANE + h, jnp.sum(hot * line, axis=1, keepdims=True), 0.0)
            table[...] = total


def attend_back(place, bucket, q, k, v, p, g, block, begin, keep, after=None):
    heads, seq, size = q.shape
    rows = g.shape[0]
    start = begin // block
    last = keep is not None
    lanes = bucket.shape[1]
    sum_shape = (heads, size, seq)
    diag_shape = (heads, TILE, lanes)
    wide = heads * size
    in_specs = [
        smem_spec(),
        full_spec(bucket.shape),
        pl.BlockSpec((heads, block, size), lambda i: (0, i + start, 0)),
        full_spec(k.shape),
        full_spec(v.shape),
        pl.BlockSpec((heads, block, seq), lambda i: (0, i + start, 0)),
        pl.BlockSpec((block, wide), lambda i: (i, 0)),
    ]
    args = [place, bucket, q, k, v, p, g]
    sums = [shape_of(sum_shape, WIDE), shape_of(sum_shape, WIDE), shape_of(diag_shape, WIDE)]
    if last:
        in_specs += [full_spec(s.shape) for s in sums]
        args += list(keep[1:])
        in_specs += [full_spec(keep[0].shape)]
        args += [keep[0]]
        args[6] = later(g, after)
        out_specs = [full_spec((seq, 3 * wide)), full_spec((NBUCKET, 128))]
        out_shape = [shape_of((seq, 3 * wide), NARROW), shape_of((NBUCKET, 128), WIDE)]
        scratch = [VMEM(s.shape, WIDE) for s in sums]

        def kernel(*refs):
            earlier = refs[10]
            out = refs[11]

            @pl.when(pl.program_id(0) == 0)
            def _():
                out[: earlier.shape[0], :wide] = earlier[...]

            attend_back_kernel(begin // TILE, True, *refs[:10], *refs[11:])

    else:
        out_specs = [pl.BlockSpec((block, wide), lambda i: (i, 0))] + [full_spec(s.shape) for s in sums]
        out_shape = [shape_of((rows, wide), NARROW)] + sums
        scratch = []
        kernel = functools.partial(attend_back_kernel, begin // TILE, False)
    return pl.pallas_call(
        kernel,
        grid=(rows // block,),
        in_specs=in_specs,
        out_specs=out_specs,
        out_shape=out_shape,
        scratch_shapes=scratch,
        compiler_params=params(),
        cost_estimate=cost(12),
        name="attend_back",
    )(*args)


def column(lines):
    count = lines.shape[0]
    wide = jnp.concatenate([lines, jnp.zeros((128 - count, 128), lines.dtype)], axis=0).T
    return jnp.concatenate([wide[:, i : i + 1] for i in range(count)], axis=0)


def gate_values(hn, route, router):
    count = router.shape[0]
    logits = [jnp.sum(hn * router[e : e + 1], axis=1, keepdims=True) for e in range(count)]
    top = functools.reduce(jnp.maximum, logits)
    raised = [jnp.exp(x - top) for x in logits]
    total = functools.reduce(jnp.add, raised)
    probs = [x / total for x in raised]
    hots = [(route == float(e)).astype(WIDE) for e in range(count)]
    gate = functools.reduce(jnp.add, [p * o for p, o in zip(probs, hots)])
    return probs, hots, gate


def hidden_kernel(place, a_mine, a_row, a_col, a_diag, w_mine, w_other, tok, gain, router, kinds, hidden, att, rows, scale, pack, route):
    row = place[0]
    step = pl.program_id(0)
    size = a_mine.shape[1]

    @pl.when(step == 0)
    def _():
        route[...] = column(kinds[...])

    @pl.when(row == 0)
    def _():
        pack[0, :, :size] = a_mine[...]
        pack[0, :, size:] = a_row[...]
        pack[1, :, :size] = a_col[...]
        pack[1, :, size:] = a_diag[...]

    @pl.when(row == 1)
    def _():
        pack[0, :, size:] = a_mine[...]
        pack[0, :, :size] = a_row[...]
        pack[1, :, size:] = a_col[...]
        pack[1, :, :size] = a_diag[...]

    branch = dot_nt(pack[0], w_mine[...]) + dot_nt(pack[1], w_other[...])
    wide = tok[...].astype(WIDE) + branch

    @pl.when(step < 2)
    def _():
        hidden[...] = wide
        att[...] = pack[0]

    inverse = lax.rsqrt(jnp.mean(wide * wide, axis=-1, keepdims=True) + EPS)
    hn = wide * inverse * gain[...].astype(WIDE)
    block = wide.shape[0]
    kind = route[pl.ds(pl.multiple_of(step * block, 16), block), :]
    _, hots, gate = gate_values(hn, kind, router)
    chosen = jnp.where(kind == row.astype(WIDE), 1.0, 0.0)
    rows[...] = (hn * chosen).astype(NARROW)
    scale[...] = gate * chosen


def hidden_rows(place, pieces, w_mine, w_other, tok_all, gain, router, route_all):
    seq, width = tok_all.shape
    block = seq // 4
    size = pieces[0].shape[1]
    half = w_mine.shape[1]
    turned = pl.BlockSpec((block, size), lambda i: (lax.rem(i + 2, 4), 0))
    plain = pl.BlockSpec((block, size), lambda i: (i, 0))
    wide_spec = pl.BlockSpec((block, width), lambda i: (i, 0))
    own_spec = pl.BlockSpec((block, width), lambda i: (jnp.minimum(i, 1), 0))
    mixed = pl.BlockSpec((block, width), lambda i: (lax.rem(i, 2) * 2 + lax.div(i, 2), 0))
    mixed_line = pl.BlockSpec((block, 1), lambda i: (lax.rem(i, 2) * 2 + lax.div(i, 2), 0))
    return pl.pallas_call(
        hidden_kernel,
        grid=(4,),
        in_specs=[
            smem_spec(),
            plain,
            turned,
            plain,
            turned,
            full_spec(w_mine.shape),
            full_spec(w_other.shape),
            wide_spec,
            full_spec(gain.shape),
            full_spec(router.shape),
            full_spec(route_all.shape),
        ],
        out_specs=[own_spec, pl.BlockSpec((block, half), lambda i: (jnp.minimum(i, 1), 0)), mixed, mixed_line],
        out_shape=[
            shape_of((seq // 2, width), WIDE),
            shape_of((seq // 2, half), NARROW),
            shape_of((seq, width), NARROW),
            shape_of((seq, 1), WIDE),
        ],
        scratch_shapes=[VMEM((2, block, half), NARROW), VMEM((seq, 1), WIDE)],
        compiler_params=params(),
        cost_estimate=cost(6),
        name="hidden_rows",
    )(place, *pieces, w_mine, w_other, tok_all, gain, router, route_all)


def scale_kernel(place, own, got, got_col, scale, out):
    col = place[1]
    block = got.shape[0]
    for half in range(2):
        first = pl.ds(2 * half * block, block)
        second = pl.ds((2 * half + 1) * block, block)
        out[first, :] = (own[half * block : (half + 1) * block, :].astype(WIDE) * scale[first, :]).astype(NARROW)
        other = jnp.where(col == half, got[...].astype(WIDE), got_col[...].astype(WIDE))
        out[second, :] = (other * scale[second, :]).astype(NARROW)


def scale_grads(place, own, got, got_col, scale):
    args = (place, own, got, got_col, scale)
    vmem = pl.BlockSpec(memory_space=VMEM)
    return pl.pallas_call(
        scale_kernel,
        in_specs=[smem_spec()] + [vmem] * 4,
        out_specs=vmem,
        out_shape=shape_of((2 * own.shape[0], own.shape[1]), NARROW),
        compiler_params=params(10),
        cost_estimate=cost(1.4),
        name="scale_grads",
    )(*args)


def store_quarters(mine, value, keeps, sends):
    rows = keeps[0].shape[0]
    for part in range(2):
        low = slice(part * rows, (part + 1) * rows)
        high = slice((2 + part) * rows, (3 + part) * rows)

        @pl.when(mine == 0)
        def _():
            keeps[part][...] = value[low].astype(NARROW)
            sends[part][...] = value[high].astype(NARROW)

        @pl.when(mine == 1)
        def _():
            keeps[part][...] = value[high].astype(NARROW)
            sends[part][...] = value[low].astype(NARROW)


def expert_out_kernel(place, x, w_in, w_out, act, slope, keep_own, keep_other, send_own, send_other, total):
    step = pl.program_id(0)
    pre = dot_nn(x[...], w_in[...])
    square = pre * pre
    bent = jnp.tanh(pre * (0.7978845608028654 + (0.7978845608028654 * 0.044715) * square))
    half = 0.5 + 0.5 * bent
    act_low = (pre * half).astype(NARROW)
    act[...] = act_low
    inner = 0.7978845608028654 + (0.7978845608028654 * 0.134145) * square
    slope[...] = (half + (0.5 * pre) * ((1.0 - bent * bent) * inner)).astype(NARROW)
    piece = dot_nt(act_low, w_out[...])

    @pl.when(step == 0)
    def _():
        total[...] = piece

    @pl.when(step > 0)
    def _():
        total[...] += piece

    @pl.when(step == pl.num_programs(0) - 1)
    def _():
        store_quarters(place[1], total, (keep_own, keep_other), (send_own, send_other))


def expert_back_kernel(place, g, slope, w_in, w_out, grad_pre, keep_own, keep_other, send_own, send_other, total):
    step = pl.program_id(0)
    low = (dot_nn(g[...], w_out[...]) * slope[...].astype(WIDE)).astype(NARROW)
    grad_pre[...] = low
    piece = dot_nt(low, w_in[...])

    @pl.when(step == 0)
    def _():
        total[...] = piece

    @pl.when(step > 0)
    def _():
        total[...] += piece

    @pl.when(step == pl.num_programs(0) - 1)
    def _():
        store_quarters(place[1], total, (keep_own, keep_other), (send_own, send_other))


def expert_forward(place, x, w_in, w_out, block):
    seq, width = x.shape
    units = w_in.shape[1]
    w_spec = pl.BlockSpec((width, block), lambda i: (0, i))
    unit_spec = pl.BlockSpec((seq, block), lambda i: (0, i))
    quarter = (seq // 4, width)
    return pl.pallas_call(
        expert_out_kernel,
        grid=(units // block,),
        in_specs=[smem_spec(), full_spec(x.shape), w_spec, w_spec],
        out_specs=[unit_spec, unit_spec] + [full_spec(quarter)] * 4,
        out_shape=[shape_of((seq, units), NARROW), pltpu.HBM((seq, units), NARROW)] + [shape_of(quarter, NARROW)] * 4,
        scratch_shapes=[VMEM(x.shape, WIDE)],
        compiler_params=params(),
        cost_estimate=cost(9.4),
        name="expert_forward",
    )(place, x, w_in, w_out)


def expert_backward(place, g, slope, w_in, w_out, block, *after):
    seq, width = g.shape
    units = w_in.shape[1]
    w_spec = pl.BlockSpec((width, block), lambda i: (0, i))
    unit_spec = pl.BlockSpec((seq, block), lambda i: (0, i))
    quarter = (seq // 4, width)
    return pl.pallas_call(
        expert_back_kernel,
        grid=(units // block,),
        in_specs=[smem_spec(), full_spec(g.shape), unit_spec, w_spec, w_spec],
        out_specs=[unit_spec] + [full_spec(quarter)] * 4,
        out_shape=[shape_of((seq, units), NARROW)] + [shape_of(quarter, NARROW)] * 4,
        scratch_shapes=[VMEM(g.shape, WIDE)],
        compiler_params=params(),
        cost_estimate=cost(8),
        name="expert_backward",
    )(place, later(g, *after), slope, w_in, w_out)


def store_chunks(place, bit, value, keep, send, lanes=slice(None)):
    rows = keep.shape[1]
    mine = (place[2] >> bit) & 1
    low = (1 << bit) - 1
    for j in range(2 * keep.shape[0]):
        at = ((j >> (bit + 1)) << bit) | (j & low)
        chunk = value[j * rows : (j + 1) * rows].astype(NARROW)

        @pl.when(mine == (j >> bit) & 1)
        def _():
            keep[at, :, lanes] = chunk

        @pl.when(mine != (j >> bit) & 1)
        def _():
            send[at, :, lanes] = chunk


def weight_grad_kernel(bits, lanes, place, left, right, *refs):
    turned = refs[-1]
    turned[...] = left[...].T
    for piece, bit in enumerate(bits):
        value = dot_nn(turned[...], right[:, piece * lanes : (piece + 1) * lanes])
        store_chunks(place, bit, value, refs[2 * piece], refs[2 * piece + 1])


def weight_grad(place, left, right, bits, lanes, count, after):
    seq, width = left.shape
    shape = shape_of((count // 2, width // count, lanes), NARROW)
    vmem = pl.BlockSpec(memory_space=VMEM)
    outs = [shape] * (2 * len(bits))
    return pl.pallas_call(
        functools.partial(weight_grad_kernel, bits, lanes),
        in_specs=[smem_spec()] + [vmem] * 2,
        out_specs=[vmem] * len(outs),
        out_shape=outs,
        scratch_shapes=[VMEM((width, seq), NARROW)],
        compiler_params=params(16),
        cost_estimate=cost(0.2),
        name="weight_grad",
    )(place, later(left, after), right)


def weight_grads_kernel(start, place, rows, grad_pre, grads, act, keep, send, keep_next, send_next, keep_out, send_out, turned):
    lanes = keep.shape[2]
    turned[...] = rows[...].T
    store_chunks(place, 0, dot_nn(turned[...], grad_pre[:, :lanes]), keep, send)
    store_chunks(place, 0, dot_nn(turned[...], grad_pre[:, lanes:]), keep_next, send_next)
    turned[...] = grads[...].T
    store_chunks(place, 1, dot_nn(turned[...], act[:, start:]), keep_out, send_out)


def weight_grads(place, rows, grad_pre, grads, act, start, count, after):
    seq, width = rows.shape
    units = act.shape[1]
    first = shape_of((count // 2, width // count, units // 2), NARROW)
    second = shape_of((count // 2, width // count, units - start), NARROW)
    vmem = pl.BlockSpec(memory_space=VMEM)
    return pl.pallas_call(
        functools.partial(weight_grads_kernel, start),
        in_specs=[smem_spec()] + [vmem] * 4,
        out_specs=[vmem] * 6,
        out_shape=[first] * 4 + [second] * 2,
        scratch_shapes=[VMEM((width, seq), NARROW)],
        compiler_params=params(16),
        cost_estimate=cost(0.2),
        name="weight_grads",
    )(place, later(rows, after), grad_pre, grads, act)


def combine_kernel(
    place, hidden, outs, out_far, out_row, out_row_far, backs, back_far, back_row, back_row_far, grad, kinds, gain, router, w_mine, att,
    output, grad_hidden, sums, back_own, back_send, w_keep, w_send, w_sum, route,
):
    row, col = place[0], place[1]
    step = pl.program_id(0)
    block = hidden.shape[0]
    count = router.shape[0]
    size = back_own.shape[1]

    @pl.when(step == 0)
    def _():
        route[...] = column(kinds[...])
        sums[...] = jnp.zeros_like(sums)

    gain_wide = gain[...].astype(WIDE)
    mine = col == step

    def chosen(own, own_row, far, far_row):
        return jnp.where(mine, own[...].astype(WIDE) + own_row[...].astype(WIDE), far[...].astype(WIDE) + far_row[...].astype(WIDE))

    expert_out = chosen(outs, out_row, out_far, out_row_far)
    grad_rows = chosen(backs, back_row, back_far, back_row_far)
    wide = hidden[...]
    grad_wide = grad[...].astype(WIDE)
    inverse = lax.rsqrt(jnp.mean(wide * wide, axis=-1, keepdims=True) + EPS)
    scaled = wide * inverse
    hn = scaled * gain_wide
    probs, hots, gate = gate_values(hn, route[pl.ds(pl.multiple_of(step * block, 16), block), :], router)
    output[...] = (wide + gate * expert_out).astype(NARROW)
    grad_gate = jnp.sum(grad_wide * expert_out, axis=1, keepdims=True) * gate
    grad_hn = grad_rows
    line = lax.broadcasted_iota(jnp.int32, sums.shape, 0)
    packed = jnp.zeros(sums.shape, WIDE)
    for e in range(count):
        grad_logit = grad_gate * (hots[e] - probs[e])
        grad_hn = grad_hn + grad_logit * router[e : e + 1]
        packed = packed + jnp.where(line == 1 + e, jnp.sum(hn * grad_logit, axis=0, keepdims=True), 0.0)
    sums[...] += packed + jnp.where(line == 0, jnp.sum(grad_hn * scaled, axis=0, keepdims=True), 0.0)
    u = grad_hn * gain_wide
    back = grad_wide + inverse * u - wide * (inverse * inverse * inverse) * jnp.mean(u * wide, axis=-1, keepdims=True)
    grad_hidden[...] = back
    low = back.astype(NARROW)
    grad_att = dot_nn(low, w_mine[...]).astype(NARROW)

    @pl.when(row == 0)
    def _():
        back_own[...] = grad_att[:, :size]
        back_send[...] = grad_att[:, size:]

    @pl.when(row == 1)
    def _():
        back_own[...] = grad_att[:, size:]
        back_send[...] = grad_att[:, :size]

    piece = dot_tn(low, att[...])

    @pl.when(step == 0)
    def _():
        w_sum[...] = piece

    @pl.when(step == 1)
    def _():
        store_chunks(place, 0, w_sum[...] + piece, w_keep, w_send)


def combine(place, hidden, outs, backs, grad, kinds, gain, router, w_mine, att, size, count, after):
    tokens, width = hidden.shape
    half = w_mine.shape[1]
    block = tokens // 2
    rows = pl.BlockSpec((block, width), lambda i: (i, 0))
    narrow = pl.BlockSpec((block, size), lambda i: (i, 0))
    chunks = (count // 2, width // count, half)
    return pl.pallas_call(
        combine_kernel,
        grid=(2,),
        in_specs=[smem_spec(), rows]
        + [full_spec((block, width))] * 8
        + [rows]
        + [full_spec(x.shape) for x in (kinds, gain, router, w_mine)]
        + [pl.BlockSpec((block, half), lambda i: (i, 0))],
        out_specs=[rows, rows, full_spec((8, width)), narrow, narrow, full_spec(chunks), full_spec(chunks)],
        out_shape=[
            shape_of((tokens, width), NARROW),
            shape_of((tokens, width), WIDE),
            shape_of((8, width), WIDE),
            shape_of((tokens, size), NARROW),
            shape_of((tokens, size), NARROW),
            shape_of(chunks, NARROW),
            shape_of(chunks, NARROW),
        ],
        scratch_shapes=[VMEM((width, half), WIDE), VMEM((tokens, 1), WIDE)],
        compiler_params=params(),
        cost_estimate=cost(0.1),
        name="combine",
    )(place, later(hidden, after), *outs, *backs, grad, kinds, gain, router, w_mine, att)


def project_back_kernel(place, g, w_all, keep_own, keep_other, send_own, send_other, back_all):
    block = g.shape[0] // 4
    back = dot_nt(g[...], w_all[...]).astype(NARROW)
    for i in range(4):
        at = (i % 2) * 2 * block + (i // 2) * block
        back_all[at : at + block] = back[i * block : (i + 1) * block]
    store_quarters(place[1], back_all, (keep_own, keep_other), (send_own, send_other))


def project_back(place, g, w_all, after):
    seq, cols = g.shape
    width = w_all.shape[0]
    vmem = pl.BlockSpec(memory_space=VMEM)
    quarter = shape_of((seq // 4, width), NARROW)
    return pl.pallas_call(
        project_back_kernel,
        in_specs=[smem_spec()] + [vmem] * 2,
        out_specs=[vmem] * 4,
        out_shape=[quarter] * 4,
        scratch_shapes=[VMEM((seq, width), NARROW)],
        compiler_params=params(16),
        cost_estimate=cost(0.2),
        name="project_back",
    )(place, later(g, after), w_all)


def project_grad_kernel(place, g, normed, w_all, gain, sums, table, keep, send):
    width = normed.shape[1]
    wide = g.shape[1] // 3
    per_row = width // (4 * keep.shape[0])
    grads = dot_tn(normed[...], g[...])
    store_chunks(place, 0, grads[:, : 2 * wide], keep, send, slice(0, 2 * wide))
    gain_grad = jnp.sum(grads * w_all[...].astype(WIDE), axis=1, keepdims=True)
    line = lax.broadcasted_iota(jnp.int32, (128, width), 0)
    lines = jnp.where(line == 0, 1.0 / gain[...].astype(WIDE), 0.0)
    for e in range(TABLE_LANE - 1):
        lines = lines + jnp.where(line == 1 + e, sums[e : e + 1], 0.0)
    lane = lax.broadcasted_iota(jnp.int32, (width, 128), 1)
    turned = lines.T
    turned = turned * jnp.where(lane == 0, gain_grad, 1.0)
    gap = jnp.zeros((per_row - NBUCKET, 128), WIDE)
    tables = jnp.concatenate([table[...], gap] * (width // per_row), axis=0)
    store_chunks(place, 0, turned + tables, keep, send, slice(2 * wide, 2 * wide + 128))
    store_chunks(place, 0, grads[:, 2 * wide :], keep, send, slice(2 * wide + 128, 3 * wide + 128))


def project_grad(place, g, normed, w_all, gain, sums, table, count, after):
    seq, width = normed.shape
    wide = g.shape[1] // 3
    args = (place, g, normed, w_all, gain, sums, later(table, after))
    chunks = (count // 2, width // count)
    vmem = pl.BlockSpec(memory_space=VMEM)
    shape = shape_of((*chunks, 3 * wide + 128), NARROW)
    return pl.pallas_call(
        project_grad_kernel,
        in_specs=[smem_spec()] + [vmem] * 6,
        out_specs=[vmem] * 2,
        out_shape=[shape] * 2,
        compiler_params=params(20),
        cost_estimate=cost(0.2),
        name="project_grad",
    )(*args)


def finish_kernel(place, tok, gain, grad_hidden, mine, far, row, row_far, out):
    col = place[1]
    block = mine.shape[0]
    gain_wide = gain[...].astype(WIDE)
    for half in range(2):
        part = pl.ds(half * block, block)
        grad_normed = jnp.where(col == half, mine[...].astype(WIDE) + row[...].astype(WIDE), far[...].astype(WIDE) + row_far[...].astype(WIDE))
        rows = tok[part, :].astype(WIDE)
        inverse = lax.rsqrt(jnp.mean(rows * rows, axis=-1, keepdims=True) + EPS)
        u = grad_normed * gain_wide
        out[part, :] = grad_hidden[part, :] + inverse * u - rows * (inverse * inverse * inverse) * jnp.mean(u * rows, axis=-1, keepdims=True)


def finish(place, tok, gain, grad_hidden, *sums):
    args = (place, tok, gain, grad_hidden, *sums)
    return pl.pallas_call(
        finish_kernel,
        in_specs=[smem_spec()] + [pl.BlockSpec(memory_space=VMEM)] * (len(args) - 1),
        out_specs=pl.BlockSpec(memory_space=VMEM),
        out_shape=shape_of(tok.shape, WIDE),
        compiler_params=params(16),
        cost_estimate=cost(0.1),
        name="finish",
    )(*args)


def assemble_kernel(place, part, got, grad_q, grad_k, grad_v, grad_o, grad_router, grad_table, lines):
    row = place[0]
    wide = grad_q.shape[1] // 2
    rows = got.shape[0]
    mine = part[...].astype(WIDE)
    theirs = got[...].astype(WIDE)
    extra = 2 * wide
    late = extra + 128
    last = late + wide
    heads = grad_table.shape[1] // 2
    grad_o[...] = mine[:, last:] + theirs[:, last:]
    small = mine[:, extra:late] + theirs[:, extra:late]
    grad_router[...] = small[:, 2:4]
    lines[...] = jnp.concatenate([small, jnp.zeros((128 - rows, 128), WIDE)], axis=0).T[: lines.shape[0], :]
    at = extra + TABLE_LANE

    @pl.when(row == 0)
    def _():
        for out, lo in ((grad_q, 0), (grad_k, wide), (grad_v, late)):
            out[...] = jnp.concatenate([mine[:, lo : lo + wide], theirs[:, lo : lo + wide]], axis=1)
        grad_table[...] = jnp.concatenate([mine[:NBUCKET, at : at + heads], theirs[:NBUCKET, at : at + heads]], axis=1)

    @pl.when(row == 1)
    def _():
        for out, lo in ((grad_q, 0), (grad_k, wide), (grad_v, late)):
            out[...] = jnp.concatenate([theirs[:, lo : lo + wide], mine[:, lo : lo + wide]], axis=1)
        grad_table[...] = jnp.concatenate([theirs[:NBUCKET, at : at + heads], mine[:NBUCKET, at : at + heads]], axis=1)


def assemble(place, part, got, wide, heads, count):
    rows = got.shape[0]
    vmem = pl.BlockSpec(memory_space=VMEM)
    return pl.pallas_call(
        assemble_kernel,
        in_specs=[smem_spec()] + [vmem] * 2,
        out_specs=[vmem] * 7,
        out_shape=[shape_of((rows, 2 * wide), WIDE)] * 4
        + [shape_of((rows, count), WIDE), shape_of((NBUCKET, 2 * heads), WIDE), shape_of((8, 128), WIDE)],
        compiler_params=params(10),
        cost_estimate=cost(1.4),
        name="assemble",
    )(place, part, got)


def swap(value, axis, flip=1):
    size = lax.axis_size(axis)
    return lax.ppermute(value, axis, [(i, i ^ flip) for i in range(size)])


def pick(value, index, axis=0):
    return lax.dynamic_index_in_dim(value, index, axis, keepdims=False)


def in_order(first, mine, got, axis=0):
    return jnp.where(first, jnp.concatenate([mine, got], axis), jnp.concatenate([got, mine], axis))


def halve_kernel(bit, place, kept, got, keep, send):
    mine = (place[2] >> bit) & 1
    low = (1 << bit) - 1
    for j in range(kept.shape[0]):
        at = ((j >> (bit + 1)) << bit) | (j & low)
        chunk = (kept[j].astype(WIDE) + got[j].astype(WIDE)).astype(NARROW)

        @pl.when(mine == (j >> bit) & 1)
        def _():
            keep[at] = chunk

        @pl.when(mine != (j >> bit) & 1)
        def _():
            send[at] = chunk


def halve(place, kept, got, bit, at, after, micros=0.1):
    n, rows, lanes = kept.shape
    shape = shape_of((n // 2, rows, lanes), NARROW)
    vmem = pl.BlockSpec(memory_space=VMEM)

    def kernel(place, *refs):
        shifted = [None, None, place[2] >> (at - bit) if at > bit else place[2]]
        halve_kernel(bit, shifted, *refs)

    return pl.pallas_call(
        kernel,
        in_specs=[smem_spec()] + [vmem] * 2,
        out_specs=[vmem] * 2,
        out_shape=[shape] * 2,
        compiler_params=params(10),
        cost_estimate=cost(micros),
        name="halve",
    )(place, later(kept, after), got)


def halve_two_kernel(at, place, kept, got, kept_next, got_next, keep, send):
    mine = (place[2] >> at) & 1
    lanes = kept.shape[2]
    for first, second, part in ((kept, got, slice(0, lanes)), (kept_next, got_next, slice(lanes, keep.shape[2]))):
        for j in range(2):
            chunk = (first[j].astype(WIDE) + second[j].astype(WIDE)).astype(NARROW)

            @pl.when(mine == j)
            def _():
                keep[0, :, part] = chunk

            @pl.when(mine != j)
            def _():
                send[0, :, part] = chunk


def halve_two(place, kept, got, kept_next, got_next, at, after):
    _, rows, lanes = kept.shape
    shape = shape_of((1, rows, lanes + kept_next.shape[2]), NARROW)
    vmem = pl.BlockSpec(memory_space=VMEM)
    return pl.pallas_call(
        functools.partial(halve_two_kernel, at),
        in_specs=[smem_spec()] + [vmem] * 4,
        out_specs=[vmem] * 2,
        out_shape=[shape] * 2,
        compiler_params=params(10),
        cost_estimate=cost(0.1),
        name="halve_two",
    )(place, later(kept, after), got, kept_next, got_next)


def add_pieces_kernel(kept, got, kept_next, got_next, kept_last, got_last, first, second, beside):
    head = kept.shape[2]
    half = second.shape[1] // 2
    first[:, :head] = kept[0].astype(WIDE) + got[0].astype(WIDE)
    total = kept_next[0].astype(WIDE) + got_next[0].astype(WIDE)
    first[:, head:] = total[:, half:]
    second[:, :half] = total[:, :half]
    rest = kept_last[0].astype(WIDE) + got_last[0].astype(WIDE)
    second[:, half:] = rest[:, :half]
    beside[...] = rest[:, half:].astype(NARROW)


def add_pieces(pieces, units, after):
    vmem = pl.BlockSpec(memory_space=VMEM)
    rows = pieces[0][0].shape[1]
    rest = pieces[2][0].shape[2] - units // 2
    first, *others = [x for pair in pieces for x in pair]
    return pl.pallas_call(
        add_pieces_kernel,
        in_specs=[vmem] * 6,
        out_specs=[vmem] * 3,
        out_shape=[shape_of((rows, units), WIDE)] * 2 + [shape_of((rows, rest), NARROW)],
        compiler_params=params(10),
        cost_estimate=cost(0.1),
        name="add_pieces",
    )(later(first, after), *others)


def part_kernel(place, kept, got, beside, mine, send):
    rows = mine.shape[0]
    values = (
        (kept[0].astype(WIDE) + got[0].astype(WIDE)).astype(NARROW),
        beside[...],
    )
    at = 0
    for value in values:
        lanes = slice(at, at + value.shape[1])
        at += value.shape[1]

        @pl.when(place[0] == 0)
        def _():
            mine[:, lanes] = value[:rows]
            send[:, lanes] = value[rows:]

        @pl.when(place[0] == 1)
        def _():
            mine[:, lanes] = value[rows:]
            send[:, lanes] = value[:rows]


def parts_by_row(place, kept, got, beside):
    vmem = pl.BlockSpec(memory_space=VMEM)
    shape = shape_of((kept.shape[1] // 2, kept.shape[2] + beside.shape[1]), NARROW)
    return pl.pallas_call(
        part_kernel,
        in_specs=[smem_spec()] + [vmem] * 3,
        out_specs=[vmem] * 2,
        out_shape=[shape, shape],
        compiler_params=params(10),
        cost_estimate=cost(1),
        name="parts_by_row",
    )(place, kept, got, beside)


def add_low_kernel(keep, got, out):
    out[...] = (keep[...].astype(WIDE) + got[...].astype(WIDE)).astype(NARROW)


def add_low(keep, got, after):
    vmem = pl.BlockSpec(memory_space=VMEM)
    return pl.pallas_call(
        add_low_kernel,
        in_specs=[vmem] * 2,
        out_specs=vmem,
        out_shape=shape_of(keep.shape, NARROW),
        compiler_params=params(10),
        cost_estimate=cost(0.1),
        name="add_low",
    )(later(keep, after), got)


def along(send, bit):
    return swap(send, "dp", 1 << bit)


def local_pair(tokens, grad_out, routes, norm1_gain, w_query, w_key, w_value, w_output, rel_table, rel_bucket, norm2_gain, router, w_in, w_out):
    tok_rows, width = tokens.shape
    seq = 2 * tok_rows
    row, col = lax.axis_index("row"), lax.axis_index("col")
    count = lax.axis_size("dp")
    bits = count.bit_length() - 1
    place = jnp.stack([row, col, lax.axis_index("dp")]).astype(jnp.int32)
    col_heads = H // lax.axis_size("col")
    heads = col_heads // 2
    size = w_query.shape[1] // col_heads
    wide = heads * size

    w_own, w_send = pack(place, w_query, w_key, w_value)
    w_got = swap(w_send, "row")
    table = lax.dynamic_slice_in_dim(rel_table.astype(WIDE), col * col_heads + row * heads, heads, 1)
    bucket = jnp.pad(rel_bucket[None, :], ((0, 0), (1, 0)), constant_values=-1)
    skew = skewed_bias(bucket, table, w_send)
    tok_half = half_of(place, tokens, w_send)
    tok_got = swap(tok_half, "row")
    w_far = swap(w_got, "dp", 1)
    tok_got = later(tok_got, w_far, skew)
    tok_col = swap(tok_got, "col")
    gain_one, gain_two = norm1_gain[None, :], norm2_gain[None, :]
    router_lines = router.astype(WIDE).T

    tok_all, normed, q, k, v, w_all = project(place, (tokens, tok_got, tok_col), gain_one, (w_own, w_got, w_far), heads, size)

    kinds = routes.astype(WIDE).reshape(-1, 128)
    kinds_got = swap(later(kinds, w_send), "row")
    wo_got = swap(later(w_output, tok_half), "row")
    grad_half = half_of(place, grad_out, tok_half)
    grad_got = swap(grad_half, "row")

    att, shares = attend(place, skew, later(q, wo_got, grad_half), k, v, 256, 0, seq)
    grad_got = later(grad_got, att)
    grad_col = swap(grad_got, "col")
    kinds_got, wo_got, _ = lax.optimization_barrier((kinds_got, wo_got, att))
    kinds_all = jnp.concatenate([kinds, kinds_got], 0)
    w_mine = in_order(row == 0, w_output, wo_got)
    w_other = swap(w_mine, "col")
    att_row = swap(att, "row")
    att_col = swap(att, "col")
    att_row = later(att_row, w_mine, kinds_all, gain_two, router_lines)
    pieces = (att, att_row, att_col, swap(att_row, "col"))
    hidden, att_own, rows, scale = hidden_rows(place, pieces, w_mine, w_other, tok_all, gain_two, router_lines, kinds_all)

    weight_in, weight_out = w_in[0], w_out[0]
    act, slope, out_own, out_other, out_own_send, out_other_send = expert_forward(place, rows, weight_in, weight_out, 512)
    out_other_col = swap(later(out_other_send, grad_col), "col")
    grads = scale_grads(place, grad_out, grad_got, grad_col, scale)
    units = act.shape[1]
    third = units // 3
    keep_o, send_o, keep_p, send_p = weight_grad(place, grads, act, (0, 1), third, count, grads)
    got_o, got_p = along(send_o, 0), along(send_p, 1)
    out_other = add_low(out_other, out_other_col, keep_o)
    out_row = swap(out_other, "row")
    out_own_col = swap(out_own_send, "col")
    grad_pre, rows_own, rows_other, rows_own_send, rows_other_send = expert_backward(
        place, grads, slope, weight_in, weight_out, 512, out_other, keep_o
    )
    out_row = later(out_row, rows_own)
    rows_other_col = swap(later(rows_other_send, out_row), "col")
    rows_other = add_low(later(rows_other, got_o, got_p), rows_other_col, rows_own)
    rows_row = swap(rows_other, "row")
    rows_own_col = swap(rows_own_send, "col")
    keep_o, send_o = halve(place, keep_o, got_o, 0, 1, rows_other)
    got_o = along(send_o, 1)
    keep_p, send_p = halve(place, keep_p, got_p, 0, 0, keep_o)
    got_p = along(send_p, 0)
    keep_i, send_i, keep_j, send_j, keep_q, send_q = weight_grads(place, rows, grad_pre, grads, act, 2 * third, count, keep_p)
    got_i = along(later(send_i, got_p), 0)
    got_q = along(send_q, 1)
    out_mine = add_low(out_own, out_own_col, keep_i)
    outs = (out_mine, swap(out_mine, "col"), out_row, swap(out_row, "col"))
    rows_mine = add_low(rows_own, rows_own_col, keep_i)
    rows_row = later(rows_row, rows_mine, out_mine, got_o, got_p)
    backs = (rows_mine, swap(rows_mine, "col"), rows_row, swap(rows_row, "col"))

    output, grad_hidden, sums, back_own, back_send, wo_keep, wo_send = combine(
        place, hidden, outs, backs, grad_out, kinds, gain_two, router_lines, w_mine, att_own, wide, count, keep_i
    )
    back_oth = swap(back_send, "row")
    keep_j, send_j = jnp.concatenate([keep_j, wo_keep], 2), jnp.concatenate([send_j, wo_send], 2)
    keep_o, send_o = halve_two(place, keep_o, got_o, keep_p, got_p, 2, send_j)
    got_o = along(send_o, 2)
    keep_q, send_q = halve(place, keep_q, got_q, 0, 0, keep_o)
    got_q = along(send_q, 0)
    got_j = along(later(send_j, send_q), 0)
    keep = attend_back(place, bucket, q, k, v, shares, later(back_own, keep_q), 256, 0, None)
    keep_i, send_i = halve(place, later(keep_i, got_o), got_i, 0, 1, keep[0])
    got_i = along(send_i, 1)
    g, table_part = attend_back(place, bucket, q, k, v, shares, back_oth, 256, tok_rows, keep, keep_i)
    keep_i, send_i = halve_two(place, keep_i, got_i, keep_q, got_q, 2, g)
    got_i = along(send_i, 2)

    keep_f, send_f = project_grad(place, g, normed, w_all, gain_one, sums, table_part, count, keep_i)
    got_f = along(send_f, 0)
    normed_own, normed_other, normed_own_send, normed_other_send = project_back(place, g, w_all, keep_f)
    normed_other_col = swap(normed_other_send, "col")
    keep_j, send_j = halve(place, later(keep_j, got_i), got_j, 0, 1, normed_own, 12)
    got_j = along(send_j, 1)
    normed_other = add_low(normed_other, normed_other_col, keep_j)
    normed_row = swap(normed_other, "row")
    normed_own_col = swap(normed_own_send, "col")
    keep_f, send_f = halve(place, keep_f, got_f, 0, 1, normed_other)
    got_f = along(send_f, 1)
    normed_mine = add_low(normed_own, normed_own_col, keep_f)
    normed_far = swap(normed_mine, "col")
    keep_j, send_j = halve(place, keep_j, got_j, 0, 2, normed_mine)
    got_j = along(send_j, 2)
    normed_row = later(normed_row, keep_j)
    normed_row_far = swap(normed_row, "col")
    keep_f, send_f = halve(place, keep_f, got_f, 0, 2, normed_row)
    got_f = along(send_f, 2)
    grad_tokens = finish(place, tokens, gain_one, later(grad_hidden, keep_f), normed_mine, normed_far, normed_row, normed_row_far)
    grad_out_part, grad_in_part, part_wo = add_pieces(((keep_o, got_o), (keep_i, got_i), (keep_j, got_j)), units, grad_tokens)
    mine, send = parts_by_row(place, keep_f, later(got_f, grad_in_part), part_wo)
    per_row = mine.shape[0]
    got = swap(send, "row")
    grad_q, grad_k, grad_v, grad_o, grad_router, grad_table, lines = assemble(place, mine, got, wide, heads, router.shape[1])
    lines = lines[:, :per_row]
    return (
        output,
        grad_tokens,
        (lines + swap(lines, "col"))[0],
        grad_q,
        grad_k,
        grad_v,
        grad_o,
        grad_table,
        lines[1],
        grad_router,
        grad_in_part[None],
        grad_out_part[None],
    )


def solution(mesh):
    in_specs = (
        P(("dp", "row"), None),
        P(("dp", "row"), None),
        P(("dp", "row"), None),
        P(),
        P("row", "col"),
        P("row", "col"),
        P("row", "col"),
        P("row", "col"),
        P(),
        P(),
        P(),
        P(),
        P("row", None, "col"),
        P("row", None, "col"),
    )
    out_specs = (
        P(("dp", "row"), None),
        P(("dp", "row"), None),
        P(("dp", "row")),
        P(("dp", "row"), "col"),
        P(("dp", "row"), "col"),
        P(("dp", "row"), "col"),
        P(("dp", "row"), "col"),
        P(None, "col"),
        P(("dp", "row")),
        P(("dp", "row"), None),
        P("row", "dp", "col"),
        P("row", "dp", "col"),
    )
    paired = mesh.shape["row"] == 2 and mesh.shape["col"] == 2 and mesh.shape["dp"] == 8
    return jax.shard_map(local_pair if paired else local, mesh=mesh, in_specs=in_specs, out_specs=out_specs, check_vma=False)
```

```python
import functools

import jax
import jax.numpy as jnp
from jax import lax
from jax.experimental import pallas as pl
from jax.experimental.pallas import tpu as pltpu
from jax.sharding import PartitionSpec as P

H = 12
NBUCKET = 32


EPS = 1e-06
SCALE = 0.125
HIGHEST = lax.Precision.HIGHEST
NARROW = jnp.bfloat16
WIDE = jnp.float32


def gelu_tanh(values):
    return jax.nn.gelu(values, approximate=True)


def norm_forward(rows, gain):
    inverse = lax.rsqrt(jnp.mean(rows * rows, axis=-1, keepdims=True) + EPS)
    return (rows * inverse * gain, inverse)


def norm_backward(rows, inverse, gain, grad_normed):
    scaled = grad_normed * gain
    grad_rows = inverse * scaled - rows * inverse**3 * jnp.mean(
        scaled * rows, axis=-1, keepdims=True
    )
    return (grad_rows, jnp.sum(grad_normed * rows * inverse, axis=0))


def contract_rows(left, right):
    return lax.dot_general(left, right, (((0,), (0,)), ((), ())), preferred_element_type=WIDE)


def contract_cols(left, right):
    return lax.dot_general(left, right, (((1,), (1,)), ((), ())), preferred_element_type=WIDE)


def split_heads(matrix, heads):
    return matrix.reshape(matrix.shape[0], heads, -1).transpose(1, 0, 2)


def join_heads(stacked):
    return stacked.transpose(1, 0, 2).reshape(stacked.shape[1], -1)


def diagonal_sums(block):
    heads, height, breadth = block.shape
    shifted = jnp.pad(block, ((0, 0), (0, 0), (height, 0))).reshape(
        heads, height * (height + breadth)
    )
    shifted = jnp.pad(shifted, ((0, 0), (0, height))).reshape(heads, height, height + breadth + 1)
    totals = jnp.sum(shifted, axis=1, dtype=WIDE)
    return totals[:, 1 : height + breadth]


def bias_block(offsets, query_start, key_start, queries, keys, seq_len):
    heads = offsets.shape[0]
    begin = key_start - query_start + seq_len - queries
    window = lax.dynamic_slice_in_dim(offsets, begin, queries + keys - 1, 1)
    period = queries + keys
    padded = jnp.pad(window, ((0, 0), (0, 1)))
    spread = jnp.broadcast_to(padded[:, None, :], (heads, queries, period)).reshape(
        heads, queries * period
    )
    skewed = spread[:, : queries * (period - 1)].reshape(heads, queries, period - 1)
    return skewed[:, :, queries - 1 : queries - 1 + keys]


def batch_scores(query_heads, key_heads, bias):
    return (
        SCALE * jnp.einsum("hqd,hkd->hqk", query_heads, key_heads, preferred_element_type=WIDE)
        + bias
    )


def local(
    tokens,
    grad_out,
    routes,
    norm1_gain,
    w_query,
    w_key,
    w_value,
    w_output,
    rel_table,
    rel_bucket,
    norm2_gain,
    router,
    w_in,
    w_out,
):
    tok_rows, width = tokens.shape
    seq_len = tok_rows * lax.axis_size("row")
    heads = H // lax.axis_size("col")
    row_start = lax.axis_index("row") * tok_rows
    tokens_wide = tokens.astype(WIDE)
    gain_one = norm1_gain.astype(WIDE)
    normed, inverse_one = norm_forward(tokens_wide, gain_one)
    normed_low = normed.astype(NARROW)
    query_weight, key_weight, value_weight, output_weight = (
        lax.all_gather(w_query, "row", axis=0, tiled=True),
        lax.all_gather(w_key, "row", axis=0, tiled=True),
        lax.all_gather(w_value, "row", axis=0, tiled=True),
        lax.all_gather(w_output, "row", axis=0, tiled=True),
    )
    query = jnp.dot(normed_low, query_weight, preferred_element_type=WIDE).astype(NARROW)
    key = jnp.dot(normed_low, key_weight, preferred_element_type=WIDE).astype(NARROW)
    value = jnp.dot(normed_low, value_weight, preferred_element_type=WIDE).astype(NARROW)
    keys_all, values_all = (
        lax.all_gather(key, "row", axis=0, tiled=True),
        lax.all_gather(value, "row", axis=0, tiled=True),
    )
    bucket_hot = (rel_bucket[None, :] == jnp.arange(NBUCKET, dtype=jnp.int32)[:, None]).astype(WIDE)
    table_local = lax.dynamic_slice_in_dim(
        rel_table.astype(WIDE), lax.axis_index("col") * heads, heads, 1
    )
    offsets = jnp.dot(table_local.T, bucket_hot, precision=HIGHEST)
    bias = bias_block(offsets, row_start, 0, tok_rows, seq_len, seq_len)
    query_heads = split_heads(query, heads)
    key_heads = split_heads(keys_all, heads)
    value_heads = split_heads(values_all, heads)
    scores = batch_scores(query_heads, key_heads, bias)
    ceiling = jnp.max(scores, axis=2, keepdims=True)
    raised = jnp.exp(scores - ceiling)
    summed = jnp.sum(raised, axis=2, keepdims=True)
    attended_heads = jnp.einsum(
        "hqk,hkd->hqd", (raised / summed).astype(NARROW), value_heads, preferred_element_type=WIDE
    )
    log_total = ceiling[:, :, 0] + jnp.log(summed[:, :, 0])
    attended = join_heads(attended_heads).astype(NARROW)
    branch = lax.psum(contract_cols(attended, output_weight), "col")
    hidden = tokens_wide + branch
    gain_two = norm2_gain.astype(WIDE)
    hn, inverse_two = norm_forward(hidden, gain_two)
    router_wide = router.astype(WIDE)
    gate_probs = jax.nn.softmax(jnp.dot(hn, router_wide, precision=HIGHEST), axis=-1)
    n_exp = router.shape[1]
    capacity = 2 * tok_rows // n_exp
    expert_ids = routes[:, 0]
    one_hot_int = (expert_ids[:, None] == jnp.arange(n_exp, dtype=jnp.int32)[None, :]).astype(
        jnp.int32
    )
    one_hot = one_hot_int.astype(WIDE)
    gate = jnp.sum(gate_probs * one_hot, axis=1)
    rank_own = jnp.sum((jnp.cumsum(one_hot_int, axis=0) - 1) * one_hot_int, axis=1)
    slot_ids = expert_ids * capacity + rank_own
    grad_wide = grad_out.astype(WIDE)
    send_rows = hn.astype(NARROW)
    send_grads = (gate[:, None] * grad_wide).astype(NARROW)
    box_rows = (
        jnp.zeros((n_exp * capacity, width), NARROW)
        .at[slot_ids]
        .set(send_rows)
        .reshape(n_exp, capacity, width)
    )
    box_grads = (
        jnp.zeros((n_exp * capacity, width), NARROW)
        .at[slot_ids]
        .set(send_grads)
        .reshape(n_exp, capacity, width)
    )
    got_rows, got_grads = (
        lax.all_to_all(box_rows, "row", split_axis=0, concat_axis=0, tiled=True),
        lax.all_to_all(box_grads, "row", split_axis=0, concat_axis=0, tiled=True),
    )
    expert_in = got_rows.reshape(-1, width)
    expert_grad = got_grads.reshape(-1, width)
    weight_in = w_in[0]
    weight_out = w_out[0]
    pre = jnp.dot(expert_in, weight_in, preferred_element_type=WIDE)
    act, act_back = jax.vjp(gelu_tanh, pre)
    act_low = act.astype(NARROW)
    out_part = contract_cols(act_low, weight_out)
    grad_act = jnp.dot(expert_grad, weight_out, preferred_element_type=WIDE)
    grad_pre = act_back(grad_act)[0].astype(NARROW)
    rows_part = contract_cols(grad_pre, weight_in)
    grad_weight_in = contract_rows(expert_in, grad_pre)
    grad_weight_out = contract_rows(expert_grad, act_low)
    out_sum, rows_sum = lax.psum((out_part, rows_part), "col")
    back_out, back_rows = (
        lax.all_to_all(
            out_sum.astype(NARROW).reshape(n_exp, capacity, width),
            "row",
            split_axis=0,
            concat_axis=0,
            tiled=True,
        ),
        lax.all_to_all(
            rows_sum.astype(NARROW).reshape(n_exp, capacity, width),
            "row",
            split_axis=0,
            concat_axis=0,
            tiled=True,
        ),
    )
    expert_out = back_out.reshape(-1, width)[slot_ids].astype(WIDE)
    grad_rows = back_rows.reshape(-1, width)[slot_ids].astype(WIDE)
    output = (hidden + gate[:, None] * expert_out).astype(NARROW)
    grad_in_shard, grad_out_shard = (
        lax.psum_scatter(
            grad_weight_in.astype(jnp.bfloat16), "dp", scatter_dimension=0, tiled=True
        ).astype(jnp.float32),
        lax.psum_scatter(
            grad_weight_out.astype(jnp.bfloat16), "dp", scatter_dimension=0, tiled=True
        ).astype(jnp.float32),
    )
    grad_gate = jnp.sum(grad_wide * expert_out, axis=1)
    grad_logits = (grad_gate * gate)[:, None] * (one_hot - gate_probs)
    grad_router = jnp.dot(hn.T, grad_logits, precision=HIGHEST)
    grad_hn = grad_rows + jnp.dot(grad_logits, router_wide.T, precision=HIGHEST)
    grad_hidden_norm, grad_gain_two = norm_backward(hidden, inverse_two, gain_two, grad_hn)
    grad_hidden = grad_wide + grad_hidden_norm
    grad_branch = grad_hidden.astype(NARROW)
    grad_w_output = contract_rows(grad_branch, attended)
    grad_attended = jnp.dot(grad_branch, output_weight, preferred_element_type=WIDE).astype(NARROW)
    grad_heads = split_heads(grad_attended, heads)
    diagonal_start = seq_len - row_start - tok_rows
    shares = jnp.exp(batch_scores(query_heads, key_heads, bias) - log_total[:, :, None])
    grad_shares = jnp.einsum("hqd,hkd->hqk", grad_heads, value_heads, preferred_element_type=WIDE)
    deltas = jnp.sum(shares * grad_shares, axis=2)
    grad_scores = (shares * (grad_shares - deltas[:, :, None])).astype(NARROW)
    grad_query_heads = SCALE * jnp.einsum(
        "hqk,hkd->hqd", grad_scores, key_heads, preferred_element_type=WIDE
    )
    diagonals = diagonal_sums(grad_scores)
    bucket_window = lax.dynamic_slice_in_dim(bucket_hot, diagonal_start, tok_rows + seq_len - 1, 1)
    table_part = jnp.dot(bucket_window, diagonals.T, precision=HIGHEST)
    grad_key_heads = SCALE * jnp.einsum(
        "hqk,hqd->hkd", grad_scores, query_heads, preferred_element_type=WIDE
    )
    grad_value_heads = jnp.einsum(
        "hqk,hqd->hkd", shares.astype(NARROW), grad_heads, preferred_element_type=WIDE
    )
    grad_key, grad_value = (
        lax.psum_scatter(
            join_heads(grad_key_heads).astype(jnp.bfloat16), "row", scatter_dimension=0, tiled=True
        ).astype(jnp.float32),
        lax.psum_scatter(
            join_heads(grad_value_heads).astype(jnp.bfloat16),
            "row",
            scatter_dimension=0,
            tiled=True,
        ).astype(jnp.float32),
    )
    grad_query = join_heads(grad_query_heads).astype(NARROW)
    grad_key_low = grad_key.astype(NARROW)
    grad_value_low = grad_value.astype(NARROW)
    grad_w_query = contract_rows(normed_low, grad_query)
    grad_w_key = contract_rows(normed_low, grad_key_low)
    grad_w_value = contract_rows(normed_low, grad_value_low)
    normed_part = (
        contract_cols(grad_query, query_weight)
        + contract_cols(grad_key_low, key_weight)
        + contract_cols(grad_value_low, value_weight)
    )
    grad_normed = lax.psum(normed_part.astype(jnp.bfloat16), "col").astype(jnp.float32)
    grad_tokens_norm, grad_gain_one = norm_backward(tokens_wide, inverse_one, gain_one, grad_normed)
    grad_tokens = grad_hidden + grad_tokens_norm
    grad_table = lax.psum(table_part, ("dp", "row"))
    (
        grads_query,
        grads_key,
        grads_value,
        grads_output,
        grads_gain_one,
        grads_gain_two,
        grads_router,
    ) = (
        lax.psum_scatter(grad_w_query, ("dp", "row"), scatter_dimension=0, tiled=True),
        lax.psum_scatter(grad_w_key, ("dp", "row"), scatter_dimension=0, tiled=True),
        lax.psum_scatter(grad_w_value, ("dp", "row"), scatter_dimension=0, tiled=True),
        lax.psum_scatter(grad_w_output, ("dp", "row"), scatter_dimension=0, tiled=True),
        lax.psum_scatter(grad_gain_one, ("dp", "row"), scatter_dimension=0, tiled=True),
        lax.psum_scatter(grad_gain_two, ("dp", "row"), scatter_dimension=0, tiled=True),
        lax.psum_scatter(grad_router, ("dp", "row"), scatter_dimension=0, tiled=True),
    )
    return (
        output,
        grad_tokens,
        grads_gain_one,
        grads_query,
        grads_key,
        grads_value,
        grads_output,
        grad_table,
        grads_gain_two,
        grads_router,
        grad_in_shard[None],
        grad_out_shard[None],
    )


VMEM = pltpu.VMEM
SMEM = pltpu.SMEM


def dot_nn(a, b):
    return lax.dot_general(a, b, (((1,), (0,)), ((), ())), preferred_element_type=WIDE)


def dot_nt(a, b):
    return lax.dot_general(a, b, (((1,), (1,)), ((), ())), preferred_element_type=WIDE)


def dot_tn(a, b):
    return lax.dot_general(a, b, (((0,), (0,)), ((), ())), preferred_element_type=WIDE)


def later(value, *others):
    return lax.optimization_barrier((value, *others))[0]


def full_spec(shape):
    return pl.BlockSpec(shape, lambda *_: (0,) * len(shape))


def smem_spec():
    return pl.BlockSpec(memory_space=SMEM)


def params(megabytes=28):
    return pltpu.CompilerParams(vmem_limit_bytes=megabytes * 1024 * 1024)


def cost(micros):
    return pl.CostEstimate(flops=int(micros * 575e6), bytes_accessed=0, transcendentals=0)


def shape_of(shape, dtype):
    return jax.ShapeDtypeStruct(shape, dtype)


def pack_kernel(place, w_query, w_key, w_value, own, send):
    row, bit = place[0], place[2] & 1
    wide = own.shape[1] // 3
    part = pl.ds(pl.multiple_of(bit * send.shape[0], 16), send.shape[0])
    for i, w in enumerate((w_query, w_key, w_value)):
        lanes = slice(i * wide, (i + 1) * wide)

        @pl.when(row == 0)
        def _():
            own[:, lanes] = w[:, :wide]
            send[:, lanes] = w[part, wide:]

        @pl.when(row == 1)
        def _():
            own[:, lanes] = w[:, wide:]
            send[:, lanes] = w[part, :wide]


def pack(place, w_query, w_key, w_value):
    rows, cols = w_query.shape
    vmem = pl.BlockSpec(memory_space=VMEM)
    return pl.pallas_call(
        pack_kernel,
        in_specs=[smem_spec()] + [vmem] * 3,
        out_specs=[vmem] * 2,
        out_shape=[shape_of((rows, 3 * cols // 2), NARROW), shape_of((rows // 2, 3 * cols // 2), NARROW)],
        compiler_params=params(60),
        cost_estimate=cost(2),
        name="pack",
    )(place, w_query, w_key, w_value)


def half_kernel(place, value, out):
    out[...] = value[...]


def half_of(place, value, after):
    rows, width = value.shape[0] // 2, value.shape[1]
    return pl.pallas_call(
        half_kernel,
        grid_spec=pltpu.PrefetchScalarGridSpec(
            num_scalar_prefetch=1,
            grid=(1,),
            in_specs=[pl.BlockSpec((rows, width), lambda i, place: (place[1], 0))],
            out_specs=pl.BlockSpec((rows, width), lambda i, place: (0, 0)),
        ),
        out_shape=shape_of((rows, width), value.dtype),
        compiler_params=params(10),
        cost_estimate=cost(1),
        name="half_of",
    )(place, later(value, after))


def project_kernel(place, tok_own, tok_got, tok_col, gain, w_own, w_got, w_far, tok, normed, q, k, v, w_all):
    half = w_own.shape[0]
    quarter = w_got.shape[0]
    row, col, bit = place[0], place[1], place[2] & 1
    step = pl.program_id(0)

    @pl.when(step == 0)
    def _():
        base = (1 - row) * half
        w_all[pl.ds(pl.multiple_of(row * half, 16), half)] = w_own[...]
        w_all[pl.ds(pl.multiple_of(base + bit * quarter, 16), quarter)] = w_got[...]
        w_all[pl.ds(pl.multiple_of(base + (1 - bit) * quarter, 16), quarter)] = w_far[...]

    @pl.when(step < 2)
    def _():
        tok[...] = tok_own[...]

    @pl.when(step - 2 == col)
    def _():
        tok[...] = tok_got[...]

    @pl.when(step - 2 == 1 - col)
    def _():
        tok[...] = tok_col[...]

    rows = tok[...].astype(WIDE)
    inverse = lax.rsqrt(jnp.mean(rows * rows, axis=-1, keepdims=True) + EPS)
    low = (rows * inverse * gain[...].astype(WIDE)).astype(NARROW)
    normed[...] = low
    out = dot_nn(low, w_all[...])
    heads, _, size = q.shape
    wide = heads * size
    for h in range(heads):
        q[h] = (out[:, h * size : (h + 1) * size] * SCALE).astype(NARROW)
        k[h] = out[:, wide + h * size : wide + (h + 1) * size].astype(NARROW)
        v[h] = out[:, 2 * wide + h * size : 2 * wide + (h + 1) * size].astype(NARROW)


def project(place, toks, gain, w_parts, heads, size):
    block, width = toks[1].shape
    seq = 4 * block
    cols = w_parts[0].shape[1]
    head_spec = pl.BlockSpec((heads, block, size), lambda i: (0, i, 0))
    row_spec = pl.BlockSpec((block, width), lambda i: (i, 0))
    head_shape = shape_of((heads, seq, size), NARROW)
    return pl.pallas_call(
        project_kernel,
        grid=(4,),
        in_specs=[smem_spec(), pl.BlockSpec((block, width), lambda i: (jnp.minimum(i, 1), 0))]
        + [full_spec(x.shape) for x in (*toks[1:], gain, *w_parts)],
        out_specs=[row_spec, row_spec, head_spec, head_spec, head_spec, full_spec((width, cols))],
        out_shape=[shape_of((seq, width), NARROW)] * 2 + [head_shape] * 3 + [shape_of((width, cols), NARROW)],
        compiler_params=params(28),
        cost_estimate=cost(3.3),
        name="project",
    )(
        place,
        pltpu.with_memory_space_constraint(toks[0], pltpu.HBM),
        *toks[1:],
        gain,
        pltpu.with_memory_space_constraint(w_parts[0], pltpu.HBM),
        *w_parts[1:],
    )


TILE = 128
TABLE_LANE = 4


def bias_lanes(row, block_index, blocks):
    half = blocks // 2
    query = lax.rem(block_index + half * row, blocks)
    own = half * row - query + blocks
    other = half * (1 - row) - query + blocks
    return pl.multiple_of(own * TILE, TILE), pl.multiple_of(other * TILE, TILE)


def skew_kernel(bucket, table, skew):
    n = bucket.shape[1]
    hot = (bucket[...] == lax.broadcasted_iota(jnp.int32, (NBUCKET, n), 0)).astype(WIDE)
    for h in range(skew.shape[0]):
        line = jnp.sum(hot * table[:, h : h + 1], axis=0, keepdims=True)
        skew[h] = pltpu.roll(jnp.broadcast_to(line, (TILE, n)), 0, 1, stride=1, stride_axis=0)


def skewed_bias(bucket, table, after):
    vmem = pl.BlockSpec(memory_space=VMEM)
    return pl.pallas_call(
        skew_kernel,
        in_specs=[vmem] * 2,
        out_specs=vmem,
        out_shape=shape_of((table.shape[1], TILE, bucket.shape[1]), WIDE),
        compiler_params=params(12),
        cost_estimate=cost(1),
        name="skewed_bias",
    )(bucket, later(table, after))


def attend_kernel(first, place, skew, q, k, v, att, p):
    heads, block, size = q.shape
    seq = k.shape[1]
    half = seq // 2
    row = place[0]
    step = pl.program_id(0)

    for h in range(heads):
        raw = dot_nt(q[h], k[h])
        parts = []
        for sub in range(block // TILE):
            own, other = bias_lanes(row, first + step * (block // TILE) + sub, seq // TILE)
            bias = jnp.concatenate([skew[h, :, pl.ds(own, half)], skew[h, :, pl.ds(other, half)]], axis=1)
            scores = raw[sub * TILE : (sub + 1) * TILE] + bias
            raised = jnp.exp(scores - jnp.max(scores, axis=1, keepdims=True))
            share = raised * (1.0 / jnp.sum(raised, axis=1, keepdims=True))
            parts.append(share.astype(NARROW))
        shares = jnp.concatenate(parts, axis=0)
        p[h] = shares
        att[:, h * size : (h + 1) * size] = dot_nn(shares, v[h]).astype(NARROW)


def attend(place, skew, q, k, v, block, begin, rows):
    heads, seq, size = q.shape
    start = begin // block
    return pl.pallas_call(
        functools.partial(attend_kernel, begin // TILE),
        grid=(rows // block,),
        in_specs=[
            smem_spec(),
            full_spec(skew.shape),
            pl.BlockSpec((heads, block, size), lambda i: (0, i + start, 0)),
            full_spec(k.shape),
            full_spec(v.shape),
        ],
        out_specs=[
            pl.BlockSpec((block, heads * size), lambda i: (i, 0)),
            pl.BlockSpec((heads, block, seq), lambda i: (0, i, 0)),
        ],
        out_shape=[shape_of((rows, heads * size), NARROW), pltpu.HBM((heads, rows, seq), NARROW)],
        compiler_params=params(),
        cost_estimate=cost(9.3),
        name="attend",
    )(place, skew, q, k, v)


def attend_back_kernel(first, last, place, bucket, q, k, v, p, g, *refs):
    if first == 0:
        keep_in = None
    else:
        keep_in, refs = refs[:3], refs[3:]
    if last:
        out, table, key_sum, value_sum, diag = refs
        query_out = None
    else:
        query_out, key_sum, value_sum, diag = refs
        out = None
    heads, block, size = q.shape
    seq = k.shape[1]
    half = seq // 2
    row = place[0]
    step = pl.program_id(0)

    @pl.when(step == 0)
    def _():
        if keep_in is None:
            key_sum[...] = jnp.zeros_like(key_sum)
            value_sum[...] = jnp.zeros_like(value_sum)
            diag[...] = jnp.zeros_like(diag)
        else:
            key_sum[...] = keep_in[0][...]
            value_sum[...] = keep_in[1][...]
            diag[...] = keep_in[2][...]

    wide = heads * size
    for h in range(heads):
        grad = g[:, h * size : (h + 1) * size]
        share_low = p[h]
        share = share_low.astype(WIDE)
        grad_share = dot_nt(grad, v[h])
        delta = jnp.sum(share * grad_share, axis=1, keepdims=True)
        grad_score = share * (grad_share - delta)
        for sub in range(block // TILE):
            own, other = bias_lanes(row, first + step * (block // TILE) + sub, seq // TILE)
            piece = grad_score[sub * TILE : (sub + 1) * TILE]
            diag[h, :, pl.ds(own, half)] += piece[:, :half]
            diag[h, :, pl.ds(other, half)] += piece[:, half:]
        low = grad_score.astype(NARROW)
        grad_query = (SCALE * dot_nn(low, k[h])).astype(NARROW)
        if last:
            out[pl.ds(pl.multiple_of(first * TILE + step * block, block), block), h * size : (h + 1) * size] = grad_query
        else:
            query_out[:, h * size : (h + 1) * size] = grad_query
        key_sum[h] += dot_tn(q[h], low)
        value_sum[h] += dot_tn(grad, share_low)

    if last:
        lanes = diag.shape[2]

        @pl.when(step == pl.num_programs(0) - 1)
        def _():
            hot = (bucket[...] == lax.broadcasted_iota(jnp.int32, (NBUCKET, lanes), 0)).astype(WIDE)
            lane = lax.broadcasted_iota(jnp.int32, table.shape, 1)
            total = jnp.zeros(table.shape, WIDE)
            for h in range(heads):
                lo = h * size
                out[:, wide + lo : wide + lo + size] = key_sum[h].T.astype(NARROW)
                out[:, 2 * wide + lo : 2 * wide + lo + size] = value_sum[h].T.astype(NARROW)
                sums = diag[h]
                height = TILE // 2
                while height >= 8:
                    sums = sums[:height] + pltpu.roll(sums[height:], lanes - height, 1)
                    height //= 2
                where = lax.broadcasted_iota(jnp.int32, sums.shape, 0)
                for bit in (4, 2, 1):
                    sums = jnp.where((where & bit) != 0, pltpu.roll(sums, lanes - bit, 1), sums)
                line = jnp.sum(sums, axis=0, keepdims=True)
                total = total + jnp.where(lane == TABLE_LANE + h, jnp.sum(hot * line, axis=1, keepdims=True), 0.0)
            table[...] = total


def attend_back(place, bucket, q, k, v, p, g, block, begin, keep, after=None):
    heads, seq, size = q.shape
    rows = g.shape[0]
    start = begin // block
    last = keep is not None
    lanes = bucket.shape[1]
    sum_shape = (heads, size, seq)
    diag_shape = (heads, TILE, lanes)
    wide = heads * size
    in_specs = [
        smem_spec(),
        full_spec(bucket.shape),
        pl.BlockSpec((heads, block, size), lambda i: (0, i + start, 0)),
        full_spec(k.shape),
        full_spec(v.shape),
        pl.BlockSpec((heads, block, seq), lambda i: (0, i + start, 0)),
        pl.BlockSpec((block, wide), lambda i: (i, 0)),
    ]
    args = [place, bucket, q, k, v, p, g]
    sums = [shape_of(sum_shape, WIDE), shape_of(sum_shape, WIDE), shape_of(diag_shape, WIDE)]
    if last:
        in_specs += [full_spec(s.shape) for s in sums]
        args += list(keep[1:])
        in_specs += [full_spec(keep[0].shape)]
        args += [keep[0]]
        args[6] = later(g, after)
        out_specs = [full_spec((seq, 3 * wide)), full_spec((NBUCKET, 128))]
        out_shape = [shape_of((seq, 3 * wide), NARROW), shape_of((NBUCKET, 128), WIDE)]
        scratch = [VMEM(s.shape, WIDE) for s in sums]

        def kernel(*refs):
            earlier = refs[10]
            out = refs[11]

            @pl.when(pl.program_id(0) == 0)
            def _():
                out[: earlier.shape[0], :wide] = earlier[...]

            attend_back_kernel(begin // TILE, True, *refs[:10], *refs[11:])

    else:
        out_specs = [pl.BlockSpec((block, wide), lambda i: (i, 0))] + [full_spec(s.shape) for s in sums]
        out_shape = [shape_of((rows, wide), NARROW)] + sums
        scratch = []
        kernel = functools.partial(attend_back_kernel, begin // TILE, False)
    return pl.pallas_call(
        kernel,
        grid=(rows // block,),
        in_specs=in_specs,
        out_specs=out_specs,
        out_shape=out_shape,
        scratch_shapes=scratch,
        compiler_params=params(),
        cost_estimate=cost(12),
        name="attend_back",
    )(*args)


def column(lines):
    count = lines.shape[0]
    wide = jnp.concatenate([lines, jnp.zeros((128 - count, 128), lines.dtype)], axis=0).T
    return jnp.concatenate([wide[:, i : i + 1] for i in range(count)], axis=0)


def gate_values(hn, route, router):
    count = router.shape[0]
    logits = [jnp.sum(hn * router[e : e + 1], axis=1, keepdims=True) for e in range(count)]
    top = functools.reduce(jnp.maximum, logits)
    raised = [jnp.exp(x - top) for x in logits]
    total = functools.reduce(jnp.add, raised)
    probs = [x / total for x in raised]
    hots = [(route == float(e)).astype(WIDE) for e in range(count)]
    gate = functools.reduce(jnp.add, [p * o for p, o in zip(probs, hots)])
    return probs, hots, gate


def hidden_kernel(place, a_mine, a_row, a_col, a_diag, w_mine, w_other, tok, gain, router, kinds, hidden, att, rows, scale, pack, route):
    row = place[0]
    step = pl.program_id(0)
    size = a_mine.shape[1]

    @pl.when(step == 0)
    def _():
        route[...] = column(kinds[...])

    @pl.when(row == 0)
    def _():
        pack[0, :, :size] = a_mine[...]
        pack[0, :, size:] = a_row[...]
        pack[1, :, :size] = a_col[...]
        pack[1, :, size:] = a_diag[...]

    @pl.when(row == 1)
    def _():
        pack[0, :, size:] = a_mine[...]
        pack[0, :, :size] = a_row[...]
        pack[1, :, size:] = a_col[...]
        pack[1, :, :size] = a_diag[...]

    branch = dot_nt(pack[0], w_mine[...]) + dot_nt(pack[1], w_other[...])
    wide = tok[...].astype(WIDE) + branch

    @pl.when(step < 2)
    def _():
        hidden[...] = wide
        att[...] = pack[0]

    inverse = lax.rsqrt(jnp.mean(wide * wide, axis=-1, keepdims=True) + EPS)
    hn = wide * inverse * gain[...].astype(WIDE)
    block = wide.shape[0]
    kind = route[pl.ds(pl.multiple_of(step * block, 16), block), :]
    _, hots, gate = gate_values(hn, kind, router)
    chosen = jnp.where(kind == row.astype(WIDE), 1.0, 0.0)
    rows[...] = (hn * chosen).astype(NARROW)
    scale[...] = gate * chosen


def hidden_rows(place, pieces, w_mine, w_other, tok_all, gain, router, route_all):
    seq, width = tok_all.shape
    block = seq // 4
    size = pieces[0].shape[1]
    half = w_mine.shape[1]
    turned = pl.BlockSpec((block, size), lambda i: (lax.rem(i + 2, 4), 0))
    plain = pl.BlockSpec((block, size), lambda i: (i, 0))
    wide_spec = pl.BlockSpec((block, width), lambda i: (i, 0))
    own_spec = pl.BlockSpec((block, width), lambda i: (jnp.minimum(i, 1), 0))
    mixed = pl.BlockSpec((block, width), lambda i: (lax.rem(i, 2) * 2 + lax.div(i, 2), 0))
    mixed_line = pl.BlockSpec((block, 1), lambda i: (lax.rem(i, 2) * 2 + lax.div(i, 2), 0))
    return pl.pallas_call(
        hidden_kernel,
        grid=(4,),
        in_specs=[
            smem_spec(),
            plain,
            turned,
            plain,
            turned,
            full_spec(w_mine.shape),
            full_spec(w_other.shape),
            wide_spec,
            full_spec(gain.shape),
            full_spec(router.shape),
            full_spec(route_all.shape),
        ],
        out_specs=[own_spec, pl.BlockSpec((block, half), lambda i: (jnp.minimum(i, 1), 0)), mixed, mixed_line],
        out_shape=[
            shape_of((seq // 2, width), WIDE),
            shape_of((seq // 2, half), NARROW),
            shape_of((seq, width), NARROW),
            shape_of((seq, 1), WIDE),
        ],
        scratch_shapes=[VMEM((2, block, half), NARROW), VMEM((seq, 1), WIDE)],
        compiler_params=params(),
        cost_estimate=cost(6),
        name="hidden_rows",
    )(place, *pieces, w_mine, w_other, tok_all, gain, router, route_all)


def scale_kernel(place, own, got, got_col, scale, out):
    col = place[1]
    block = got.shape[0]
    for half in range(2):
        first = pl.ds(2 * half * block, block)
        second = pl.ds((2 * half + 1) * block, block)
        out[first, :] = (own[half * block : (half + 1) * block, :].astype(WIDE) * scale[first, :]).astype(NARROW)
        other = jnp.where(col == half, got[...].astype(WIDE), got_col[...].astype(WIDE))
        out[second, :] = (other * scale[second, :]).astype(NARROW)


def scale_grads(place, own, got, got_col, scale):
    args = (place, own, got, got_col, scale)
    vmem = pl.BlockSpec(memory_space=VMEM)
    return pl.pallas_call(
        scale_kernel,
        in_specs=[smem_spec()] + [vmem] * 4,
        out_specs=vmem,
        out_shape=shape_of((2 * own.shape[0], own.shape[1]), NARROW),
        compiler_params=params(10),
        cost_estimate=cost(1.4),
        name="scale_grads",
    )(*args)


def store_quarters(mine, value, keeps, sends):
    rows = keeps[0].shape[0]
    for part in range(2):
        low = slice(part * rows, (part + 1) * rows)
        high = slice((2 + part) * rows, (3 + part) * rows)

        @pl.when(mine == 0)
        def _():
            keeps[part][...] = value[low].astype(NARROW)
            sends[part][...] = value[high].astype(NARROW)

        @pl.when(mine == 1)
        def _():
            keeps[part][...] = value[high].astype(NARROW)
            sends[part][...] = value[low].astype(NARROW)


def expert_out_kernel(place, x, w_in, w_out, act, slope, keep_own, keep_other, send_own, send_other, total):
    step = pl.program_id(0)
    pre = dot_nn(x[...], w_in[...])
    square = pre * pre
    bent = jnp.tanh(pre * (0.7978845608028654 + (0.7978845608028654 * 0.044715) * square))
    half = 0.5 + 0.5 * bent
    act_low = (pre * half).astype(NARROW)
    act[...] = act_low
    inner = 0.7978845608028654 + (0.7978845608028654 * 0.134145) * square
    slope[...] = (half + (0.5 * pre) * ((1.0 - bent * bent) * inner)).astype(NARROW)
    piece = dot_nt(act_low, w_out[...])

    @pl.when(step == 0)
    def _():
        total[...] = piece

    @pl.when(step > 0)
    def _():
        total[...] += piece

    @pl.when(step == pl.num_programs(0) - 1)
    def _():
        store_quarters(place[1], total, (keep_own, keep_other), (send_own, send_other))


def expert_back_kernel(place, g, slope, w_in, w_out, grad_pre, keep_own, keep_other, send_own, send_other, total):
    step = pl.program_id(0)
    low = (dot_nn(g[...], w_out[...]) * slope[...].astype(WIDE)).astype(NARROW)
    grad_pre[...] = low
    piece = dot_nt(low, w_in[...])

    @pl.when(step == 0)
    def _():
        total[...] = piece

    @pl.when(step > 0)
    def _():
        total[...] += piece

    @pl.when(step == pl.num_programs(0) - 1)
    def _():
        store_quarters(place[1], total, (keep_own, keep_other), (send_own, send_other))


def expert_forward(place, x, w_in, w_out, block):
    seq, width = x.shape
    units = w_in.shape[1]
    w_spec = pl.BlockSpec((width, block), lambda i: (0, i))
    unit_spec = pl.BlockSpec((seq, block), lambda i: (0, i))
    quarter = (seq // 4, width)
    return pl.pallas_call(
        expert_out_kernel,
        grid=(units // block,),
        in_specs=[smem_spec(), full_spec(x.shape), w_spec, w_spec],
        out_specs=[unit_spec, unit_spec] + [full_spec(quarter)] * 4,
        out_shape=[shape_of((seq, units), NARROW), pltpu.HBM((seq, units), NARROW)] + [shape_of(quarter, NARROW)] * 4,
        scratch_shapes=[VMEM(x.shape, WIDE)],
        compiler_params=params(),
        cost_estimate=cost(9.4),
        name="expert_forward",
    )(place, x, w_in, w_out)


def expert_backward(place, g, slope, w_in, w_out, block, *after):
    seq, width = g.shape
    units = w_in.shape[1]
    w_spec = pl.BlockSpec((width, block), lambda i: (0, i))
    unit_spec = pl.BlockSpec((seq, block), lambda i: (0, i))
    quarter = (seq // 4, width)
    return pl.pallas_call(
        expert_back_kernel,
        grid=(units // block,),
        in_specs=[smem_spec(), full_spec(g.shape), unit_spec, w_spec, w_spec],
        out_specs=[unit_spec] + [full_spec(quarter)] * 4,
        out_shape=[shape_of((seq, units), NARROW)] + [shape_of(quarter, NARROW)] * 4,
        scratch_shapes=[VMEM(g.shape, WIDE)],
        compiler_params=params(),
        cost_estimate=cost(8),
        name="expert_backward",
    )(place, later(g, *after), slope, w_in, w_out)


def store_chunks(place, bit, value, keep, send, lanes=slice(None)):
    rows = keep.shape[1]
    mine = (place[2] >> bit) & 1
    low = (1 << bit) - 1
    for j in range(2 * keep.shape[0]):
        at = ((j >> (bit + 1)) << bit) | (j & low)
        chunk = value[j * rows : (j + 1) * rows].astype(NARROW)

        @pl.when(mine == (j >> bit) & 1)
        def _():
            keep[at, :, lanes] = chunk

        @pl.when(mine != (j >> bit) & 1)
        def _():
            send[at, :, lanes] = chunk


def weight_grad_kernel(bits, lanes, place, left, right, *refs):
    turned = refs[-1]
    turned[...] = left[...].T
    for piece, bit in enumerate(bits):
        value = dot_nn(turned[...], right[:, piece * lanes : (piece + 1) * lanes])
        store_chunks(place, bit, value, refs[2 * piece], refs[2 * piece + 1])


def weight_grad(place, left, right, bits, lanes, count, after):
    seq, width = left.shape
    shape = shape_of((count // 2, width // count, lanes), NARROW)
    vmem = pl.BlockSpec(memory_space=VMEM)
    outs = [shape] * (2 * len(bits))
    return pl.pallas_call(
        functools.partial(weight_grad_kernel, bits, lanes),
        in_specs=[smem_spec()] + [vmem] * 2,
        out_specs=[vmem] * len(outs),
        out_shape=outs,
        scratch_shapes=[VMEM((width, seq), NARROW)],
        compiler_params=params(16),
        cost_estimate=cost(0.2),
        name="weight_grad",
    )(place, later(left, after), right)


def weight_grads_kernel(start, place, rows, grad_pre, grads, act, keep, send, keep_next, send_next, keep_out, send_out, turned):
    lanes = keep.shape[2]
    turned[...] = rows[...].T
    store_chunks(place, 0, dot_nn(turned[...], grad_pre[:, :lanes]), keep, send)
    store_chunks(place, 0, dot_nn(turned[...], grad_pre[:, lanes:]), keep_next, send_next)
    turned[...] = grads[...].T
    store_chunks(place, 1, dot_nn(turned[...], act[:, start:]), keep_out, send_out)


def weight_grads(place, rows, grad_pre, grads, act, start, count, after):
    seq, width = rows.shape
    units = act.shape[1]
    first = shape_of((count // 2, width // count, start), NARROW)
    second = shape_of((count // 2, width // count, units - start), NARROW)
    vmem = pl.BlockSpec(memory_space=VMEM)
    return pl.pallas_call(
        functools.partial(weight_grads_kernel, start),
        in_specs=[smem_spec()] + [vmem] * 4,
        out_specs=[vmem] * 6,
        out_shape=[first] * 2 + [second] * 4,
        scratch_shapes=[VMEM((width, seq), NARROW)],
        compiler_params=params(16),
        cost_estimate=cost(0.2),
        name="weight_grads",
    )(place, later(rows, after), grad_pre, grads, act)


def combine_kernel(
    place, hidden, outs, out_far, out_row, out_row_far, backs, back_far, back_row, back_row_far, grad, kinds, gain, router, w_mine, att,
    output, grad_hidden, sums, back_own, back_send, w_keep, w_send, w_sum, route,
):
    row, col = place[0], place[1]
    step = pl.program_id(0)
    block = hidden.shape[0]
    count = router.shape[0]
    size = back_own.shape[1]

    @pl.when(step == 0)
    def _():
        route[...] = column(kinds[...])
        sums[...] = jnp.zeros_like(sums)

    gain_wide = gain[...].astype(WIDE)
    mine = col == step

    def chosen(own, own_row, far, far_row):
        return jnp.where(mine, own[...].astype(WIDE) + own_row[...].astype(WIDE), far[...].astype(WIDE) + far_row[...].astype(WIDE))

    expert_out = chosen(outs, out_row, out_far, out_row_far)
    grad_rows = chosen(backs, back_row, back_far, back_row_far)
    wide = hidden[...]
    grad_wide = grad[...].astype(WIDE)
    inverse = lax.rsqrt(jnp.mean(wide * wide, axis=-1, keepdims=True) + EPS)
    scaled = wide * inverse
    hn = scaled * gain_wide
    probs, hots, gate = gate_values(hn, route[pl.ds(pl.multiple_of(step * block, 16), block), :], router)
    output[...] = (wide + gate * expert_out).astype(NARROW)
    grad_gate = jnp.sum(grad_wide * expert_out, axis=1, keepdims=True) * gate
    grad_hn = grad_rows
    line = lax.broadcasted_iota(jnp.int32, sums.shape, 0)
    packed = jnp.zeros(sums.shape, WIDE)
    for e in range(count):
        grad_logit = grad_gate * (hots[e] - probs[e])
        grad_hn = grad_hn + grad_logit * router[e : e + 1]
        packed = packed + jnp.where(line == 1 + e, jnp.sum(hn * grad_logit, axis=0, keepdims=True), 0.0)
    sums[...] += packed + jnp.where(line == 0, jnp.sum(grad_hn * scaled, axis=0, keepdims=True), 0.0)
    u = grad_hn * gain_wide
    back = grad_wide + inverse * u - wide * (inverse * inverse * inverse) * jnp.mean(u * wide, axis=-1, keepdims=True)
    grad_hidden[...] = back
    low = back.astype(NARROW)
    grad_att = dot_nn(low, w_mine[...]).astype(NARROW)

    @pl.when(row == 0)
    def _():
        back_own[...] = grad_att[:, :size]
        back_send[...] = grad_att[:, size:]

    @pl.when(row == 1)
    def _():
        back_own[...] = grad_att[:, size:]
        back_send[...] = grad_att[:, :size]

    piece = dot_tn(low, att[...])

    @pl.when(step == 0)
    def _():
        w_sum[...] = piece

    @pl.when(step == 1)
    def _():
        store_chunks(place, 0, w_sum[...] + piece, w_keep, w_send)


def combine(place, hidden, outs, backs, grad, kinds, gain, router, w_mine, att, size, count, after):
    tokens, width = hidden.shape
    half = w_mine.shape[1]
    block = tokens // 2
    rows = pl.BlockSpec((block, width), lambda i: (i, 0))
    narrow = pl.BlockSpec((block, size), lambda i: (i, 0))
    chunks = (count // 2, width // count, half)
    return pl.pallas_call(
        combine_kernel,
        grid=(2,),
        in_specs=[smem_spec(), rows]
        + [full_spec((block, width))] * 8
        + [rows]
        + [full_spec(x.shape) for x in (kinds, gain, router, w_mine)]
        + [pl.BlockSpec((block, half), lambda i: (i, 0))],
        out_specs=[rows, rows, full_spec((8, width)), narrow, narrow, full_spec(chunks), full_spec(chunks)],
        out_shape=[
            shape_of((tokens, width), NARROW),
            shape_of((tokens, width), WIDE),
            shape_of((8, width), WIDE),
            shape_of((tokens, size), NARROW),
            shape_of((tokens, size), NARROW),
            shape_of(chunks, NARROW),
            shape_of(chunks, NARROW),
        ],
        scratch_shapes=[VMEM((width, half), WIDE), VMEM((tokens, 1), WIDE)],
        compiler_params=params(),
        cost_estimate=cost(0.1),
        name="combine",
    )(place, later(hidden, after), *outs, *backs, grad, kinds, gain, router, w_mine, att)


def project_back_kernel(place, g, w_all, keep_own, keep_other, send_own, send_other, back_all):
    block = g.shape[0] // 4
    back = dot_nt(g[...], w_all[...]).astype(NARROW)
    for i in range(4):
        at = (i % 2) * 2 * block + (i // 2) * block
        back_all[at : at + block] = back[i * block : (i + 1) * block]
    store_quarters(place[1], back_all, (keep_own, keep_other), (send_own, send_other))


def project_back(place, g, w_all, after):
    seq, cols = g.shape
    width = w_all.shape[0]
    vmem = pl.BlockSpec(memory_space=VMEM)
    quarter = shape_of((seq // 4, width), NARROW)
    return pl.pallas_call(
        project_back_kernel,
        in_specs=[smem_spec()] + [vmem] * 2,
        out_specs=[vmem] * 4,
        out_shape=[quarter] * 4,
        scratch_shapes=[VMEM((seq, width), NARROW)],
        compiler_params=params(16),
        cost_estimate=cost(0.2),
        name="project_back",
    )(place, later(g, after), w_all)


def project_grad_kernel(place, g, normed, w_all, gain, sums, table, keep, send):
    width = normed.shape[1]
    wide = g.shape[1] // 3
    per_row = width // (4 * keep.shape[0])
    grads = dot_tn(normed[...], g[...])
    store_chunks(place, 0, grads[:, : 2 * wide], keep, send, slice(0, 2 * wide))
    gain_grad = jnp.sum(grads * w_all[...].astype(WIDE), axis=1, keepdims=True)
    line = lax.broadcasted_iota(jnp.int32, (128, width), 0)
    lines = jnp.where(line == 0, 1.0 / gain[...].astype(WIDE), 0.0)
    for e in range(TABLE_LANE - 1):
        lines = lines + jnp.where(line == 1 + e, sums[e : e + 1], 0.0)
    lane = lax.broadcasted_iota(jnp.int32, (width, 128), 1)
    turned = lines.T
    turned = turned * jnp.where(lane == 0, gain_grad, 1.0)
    gap = jnp.zeros((per_row - NBUCKET, 128), WIDE)
    tables = jnp.concatenate([table[...], gap] * (width // per_row), axis=0)
    store_chunks(place, 0, turned + tables, keep, send, slice(2 * wide, 2 * wide + 128))
    store_chunks(place, 0, grads[:, 2 * wide :], keep, send, slice(2 * wide + 128, 3 * wide + 128))


def project_grad(place, g, normed, w_all, gain, sums, table, count, after):
    seq, width = normed.shape
    wide = g.shape[1] // 3
    args = (place, g, normed, w_all, gain, sums, later(table, after))
    chunks = (count // 2, width // count)
    vmem = pl.BlockSpec(memory_space=VMEM)
    shape = shape_of((*chunks, 3 * wide + 128), NARROW)
    return pl.pallas_call(
        project_grad_kernel,
        in_specs=[smem_spec()] + [vmem] * 6,
        out_specs=[vmem] * 2,
        out_shape=[shape] * 2,
        compiler_params=params(20),
        cost_estimate=cost(0.2),
        name="project_grad",
    )(*args)


def finish_kernel(place, tok, gain, grad_hidden, mine, far, row, row_far, out):
    col = place[1]
    block = mine.shape[0]
    gain_wide = gain[...].astype(WIDE)
    for half in range(2):
        part = pl.ds(half * block, block)
        grad_normed = jnp.where(col == half, mine[...].astype(WIDE) + row[...].astype(WIDE), far[...].astype(WIDE) + row_far[...].astype(WIDE))
        rows = tok[part, :].astype(WIDE)
        inverse = lax.rsqrt(jnp.mean(rows * rows, axis=-1, keepdims=True) + EPS)
        u = grad_normed * gain_wide
        out[part, :] = grad_hidden[part, :] + inverse * u - rows * (inverse * inverse * inverse) * jnp.mean(u * rows, axis=-1, keepdims=True)


def finish(place, tok, gain, grad_hidden, *sums):
    args = (place, tok, gain, grad_hidden, *sums)
    return pl.pallas_call(
        finish_kernel,
        in_specs=[smem_spec()] + [pl.BlockSpec(memory_space=VMEM)] * (len(args) - 1),
        out_specs=pl.BlockSpec(memory_space=VMEM),
        out_shape=shape_of(tok.shape, WIDE),
        compiler_params=params(16),
        cost_estimate=cost(0.1),
        name="finish",
    )(*args)


def assemble_kernel(place, part, got, grad_q, grad_k, grad_v, grad_o, grad_router, grad_table, first, second):
    row = place[0]
    wide = grad_q.shape[1] // 2
    rows = got.shape[0]
    mine = part[...].astype(WIDE)
    theirs = got[...].astype(WIDE)
    extra = 2 * wide
    late = extra + 128
    last = late + wide
    heads = grad_table.shape[1] // 2
    grad_o[...] = mine[:, last:] + theirs[:, last:]
    small = mine[:, extra:late] + theirs[:, extra:late]
    grad_router[...] = small[:, 2:4]
    turned = jnp.concatenate([small, jnp.zeros((128 - rows, 128), WIDE)], axis=0).T
    first[...] = turned[0:1, :rows]
    second[...] = turned[1:2, :rows]
    at = extra + TABLE_LANE

    @pl.when(row == 0)
    def _():
        for out, lo in ((grad_q, 0), (grad_k, wide), (grad_v, late)):
            out[...] = jnp.concatenate([mine[:, lo : lo + wide], theirs[:, lo : lo + wide]], axis=1)
        grad_table[...] = jnp.concatenate([mine[:NBUCKET, at : at + heads], theirs[:NBUCKET, at : at + heads]], axis=1)

    @pl.when(row == 1)
    def _():
        for out, lo in ((grad_q, 0), (grad_k, wide), (grad_v, late)):
            out[...] = jnp.concatenate([theirs[:, lo : lo + wide], mine[:, lo : lo + wide]], axis=1)
        grad_table[...] = jnp.concatenate([theirs[:NBUCKET, at : at + heads], mine[:NBUCKET, at : at + heads]], axis=1)


def assemble(place, part, got, wide, heads, count):
    rows = got.shape[0]
    vmem = pl.BlockSpec(memory_space=VMEM)
    return pl.pallas_call(
        assemble_kernel,
        in_specs=[smem_spec()] + [vmem] * 2,
        out_specs=[vmem] * 8,
        out_shape=[shape_of((rows, 2 * wide), WIDE)] * 4
        + [shape_of((rows, count), WIDE), shape_of((NBUCKET, 2 * heads), WIDE), shape_of((1, rows), WIDE), shape_of((1, rows), WIDE)],
        compiler_params=params(10),
        cost_estimate=cost(1.4),
        name="assemble",
    )(place, part, got)


def swap(value, axis, flip=1):
    size = lax.axis_size(axis)
    return lax.ppermute(value, axis, [(i, i ^ flip) for i in range(size)])


def pick(value, index, axis=0):
    return lax.dynamic_index_in_dim(value, index, axis, keepdims=False)


def in_order(first, mine, got, axis=0):
    return jnp.where(first, jnp.concatenate([mine, got], axis), jnp.concatenate([got, mine], axis))


def halve_kernel(bit, place, kept, got, keep, send):
    mine = (place[2] >> bit) & 1
    low = (1 << bit) - 1
    for j in range(kept.shape[0]):
        at = ((j >> (bit + 1)) << bit) | (j & low)
        chunk = (kept[j].astype(WIDE) + got[j].astype(WIDE)).astype(NARROW)

        @pl.when(mine == (j >> bit) & 1)
        def _():
            keep[at] = chunk

        @pl.when(mine != (j >> bit) & 1)
        def _():
            send[at] = chunk


def halve(place, kept, got, bit, at, after, micros=0.1):
    n, rows, lanes = kept.shape
    shape = shape_of((n // 2, rows, lanes), NARROW)
    vmem = pl.BlockSpec(memory_space=VMEM)

    def kernel(place, *refs):
        shifted = [None, None, place[2] >> (at - bit) if at > bit else place[2]]
        halve_kernel(bit, shifted, *refs)

    return pl.pallas_call(
        kernel,
        in_specs=[smem_spec()] + [vmem] * 2,
        out_specs=[vmem] * 2,
        out_shape=[shape] * 2,
        compiler_params=params(10),
        cost_estimate=cost(micros),
        name="halve",
    )(place, later(kept, after), got)


def halve_two_kernel(at, place, kept, got, kept_next, got_next, keep, send):
    mine = (place[2] >> at) & 1
    lanes = kept.shape[2]
    for first, second, part in ((kept, got, slice(0, lanes)), (kept_next, got_next, slice(lanes, keep.shape[2]))):
        for j in range(2):
            chunk = (first[j].astype(WIDE) + second[j].astype(WIDE)).astype(NARROW)

            @pl.when(mine == j)
            def _():
                keep[0, :, part] = chunk

            @pl.when(mine != j)
            def _():
                send[0, :, part] = chunk


def halve_two(place, kept, got, kept_next, got_next, at, after):
    _, rows, lanes = kept.shape
    shape = shape_of((1, rows, lanes + kept_next.shape[2]), NARROW)
    vmem = pl.BlockSpec(memory_space=VMEM)
    return pl.pallas_call(
        functools.partial(halve_two_kernel, at),
        in_specs=[smem_spec()] + [vmem] * 4,
        out_specs=[vmem] * 2,
        out_shape=[shape] * 2,
        compiler_params=params(10),
        cost_estimate=cost(0.1),
        name="halve_two",
    )(place, later(kept, after), got, kept_next, got_next)


def add_pieces_kernel(kept, got, kept_next, got_next, kept_last, got_last, first, second, beside):
    head = kept.shape[2]
    units = second.shape[1]
    split = kept_next.shape[2] - (units - head)
    first[:, :head] = kept[0].astype(WIDE) + got[0].astype(WIDE)
    total = kept_next[0].astype(WIDE) + got_next[0].astype(WIDE)
    first[:, head:] = total[:, split:]
    second[:, :split] = total[:, :split]
    rest = kept_last[0].astype(WIDE) + got_last[0].astype(WIDE)
    second[:, split:] = rest[:, : units - split]
    beside[...] = rest[:, units - split :].astype(NARROW)


def add_pieces(pieces, units, after):
    vmem = pl.BlockSpec(memory_space=VMEM)
    rows = pieces[0][0].shape[1]
    rest = sum(pair[0].shape[2] for pair in pieces) - 2 * units
    first, *others = [x for pair in pieces for x in pair]
    return pl.pallas_call(
        add_pieces_kernel,
        in_specs=[vmem] * 6,
        out_specs=[vmem] * 3,
        out_shape=[shape_of((rows, units), WIDE)] * 2 + [shape_of((rows, rest), NARROW)],
        compiler_params=params(10),
        cost_estimate=cost(0.1),
        name="add_pieces",
    )(later(first, after), *others)


def part_kernel(place, kept, got, beside, mine, send):
    rows = mine.shape[0]
    values = (
        (kept[0].astype(WIDE) + got[0].astype(WIDE)).astype(NARROW),
        beside[...],
    )
    at = 0
    for value in values:
        lanes = slice(at, at + value.shape[1])
        at += value.shape[1]

        @pl.when(place[0] == 0)
        def _():
            mine[:, lanes] = value[:rows]
            send[:, lanes] = value[rows:]

        @pl.when(place[0] == 1)
        def _():
            mine[:, lanes] = value[rows:]
            send[:, lanes] = value[:rows]


def parts_by_row(place, kept, got, beside):
    vmem = pl.BlockSpec(memory_space=VMEM)
    shape = shape_of((kept.shape[1] // 2, kept.shape[2] + beside.shape[1]), NARROW)
    return pl.pallas_call(
        part_kernel,
        in_specs=[smem_spec()] + [vmem] * 3,
        out_specs=[vmem] * 2,
        out_shape=[shape, shape],
        compiler_params=params(10),
        cost_estimate=cost(1),
        name="parts_by_row",
    )(place, kept, got, beside)


def add_low_kernel(keep, got, out):
    out[...] = (keep[...].astype(WIDE) + got[...].astype(WIDE)).astype(NARROW)


def add_low(keep, got, after):
    vmem = pl.BlockSpec(memory_space=VMEM)
    return pl.pallas_call(
        add_low_kernel,
        in_specs=[vmem] * 2,
        out_specs=vmem,
        out_shape=shape_of(keep.shape, NARROW),
        compiler_params=params(10),
        cost_estimate=cost(0.1),
        name="add_low",
    )(later(keep, after), got)


def along(send, bit):
    return swap(send, "dp", 1 << bit)


def local_pair(tokens, grad_out, routes, norm1_gain, w_query, w_key, w_value, w_output, rel_table, rel_bucket, norm2_gain, router, w_in, w_out):
    tok_rows, width = tokens.shape
    seq = 2 * tok_rows
    row, col = lax.axis_index("row"), lax.axis_index("col")
    count = lax.axis_size("dp")
    bits = count.bit_length() - 1
    place = jnp.stack([row, col, lax.axis_index("dp")]).astype(jnp.int32)
    col_heads = H // lax.axis_size("col")
    heads = col_heads // 2
    size = w_query.shape[1] // col_heads
    wide = heads * size

    w_own, w_send = pack(place, w_query, w_key, w_value)
    w_got = swap(w_send, "row")
    table = lax.dynamic_slice_in_dim(rel_table.astype(WIDE), col * col_heads + row * heads, heads, 1)
    bucket = jnp.pad(rel_bucket[None, :], ((0, 0), (1, 0)), constant_values=-1)
    skew = skewed_bias(bucket, table, w_send)
    tok_half = half_of(place, tokens, w_send)
    tok_got = swap(tok_half, "row")
    w_far = swap(w_got, "dp", 1)
    gain_one, gain_two = norm1_gain[None, :], norm2_gain[None, :]
    tok_got = later(tok_got, w_far, skew, gain_one)
    tok_col = swap(tok_got, "col")
    router_lines = router.astype(WIDE).T

    tok_all, normed, q, k, v, w_all = project(place, (tokens, tok_got, tok_col), gain_one, (w_own, w_got, w_far), heads, size)

    kinds = routes.astype(WIDE).reshape(-1, 128)
    kinds_got = swap(later(kinds, w_send), "row")
    wo_got = swap(later(w_output, tok_half), "row")
    grad_half = half_of(place, grad_out, tok_half)
    grad_got = swap(grad_half, "row")

    att, shares = attend(place, skew, later(q, wo_got, grad_half), k, v, 256, 0, seq)
    grad_got = later(grad_got, att)
    grad_col = swap(grad_got, "col")
    kinds_got, wo_got, _ = lax.optimization_barrier((kinds_got, wo_got, att))
    kinds_all = jnp.concatenate([kinds, kinds_got], 0)
    w_mine = in_order(row == 0, w_output, wo_got)
    w_other = swap(w_mine, "col")
    att_row = swap(att, "row")
    att_col = swap(att, "col")
    att_row = later(att_row, w_mine, kinds_all, gain_two, router_lines)
    pieces = (att, att_row, att_col, swap(att_row, "col"))
    hidden, att_own, rows, scale = hidden_rows(place, pieces, w_mine, w_other, tok_all, gain_two, router_lines, kinds_all)

    weight_in, weight_out = w_in[0], w_out[0]
    act, slope, out_own, out_other, out_own_send, out_other_send = expert_forward(place, rows, weight_in, weight_out, 512)
    out_other_col = swap(later(out_other_send, grad_col), "col")
    grads = scale_grads(place, grad_out, grad_got, grad_col, scale)
    units = act.shape[1]
    third = units // 3
    keep_o, send_o, keep_p, send_p = weight_grad(place, grads, act, (0, 1), third, count, grads)
    got_o, got_p = along(send_o, 0), along(send_p, 1)
    out_other = add_low(out_other, out_other_col, keep_o)
    out_row = swap(out_other, "row")
    out_own_col = swap(out_own_send, "col")
    grad_pre, rows_own, rows_other, rows_own_send, rows_other_send = expert_backward(
        place, grads, slope, weight_in, weight_out, 512, out_other, keep_o
    )
    out_row = later(out_row, rows_own)
    rows_other_col = swap(rows_other_send, "col")
    rows_other = add_low(later(rows_other, got_o, got_p, out_row), rows_other_col, rows_own)
    rows_row = swap(rows_other, "row")
    rows_own_col = swap(rows_own_send, "col")
    keep_o, send_o = halve(place, keep_o, got_o, 0, 1, rows_other)
    got_o = along(send_o, 1)
    keep_p, send_p = halve(place, keep_p, got_p, 0, 0, keep_o)
    got_p = along(send_p, 0)
    keep_i, send_i, keep_j, send_j, keep_q, send_q = weight_grads(place, rows, grad_pre, grads, act, 2 * third, count, keep_p)
    got_i = along(later(send_i, got_p), 0)
    got_q = along(send_q, 1)
    out_mine = add_low(out_own, out_own_col, keep_i)
    outs = (out_mine, swap(out_mine, "col"), out_row, swap(out_row, "col"))
    rows_mine = add_low(rows_own, rows_own_col, keep_i)
    rows_row = later(rows_row, rows_mine, out_mine, got_o, got_p)
    backs = (rows_mine, swap(rows_mine, "col"), rows_row, swap(rows_row, "col"))

    output, grad_hidden, sums, back_own, back_send, wo_keep, wo_send = combine(
        place, hidden, outs, backs, grad_out, kinds, gain_two, router_lines, w_mine, att_own, wide, count, keep_i
    )
    back_oth = swap(back_send, "row")
    keep_j, send_j = jnp.concatenate([keep_j, wo_keep], 2), jnp.concatenate([send_j, wo_send], 2)
    keep_o, send_o = halve_two(place, keep_o, got_o, keep_p, got_p, 2, send_j)
    got_o = along(send_o, 2)
    keep_q, send_q = halve(place, keep_q, got_q, 0, 0, keep_o)
    got_q = along(send_q, 0)
    got_j = along(later(send_j, send_q), 0)
    keep = attend_back(place, bucket, q, k, v, shares, later(back_own, keep_q), 256, 0, None)
    keep_i, send_i = halve(place, later(keep_i, got_o), got_i, 0, 1, keep[0])
    got_i = along(send_i, 1)
    g, table_part = attend_back(place, bucket, q, k, v, shares, back_oth, 256, tok_rows, keep, keep_i)
    keep_i, send_i = halve_two(place, keep_i, got_i, keep_q, got_q, 2, g)
    got_i = along(send_i, 2)

    keep_f, send_f = project_grad(place, g, normed, w_all, gain_one, sums, table_part, count, keep_i)
    got_f = along(send_f, 0)
    normed_own, normed_other, normed_own_send, normed_other_send = project_back(place, g, w_all, keep_f)
    normed_other_col = swap(normed_other_send, "col")
    keep_j, send_j = halve(place, later(keep_j, got_i), got_j, 0, 1, normed_own, 12)
    got_j = along(send_j, 1)
    normed_other = add_low(normed_other, normed_other_col, keep_j)
    normed_row = swap(normed_other, "row")
    normed_own_col = swap(normed_own_send, "col")
    keep_f, send_f = halve(place, keep_f, got_f, 0, 1, normed_other)
    got_f = along(send_f, 1)
    normed_mine = add_low(normed_own, normed_own_col, keep_f)
    normed_far = swap(normed_mine, "col")
    keep_j, send_j = halve(place, keep_j, got_j, 0, 2, normed_mine)
    got_j = along(send_j, 2)
    normed_row = later(normed_row, keep_j)
    normed_row_far = swap(normed_row, "col")
    keep_f, send_f = halve(place, keep_f, got_f, 0, 2, normed_row)
    got_f = along(send_f, 2)
    grad_tokens = finish(place, tokens, gain_one, later(grad_hidden, keep_f), normed_mine, normed_far, normed_row, normed_row_far)
    grad_out_part, grad_in_part, part_wo = add_pieces(((keep_o, got_o), (keep_i, got_i), (keep_j, got_j)), units, grad_tokens)
    mine, send = parts_by_row(place, keep_f, later(got_f, grad_in_part), part_wo)
    got = swap(send, "row")
    grad_q, grad_k, grad_v, grad_o, grad_router, grad_table, grad_one, grad_two = assemble(place, mine, got, wide, heads, router.shape[1])
    return (
        output,
        grad_tokens,
        (grad_one + swap(grad_one, "col"))[0],
        grad_q,
        grad_k,
        grad_v,
        grad_o,
        grad_table,
        grad_two[0],
        grad_router,
        grad_in_part[None],
        grad_out_part[None],
    )


def solution(mesh):
    in_specs = (
        P(("dp", "row"), None),
        P(("dp", "row"), None),
        P(("dp", "row"), None),
        P(),
        P("row", "col"),
        P("row", "col"),
        P("row", "col"),
        P("row", "col"),
        P(),
        P(),
        P(),
        P(),
        P("row", None, "col"),
        P("row", None, "col"),
    )
    out_specs = (
        P(("dp", "row"), None),
        P(("dp", "row"), None),
        P(("dp", "row")),
        P(("dp", "row"), "col"),
        P(("dp", "row"), "col"),
        P(("dp", "row"), "col"),
        P(("dp", "row"), "col"),
        P(None, "col"),
        P(("dp", "row")),
        P(("dp", "row"), None),
        P("row", "dp", "col"),
        P("row", "dp", "col"),
    )
    paired = mesh.shape["row"] == 2 and mesh.shape["col"] == 2 and mesh.shape["dp"] == 8
    return jax.shard_map(local_pair if paired else local, mesh=mesh, in_specs=in_specs, out_specs=out_specs, check_vma=False)
```
